256 devices in a mesh: dp: 32 (over y_hi, z, core), space: 8 (over x, y_lo).
Axes of the slice: x: 4, y: 4 (y_hi: 2, y_lo: 2; y = y_hi * 2 + y_lo), z: 8, core: 2. Of those that a mesh axis runs over, the one named last changes fastest.
Arguments:
- clip_qkv: bfloat16 [32, 16, 256, 4992], P('dp', None, 'space'), may hold values from -48 to 48
- temporal_qk: bfloat16 [32, 16, 256, 3328], P('dp', None, 'space'), may hold values from -48 to 48
- proj_weight: bfloat16 [1664, 512], replicated, may hold values from -0.15625 to 0.15625
- caption_tokens: bfloat16 [32, 77, 512], P('dp'), may hold values from -18 to 18
- caption_lens: int32 [32], P('dp'), may hold values from 8 to 77, as said below
- positive: int32 [32], P('dp'), may hold values from 0 to 31, each once
Outputs:
- video_emb: bfloat16 [32, 16, 256, 512], P('dp', None, 'space')
- caption_grad: float32 [32, 77, 512], P('dp')
- clip_loss: float32 [32], P('dp')
The draws below stay inside these ranges and needn't reach their ends.
Inputs may be any that keep to these rules, and one draw needn't show every extreme that they name: `caption_lens`: some caption fills all 77 slots in every draw.
All inputs are finite; a program needn't handle non-finite values.
Results may differ from the reference program's by a relative error of at most 0.029.
Values may be sent and summed in bfloat16 or wider, within the bound.
No kernel may reach another device: no remote copies, remote signals or barrier semaphores. Data moves between devices by JAX's collectives and lax.ppermute only.
A program may use at most 192 MiB of HBM per device.

```python
import jax
import jax.numpy as jnp
from jax import lax

HEADS = 13
HD = 128
EMB = 512
PATCHES = 256
FRAMES = 16
CAPTION_TOKEN_MAX = 77
CLIP_TOTAL = 32
FEATURES = 1664


def drawn_pairs(key, shape):
    return jax.random.normal(key, shape, jnp.float32).astype(jnp.bfloat16)


def draw_clip_qkv(key, part):
    key = jax.random.fold_in(key, 11)
    features = HEADS * HD
    shape = (CLIP_TOTAL, FRAMES, PATCHES, 3 * features)
    return drawn_pairs(key, shape)


def draw_temporal_qk(key, part):
    key = jax.random.fold_in(key, 23)
    features = HEADS * HD
    shape = (CLIP_TOTAL, FRAMES, PATCHES, 2 * features)
    return drawn_pairs(key, shape)


def draw_caption_tokens(key, part):
    key = jax.random.fold_in(key, 37)
    shape = (CLIP_TOTAL, CAPTION_TOKEN_MAX, EMB)
    return (jax.random.normal(key, shape, jnp.float32) * EMB ** (-0.5)).astype(jnp.bfloat16)


def draw_caption_lens(key, part):
    key = jax.random.fold_in(key, 41)
    lowest = (CAPTION_TOKEN_MAX + 9) // 10
    lengths = jax.random.randint(key, (CLIP_TOTAL,), lowest, CAPTION_TOKEN_MAX + 1, jnp.int32)
    chosen = jax.random.randint(jax.random.fold_in(key, 1), (), 0, CLIP_TOTAL, jnp.int32)
    return jnp.where(jnp.arange(CLIP_TOTAL, dtype=jnp.int32) == chosen, CAPTION_TOKEN_MAX, lengths).astype(jnp.int32)


def normal_values(rng, extent, deviation, reach, held_as=jnp.bfloat16):
    result = jax.random.normal(rng, extent, jnp.float32) * deviation
    return jnp.minimum(jnp.maximum(result, -reach), reach).astype(held_as)


def setup_inputs(seed: int = 0) -> dict:
    keys = jax.random.split(jax.random.key(seed), 7)
    clip_qkv = draw_clip_qkv(jax.random.fold_in(keys[6], 71), 0)
    temporal_qk = draw_temporal_qk(jax.random.fold_in(keys[6], 71), 0)
    proj_weight = normal_values(keys[2], (FEATURES, EMB), FEATURES ** -0.5, 0.15625)
    caption_tokens = draw_caption_tokens(jax.random.fold_in(keys[6], 71), 0)
    caption_lens = draw_caption_lens(jax.random.fold_in(keys[6], 71), 0)
    positive = jax.random.permutation(keys[5], CLIP_TOTAL).astype(jnp.int32)
    return dict(clip_qkv=clip_qkv, temporal_qk=temporal_qk, proj_weight=proj_weight, caption_tokens=caption_tokens, caption_lens=caption_lens, positive=positive)


SHARPNESS = 4.0
LOGIT_SCALE = 10.0

def round_keep(values):
    return lax.optimization_barrier(values.astype(jnp.bfloat16)).astype(jnp.float32)

def frame_attention(frame_block):
    patch_count = frame_block.shape[0]
    features = HEADS * HD
    query_matrix = frame_block[:, :features].reshape(patch_count, HEADS, HD).astype(jnp.float32)
    key_matrix = frame_block[:, features:2 * features].reshape(patch_count, HEADS, HD).astype(jnp.float32)
    value_matrix = frame_block[:, 2 * features:].reshape(patch_count, HEADS, HD).astype(jnp.float32)
    attention_logits = jnp.einsum('phd,qhd->hpq', query_matrix, key_matrix) * HD ** (-0.5)
    row_max = lax.optimization_barrier(jnp.max(attention_logits, axis=-1, keepdims=True))
    expo_terms = jnp.exp(attention_logits - row_max)
    row_total = lax.optimization_barrier(jnp.sum(expo_terms, axis=-1))
    weights = round_keep(expo_terms)
    attended = jnp.einsum('hpq,qhd->phd', weights, value_matrix) / jnp.transpose(row_total)[:, :, None]
    return attended.astype(jnp.bfloat16).reshape(patch_count, features)

def reference(clip_qkv, temporal_qk, proj_weight, caption_tokens, caption_lens, positive):
    features = HEADS * HD
    frame_blocks = clip_qkv.reshape(CLIP_TOTAL * FRAMES, PATCHES, 3 * features)
    spatial_all = lax.map(frame_attention, frame_blocks).reshape(CLIP_TOTAL, FRAMES, PATCHES, features)

    def clip_embedding(inputs):
        spatial, time_pairs = inputs
        time_query = time_pairs[..., :features].reshape(FRAMES, PATCHES, HEADS, HD).astype(jnp.float32)
        time_key = time_pairs[..., features:].reshape(FRAMES, PATCHES, HEADS, HD).astype(jnp.float32)
        time_value = spatial.reshape(FRAMES, PATCHES, HEADS, HD).astype(jnp.float32)
        attention_logits = jnp.einsum('fphd,gphd->phfg', time_query, time_key) * HD ** (-0.5)
        row_max = lax.optimization_barrier(jnp.max(attention_logits, axis=-1, keepdims=True))
        expo_terms = jnp.exp(attention_logits - row_max)
        row_total = lax.optimization_barrier(jnp.sum(expo_terms, axis=-1))
        weights = round_keep(expo_terms)
        temporal_out = jnp.einsum('phfg,gphd->fphd', weights, time_value) / jnp.transpose(row_total, (2, 0, 1))[..., None]
        combined = (spatial.astype(jnp.float32) + temporal_out.reshape(FRAMES, PATCHES, features)).astype(jnp.bfloat16)
        projected = jnp.dot(combined.reshape(FRAMES * PATCHES, features), proj_weight, preferred_element_type=jnp.float32)
        scaled = projected * lax.rsqrt(lax.optimization_barrier(jnp.mean(projected * projected, axis=-1, keepdims=True)) + 1e-06)
        return scaled.astype(jnp.bfloat16).reshape(FRAMES, PATCHES, EMB)
    video_emb = lax.map(clip_embedding, (spatial_all, temporal_qk))
    flattened_caption = caption_tokens.reshape(CLIP_TOTAL * CAPTION_TOKEN_MAX, EMB)
    video_rows = video_emb.reshape(CLIP_TOTAL, FRAMES * PATCHES, EMB)

    def soft_of(clip_rows):
        similarity = jnp.dot(clip_rows, flattened_caption.T, preferred_element_type=jnp.float32)
        row_max = lax.optimization_barrier(jnp.max(similarity, axis=0))
        expo_sum = lax.optimization_barrier(jnp.sum(jnp.exp(SHARPNESS * (similarity - row_max)), axis=0))
        return row_max + jnp.log(expo_sum) / SHARPNESS
    soft_max = lax.map(soft_of, video_rows)
    token_mask = (jnp.arange(CAPTION_TOKEN_MAX, dtype=jnp.int32)[None, :] < caption_lens[:, None]).astype(jnp.float32)
    length_float = caption_lens.astype(jnp.float32)
    caption_score = lax.optimization_barrier(jnp.sum(soft_max.reshape(CLIP_TOTAL, CLIP_TOTAL, CAPTION_TOKEN_MAX) * token_mask[None], axis=-1)) / length_float[None, :]
    logit_matrix = LOGIT_SCALE * caption_score
    logit_max = lax.optimization_barrier(jnp.max(logit_matrix, axis=-1, keepdims=True))
    log_total = logit_max[:, 0] + jnp.log(lax.optimization_barrier(jnp.sum(jnp.exp(logit_matrix - logit_max), axis=-1)))
    onehot = (jnp.arange(CLIP_TOTAL, dtype=jnp.int32)[None, :] == positive[:, None]).astype(jnp.float32)
    clip_loss = log_total - lax.optimization_barrier(jnp.sum(logit_matrix * onehot, axis=-1))
    grad_logit = LOGIT_SCALE * (jnp.exp(logit_matrix - log_total[:, None]) - onehot)
    token_coef = (grad_logit[:, :, None] * token_mask[None] / length_float[None, :, None]).reshape(CLIP_TOTAL, CLIP_TOTAL * CAPTION_TOKEN_MAX)

    def accumulate(running, inputs):
        clip_rows, soft_row, coef_row = inputs
        similarity = jnp.dot(clip_rows, flattened_caption.T, preferred_element_type=jnp.float32)
        weights = (jnp.exp(SHARPNESS * (similarity - soft_row[None, :])) * coef_row[None, :]).astype(jnp.bfloat16)
        return (running + jnp.dot(weights.T, clip_rows, preferred_element_type=jnp.float32), None)
    caption_grad, unused = lax.scan(accumulate, jnp.zeros((CLIP_TOTAL * CAPTION_TOKEN_MAX, EMB), jnp.float32), (video_rows, soft_max, token_coef))
    return (video_emb, caption_grad.reshape(CLIP_TOTAL, CAPTION_TOKEN_MAX, EMB), clip_loss)
```

```python
import math

import jax
import jax.numpy as jnp
from jax import lax
from jax.experimental import pallas as pl
from jax.experimental.pallas import tpu as pltpu
from jax.sharding import PartitionSpec as P

HEADS = 13
HD = 128
FEATURES = HEADS * HD
EMB = 512
FRAMES = 16
PATCHES = 256
LOCAL = 32
SLOTS = 77
PADDED = 80
CAPTIONS = 32
SHARPNESS = 4.0
LOGIT_SCALE = 10.0
LOG2E = math.log2(math.e)
SCORE_LOG2 = HD ** (-0.5) * LOG2E
SHARP_LOG2 = SHARPNESS * LOG2E
MIB = 1 << 20


def nt(a, b):
    return lax.dot_general(a, b, (((1,), (1,)), ((), ())), preferred_element_type=jnp.float32)


def spatial_kernel(qkv_ref, out_ref):
    for h in range(HEADS):
        q = qkv_ref[:, 0, :, pl.ds(h * HD, HD)].reshape(PATCHES, HD)
        k = qkv_ref[:, 0, :, pl.ds(FEATURES + h * HD, HD)].reshape(PATCHES, HD)
        v = qkv_ref[:, 0, :, pl.ds(2 * FEATURES + h * HD, HD)].reshape(PATCHES, HD)
        s = nt(q, k)
        m = jnp.max(s, axis=-1, keepdims=True)
        e = jnp.exp2((s - m) * SCORE_LOG2)
        total = jnp.sum(e, axis=-1, keepdims=True)
        o = jnp.dot(e.astype(jnp.bfloat16), v, preferred_element_type=jnp.float32)
        o = (o / total).astype(jnp.bfloat16)
        out_ref[:, 0, :, pl.ds(h * HD, HD)] = o.reshape(8, LOCAL, HD)


def spatial_attention(blocks):
    frames = blocks.shape[1]
    return pl.pallas_call(
        spatial_kernel,
        grid=(frames,),
        in_specs=[pl.BlockSpec((8, 1, LOCAL, 3 * FEATURES), lambda f: (0, f, 0, 0))],
        out_specs=pl.BlockSpec((8, 1, LOCAL, FEATURES), lambda f: (0, f, 0, 0)),
        out_shape=jax.ShapeDtypeStruct((8, frames, LOCAL, FEATURES), jnp.bfloat16),
        compiler_params=pltpu.CompilerParams(vmem_limit_bytes=32 * MIB),
        cost_estimate=pl.CostEstimate(
            flops=4 * frames * HEADS * PATCHES * PATCHES * HD,
            bytes_accessed=frames * PATCHES * 4 * FEATURES * 2,
            transcendentals=frames * HEADS * PATCHES * PATCHES,
        ),
        name="spatial_attention",
    )(blocks)


def token_kernel(s_ref, tqk_ref, proj_ref, cap_ref, emb_ref, stats_ref, grad_ref, comb):
    rows = FRAMES * 16
    r = lax.broadcasted_iota(jnp.int32, (rows, rows), 0)
    c = lax.broadcasted_iota(jnp.int32, (rows, rows), 1)
    bias = jnp.where((r & 15) == (c & 15), 0.0, -1e30).astype(jnp.float32)
    for g in range(LOCAL // 16):
        part = pl.ds(g * 16, 16)
        for h in range(HEADS):
            q = tqk_ref[:, part, pl.ds(h * HD, HD)].reshape(rows, HD)
            k = tqk_ref[:, part, pl.ds(FEATURES + h * HD, HD)].reshape(rows, HD)
            v = s_ref[:, part, pl.ds(h * HD, HD)].reshape(rows, HD)
            s = nt(q, k) + bias
            m = jnp.max(s, axis=-1, keepdims=True)
            e = jnp.exp2((s - m) * SCORE_LOG2)
            total = jnp.sum(e, axis=-1, keepdims=True)
            o = jnp.dot(e.astype(jnp.bfloat16), v, preferred_element_type=jnp.float32)
            o = (v.astype(jnp.float32) + o / total).astype(jnp.bfloat16)
            comb[:, part, pl.ds(h * HD, HD)] = o.reshape(FRAMES, 16, HD)
    tokens = FRAMES * LOCAL
    projected = jnp.dot(
        comb[...].reshape(tokens, FEATURES), proj_ref[...], preferred_element_type=jnp.float32
    )
    scale = lax.rsqrt(jnp.mean(projected * projected, axis=-1, keepdims=True) + 1e-06)
    video = (projected * scale).astype(jnp.bfloat16)
    emb_ref[...] = video.reshape(FRAMES, LOCAL, EMB)

    eye = lax.broadcasted_iota(jnp.int32, (PADDED, 128), 0) == lax.broadcasted_iota(
        jnp.int32, (PADDED, 128), 1
    )
    group = 8
    for j0 in range(0, CAPTIONS, group):
        caps = cap_ref[pl.ds(j0, group)].reshape(group * PADDED, EMB)
        sim = nt(caps, video)
        top = jnp.max(sim, axis=-1, keepdims=True)
        w = jnp.exp2((sim - top) * SHARP_LOG2)
        total = jnp.sum(w, axis=-1, keepdims=True)
        for j in range(group):
            rng = slice(j * PADDED, (j + 1) * PADDED)
            stats_ref[0, pl.ds(j0 + j, 1), :] = jnp.sum(
                jnp.where(eye, top[rng], 0.0), axis=0, keepdims=True
            )
            stats_ref[1, pl.ds(j0 + j, 1), :] = jnp.sum(
                jnp.where(eye, total[rng], 0.0), axis=0, keepdims=True
            )
        grad_ref[pl.ds(j0, group)] = jnp.dot(
            w.astype(jnp.bfloat16), video, preferred_element_type=jnp.float32
        ).reshape(group, PADDED, EMB)


def token_part(spatial, temporal_qk, proj_weight, caps):
    vmem = pl.BlockSpec(memory_space=pltpu.VMEM)
    return pl.pallas_call(
        token_kernel,
        in_specs=[vmem] * 4,
        out_specs=[vmem] * 3,
        out_shape=[
            jax.ShapeDtypeStruct((FRAMES, LOCAL, EMB), jnp.bfloat16),
            jax.ShapeDtypeStruct((2, CAPTIONS, 128), jnp.float32),
            jax.ShapeDtypeStruct((CAPTIONS, PADDED, EMB), jnp.float32),
        ],
        scratch_shapes=[pltpu.VMEM((FRAMES, LOCAL, FEATURES), jnp.bfloat16)],
        compiler_params=pltpu.CompilerParams(vmem_limit_bytes=48 * MIB),
        cost_estimate=pl.CostEstimate(
            flops=4_400_000_000, bytes_accessed=16_000_000, transcendentals=3_000_000
        ),
        name="token_part",
    )(spatial, temporal_qk, proj_weight, caps)


def coef_kernel(pos_ref, me_ref, stats_ref, lens_ref, grad_ref, out_ref, loss_ref):
    tops = stats_ref[:, 0]
    totals = stats_ref[:, 1]
    top = jnp.max(tops, axis=0)
    total = jnp.sum(totals * jnp.exp2((tops - top[None]) * SHARP_LOG2), axis=0)
    soft = top + jnp.log(total) / SHARPNESS
    slot = lax.broadcasted_iota(jnp.int32, (CAPTIONS, 128), 1).astype(jnp.float32)
    lens = lens_ref[...].astype(jnp.float32)
    live = slot < lens
    lens_col = lens[:, :1]
    score = jnp.sum(jnp.where(live, soft, 0.0), axis=-1, keepdims=True) / lens_col
    logits = LOGIT_SCALE * score
    peak = jnp.max(logits, axis=0, keepdims=True)
    log_total = peak + jnp.log(jnp.sum(jnp.exp(logits - peak), axis=0, keepdims=True))
    onehot = lax.broadcasted_iota(jnp.int32, (CAPTIONS, 1), 0) == pos_ref[0]
    loss_ref[...] = log_total - jnp.sum(jnp.where(onehot, logits, 0.0), axis=0, keepdims=True)
    grad_logit = LOGIT_SCALE * (jnp.exp(logits - log_total) - onehot.astype(jnp.float32))
    coef = jnp.where(live, grad_logit / lens_col, 0.0)
    mine = stats_ref[me_ref[0], 0]
    factor = coef * jnp.exp2((mine - soft) * SHARP_LOG2)
    eye = lax.broadcasted_iota(jnp.int32, (PADDED, 128), 0) == lax.broadcasted_iota(
        jnp.int32, (PADDED, 128), 1
    )
    for j in range(CAPTIONS):
        col = jnp.sum(jnp.where(eye, factor[j : j + 1, :], 0.0), axis=-1, keepdims=True)
        out_ref[j] = (grad_ref[j] * col).astype(jnp.bfloat16)


def coef_part(pos, me, stats, lens, grad):
    vmem = pl.BlockSpec(memory_space=pltpu.VMEM)
    smem = pl.BlockSpec(memory_space=pltpu.SMEM)
    return pl.pallas_call(
        coef_kernel,
        in_specs=[smem, smem, vmem, vmem, vmem],
        out_specs=[vmem, vmem],
        out_shape=[
            jax.ShapeDtypeStruct((CAPTIONS, PADDED, EMB), jnp.bfloat16),
            jax.ShapeDtypeStruct((1, 1), jnp.float32),
        ],
        compiler_params=pltpu.CompilerParams(vmem_limit_bytes=32 * MIB),
        cost_estimate=pl.CostEstimate(
            flops=4_000_000, bytes_accessed=8_000_000, transcendentals=100_000
        ),
        name="coef_part",
    )(pos, me, stats, lens, grad)


def on_device(clip_qkv, temporal_qk, proj_weight, caption_tokens, caption_lens, positive):
    groups = lax.axis_size("space")
    lens_row = jnp.broadcast_to(
        caption_lens.astype(jnp.bfloat16)[:, None, None], (1, PADDED - SLOTS, EMB)
    )
    caps = lax.all_gather(
        jnp.concatenate([caption_tokens, lens_row], axis=1), "dp", axis=0, tiled=True
    )
    blocks = clip_qkv.reshape(groups, FRAMES // groups, LOCAL, 3 * FEATURES)
    blocks = lax.all_to_all(blocks, "space", split_axis=0, concat_axis=0, tiled=True)
    attended = spatial_attention(blocks)
    spatial = lax.all_to_all(attended, "space", split_axis=0, concat_axis=0, tiled=True)
    video, stats, grad = token_part(
        spatial.reshape(FRAMES, LOCAL, FEATURES),
        temporal_qk.reshape(FRAMES, LOCAL, 2 * FEATURES),
        proj_weight,
        caps,
    )
    stats = lax.all_gather(stats, "space", axis=0)
    me = lax.axis_index("space").astype(jnp.int32)[None]
    scaled, loss = coef_part(positive, me, stats, caps[:, SLOTS, :128], grad)
    mine = lax.psum_scatter(scaled, "dp", scatter_dimension=0, tiled=True)
    mine = lax.psum(mine, "space")
    caption_grad = mine[:, :SLOTS].astype(jnp.float32)
    return video[None], caption_grad, loss.reshape(1)


def solution(mesh):
    return jax.shard_map(
        on_device,
        mesh=mesh,
        in_specs=(
            P("dp", None, "space", None),
            P("dp", None, "space", None),
            P(),
            P("dp", None, None),
            P("dp"),
            P("dp"),
        ),
        out_specs=(P("dp", None, "space", None), P("dp", None, None), P("dp")),
        check_vma=False,
    )
```

```python
import math

import jax
import jax.numpy as jnp
from jax import lax
from jax.experimental import pallas as pl
from jax.experimental.pallas import tpu as pltpu
from jax.sharding import PartitionSpec as P

HEADS = 13
HD = 128
FEATURES = HEADS * HD
EMB = 512
FRAMES = 16
PATCHES = 256
LOCAL = 32
SLOTS = 77
PADDED = 80
CAPTIONS = 32
SHARPNESS = 4.0
LOGIT_SCALE = 10.0
LOG2E = math.log2(math.e)
SCORE_LOG2 = HD ** (-0.5) * LOG2E
SHARP_LOG2 = SHARPNESS * LOG2E
MIB = 1 << 20
VMEM = pl.BlockSpec(memory_space=pltpu.VMEM)
SMEM = pl.BlockSpec(memory_space=pltpu.SMEM)

NEAR = ((0, 1), (1, 0), (3, 0), (1, 1), (3, 1))
FAR = ((2, 0), (2, 1))


def moved(dx, dy):
    return [(s, (s // 2 + dx) % 4 * 2 + (s % 2 ^ dy)) for s in range(8)]


def nt(a, b):
    return lax.dot_general(a, b, (((1,), (1,)), ((), ())), preferred_element_type=jnp.float32)


def exchange(block):
    east = lax.ppermute(jnp.stack([block(2, 0)[0], block(2, 1)[0]]), "space", moved(1, 0))
    west = lax.ppermute(jnp.stack([block(2, 0)[1], block(2, 1)[1]]), "space", moved(3, 0))
    got = {}
    for dx, dy in NEAR:
        back = ((4 - dx) % 4, dy)
        pair = lax.ppermute(block(dx, dy), "space", moved(dx, dy))
        got[back] = [pair]
    for i, (dx, dy) in enumerate(FAR):
        got[(dx, dy)] = [
            lax.ppermute(east[i : i + 1], "space", moved(1, dy)),
            lax.ppermute(west[i : i + 1], "space", moved(3, dy)),
        ]
    return got


ORDER = ((0, 0),) + NEAR + FAR


def frame_view(refs, f):
    views = [refs[i].at[f] for i in range(6)]
    return views + [refs[6 + 2 * i + f].at[0] for i in range(2)]


def spatial_kernel(*refs):
    ins, outs = refs[:10], refs[10:]
    for f in range(2):
        src, dst = frame_view(ins, f), frame_view(outs, f)

        def rows(offset):
            return jnp.concatenate([r[:, pl.ds(offset, HD)] for r in src], axis=0)

        for h in range(HEADS):
            q = rows(h * HD)
            k = rows(FEATURES + h * HD)
            v = rows(2 * FEATURES + h * HD)
            s = nt(q, k)
            m = jnp.max(s, axis=-1, keepdims=True)
            e = jnp.exp2((s - m) * SCORE_LOG2)
            total = jnp.sum(e, axis=-1, keepdims=True)
            o = jnp.dot(e.astype(jnp.bfloat16), v, preferred_element_type=jnp.float32)
            o = (o / total).astype(jnp.bfloat16)
            for i in range(8):
                dst[i][:, pl.ds(h * HD, HD)] = o[i * LOCAL : (i + 1) * LOCAL]


def spatial_attention(pieces):
    shapes = [(2, LOCAL, FEATURES)] * 6 + [(1, LOCAL, FEATURES)] * 4
    return pl.pallas_call(
        spatial_kernel,
        in_specs=[VMEM] * 10,
        out_specs=[VMEM] * 10,
        out_shape=[jax.ShapeDtypeStruct(s, jnp.bfloat16) for s in shapes],
        compiler_params=pltpu.CompilerParams(vmem_limit_bytes=24 * MIB),
        cost_estimate=pl.CostEstimate(
            flops=8 * HEADS * PATCHES * PATCHES * HD,
            bytes_accessed=2 * PATCHES * 4 * FEATURES * 2,
            transcendentals=2 * HEADS * PATCHES * PATCHES,
        ),
        name="spatial_attention",
    )(*pieces)


def time_kernel(tqk_ref, out_ref):
    rows = FRAMES * 16
    r = lax.broadcasted_iota(jnp.int32, (rows, rows), 0)
    c = lax.broadcasted_iota(jnp.int32, (rows, rows), 1)
    bias = jnp.where((r & 15) == (c & 15), 0.0, -1e30).astype(jnp.float32)
    for g in range(LOCAL // 16):
        part = pl.ds(g * 16, 16)
        for h in range(HEADS):
            q = tqk_ref[:, part, pl.ds(h * HD, HD)].reshape(rows, HD)
            k = tqk_ref[:, part, pl.ds(FEATURES + h * HD, HD)].reshape(rows, HD)
            s = nt(q, k) + bias
            m = jnp.max(s, axis=-1, keepdims=True)
            e = jnp.exp2((s - m) * SCORE_LOG2)
            total = jnp.sum(e, axis=-1, keepdims=True)
            out_ref[g * HEADS + h] = (e * (1.0 / total)).astype(jnp.bfloat16)


def time_weights(temporal_qk):
    rows = FRAMES * 16
    return pl.pallas_call(
        time_kernel,
        in_specs=[VMEM],
        out_specs=VMEM,
        out_shape=jax.ShapeDtypeStruct((2 * HEADS, rows, rows), jnp.bfloat16),
        compiler_params=pltpu.CompilerParams(vmem_limit_bytes=24 * MIB),
        cost_estimate=pl.CostEstimate(
            flops=4 * HEADS * rows * rows * HD,
            bytes_accessed=7_000_000,
            transcendentals=2 * HEADS * rows * rows,
        ),
        name="time_weights",
    )(temporal_qk)


def gathered_kernel(place_ref, mine_ref, other_ref, out_ref):
    y_hi, core = place_ref[0], place_ref[1]
    for z in range(8):
        for k in range(2):
            at = (y_hi ^ k) * 16 + z * 2
            out_ref[at + core] = mine_ref[z, k]
            out_ref[at + 1 - core] = other_ref[z, k]


def gather_captions(caps, place):
    far = lax.ppermute(caps, "dp", [(i, i ^ 16) for i in range(32)])
    pair = jnp.stack([caps, far])
    groups = [[a * 16 + z * 2 + c for z in range(8)] for a in range(2) for c in range(2)]
    mine = lax.all_to_all(
        jnp.broadcast_to(pair[None], (8,) + pair.shape),
        "dp", split_axis=0, concat_axis=0, axis_index_groups=groups, tiled=True,
    )
    other = lax.ppermute(mine, "dp", [(i, i ^ 1) for i in range(32)])
    return pl.pallas_call(
        gathered_kernel,
        in_specs=[SMEM, VMEM, VMEM],
        out_specs=VMEM,
        out_shape=jax.ShapeDtypeStruct((CAPTIONS, PADDED, EMB), jnp.bfloat16),
        compiler_params=pltpu.CompilerParams(vmem_limit_bytes=16 * MIB),
        cost_estimate=pl.CostEstimate(flops=0, bytes_accessed=5_200_000, transcendentals=0),
        name="gathered",
    )(place, mine, other)


def token_kernel(place_ref, *refs):
    pieces = refs[:10]
    time_ref, proj_ref, cap_ref, emb_ref, stats_ref, grad_ref, value, comb = refs[10:]
    x, y = place_ref[2], place_ref[3]
    for i, (dx, dy) in enumerate(ORDER):
        at = ((x + dx) & 3) * 4 + (y ^ dy) * 2
        for f in range(2):
            value[at + f] = frame_view(pieces, f)[i][...]
    rows = FRAMES * 16
    for g in range(LOCAL // 16):
        part = pl.ds(g * 16, 16)
        for h in range(HEADS):
            cols = pl.ds(h * HD, HD)
            v = value[:, part, cols].reshape(rows, HD)
            o = jnp.dot(time_ref[g * HEADS + h], v, preferred_element_type=jnp.float32)
            o = (v.astype(jnp.float32) + o).astype(jnp.bfloat16)
            comb[:, part, cols] = o.reshape(FRAMES, 16, HD)
    tokens = FRAMES * LOCAL
    projected = jnp.dot(
        comb[...].reshape(tokens, FEATURES), proj_ref[...], preferred_element_type=jnp.float32
    )
    scale = lax.rsqrt(jnp.mean(projected * projected, axis=-1, keepdims=True) + 1e-06)
    video = (projected * scale).astype(jnp.bfloat16)
    emb_ref[...] = video.reshape(FRAMES, LOCAL, EMB)

    eye = lax.broadcasted_iota(jnp.int32, (PADDED, 128), 0) == lax.broadcasted_iota(
        jnp.int32, (PADDED, 128), 1
    )
    group = 8
    for j0 in range(0, CAPTIONS, group):
        caps = cap_ref[pl.ds(j0, group)].reshape(group * PADDED, EMB)
        sim = nt(caps, video)
        top = jnp.max(sim, axis=-1, keepdims=True)
        w = jnp.exp2((sim - top) * SHARP_LOG2)
        total = jnp.sum(w, axis=-1, keepdims=True)
        for j in range(group):
            rng = slice(j * PADDED, (j + 1) * PADDED)
            top_row = jnp.sum(jnp.where(eye, top[rng], 0.0), axis=0, keepdims=True)
            total_row = jnp.sum(jnp.where(eye, total[rng], 0.0), axis=0, keepdims=True)
            for k in range(8):
                stats_ref[k, 0, pl.ds(j0 + j, 1), :] = top_row
                stats_ref[k, 1, pl.ds(j0 + j, 1), :] = total_row
        grad_ref[pl.ds(j0, group)] = jnp.dot(
            w.astype(jnp.bfloat16), video, preferred_element_type=jnp.float32
        ).reshape(group, PADDED, EMB)


def token_part(place, pieces, time, proj_weight, caps):
    return pl.pallas_call(
        token_kernel,
        in_specs=[SMEM] + [VMEM] * 13,
        out_specs=[VMEM] * 3,
        out_shape=[
            jax.ShapeDtypeStruct((FRAMES, LOCAL, EMB), jnp.bfloat16),
            jax.ShapeDtypeStruct((8, 2, CAPTIONS, 128), jnp.float32),
            jax.ShapeDtypeStruct((CAPTIONS, PADDED, EMB), jnp.float32),
        ],
        scratch_shapes=[pltpu.VMEM((FRAMES, LOCAL, FEATURES), jnp.bfloat16)] * 2,
        compiler_params=pltpu.CompilerParams(vmem_limit_bytes=40 * MIB),
        cost_estimate=pl.CostEstimate(
            flops=4_000_000_000, bytes_accessed=16_000_000, transcendentals=1_300_000
        ),
        name="token_part",
    )(place, *pieces, time, proj_weight, caps)


def coef_kernel(place_ref, pos_ref, stats_ref, lens_ref, grad_ref, send_ref, keep_ref, loss_ref, hold):
    tops = stats_ref[:, 0]
    totals = stats_ref[:, 1]
    top = jnp.max(tops, axis=0)
    total = jnp.sum(totals * jnp.exp2((tops - top[None]) * SHARP_LOG2), axis=0)
    soft = top + jnp.log(total) / SHARPNESS
    slot = lax.broadcasted_iota(jnp.int32, (CAPTIONS, 128), 1).astype(jnp.float32)
    lens = lens_ref[...].astype(jnp.float32)
    live = slot < lens
    lens_col = lens[:, :1]
    score = jnp.sum(jnp.where(live, soft, 0.0), axis=-1, keepdims=True) / lens_col
    logits = LOGIT_SCALE * score
    peak = jnp.max(logits, axis=0, keepdims=True)
    log_total = peak + jnp.log(jnp.sum(jnp.exp(logits - peak), axis=0, keepdims=True))
    onehot = lax.broadcasted_iota(jnp.int32, (CAPTIONS, 1), 0) == pos_ref[0]
    loss_ref[...] = log_total - jnp.sum(jnp.where(onehot, logits, 0.0), axis=0, keepdims=True)
    grad_logit = LOGIT_SCALE * (jnp.exp(logits - log_total) - onehot.astype(jnp.float32))
    coef = jnp.where(live, grad_logit / lens_col, 0.0)
    mine = stats_ref[place_ref[2] * 2 + place_ref[3], 0]
    hold[...] = coef * jnp.exp2((mine - soft) * SHARP_LOG2)
    eye = lax.broadcasted_iota(jnp.int32, (PADDED, 128), 0) == lax.broadcasted_iota(
        jnp.int32, (PADDED, 128), 1
    )
    core = place_ref[1]
    for m in range(CAPTIONS // 2):
        for j, ref in ((2 * m + 1 - core, send_ref), (2 * m + core, keep_ref)):
            col = jnp.sum(jnp.where(eye, hold[pl.ds(j, 1), :], 0.0), axis=-1, keepdims=True)
            ref[m] = (grad_ref[j] * col).astype(jnp.bfloat16)


def coef_part(place, pos, stats, lens, grad):
    half = jax.ShapeDtypeStruct((CAPTIONS // 2, PADDED, EMB), jnp.bfloat16)
    return pl.pallas_call(
        coef_kernel,
        in_specs=[SMEM, SMEM, VMEM, VMEM, VMEM],
        out_specs=[VMEM] * 3,
        out_shape=[half, half, jax.ShapeDtypeStruct((1, 1), jnp.float32)],
        scratch_shapes=[pltpu.VMEM((CAPTIONS, 128), jnp.float32)],
        compiler_params=pltpu.CompilerParams(vmem_limit_bytes=16 * MIB),
        cost_estimate=pl.CostEstimate(
            flops=4_000_000, bytes_accessed=8_000_000, transcendentals=100_000
        ),
        name="coef_part",
    )(place, pos, stats, lens, grad)


def small_call(kernel, name, operands, out_shapes, specs=None):
    return pl.pallas_call(
        kernel,
        in_specs=specs or [VMEM] * len(operands),
        out_specs=[VMEM] * len(out_shapes),
        out_shape=[jax.ShapeDtypeStruct(s, d) for s, d in out_shapes],
        compiler_params=pltpu.CompilerParams(vmem_limit_bytes=16 * MIB),
        cost_estimate=pl.CostEstimate(flops=0, bytes_accessed=2_000_000, transcendentals=0),
        name=name,
    )(*operands)


def added(a, b):
    return (a.astype(jnp.float32) + b.astype(jnp.float32)).astype(jnp.bfloat16)


def first_sum_kernel(place_ref, keep_ref, got_ref, a_keep, a_send, b_keep, b_send):
    x = place_ref[2]
    plan = (
        (0, ((a_keep, 0, 0), (a_send, 0, 1), (a_send, 1, 2), (a_keep, 1, 3))),
        (8, ((b_keep, 0, 0), (b_keep, 1, 1), (b_send, 1, 2), (b_send, 0, 3))),
    )
    for start, parts in plan:
        for ref, at, flip in parts:
            cols = pl.ds(pl.multiple_of((x ^ flip) * 128, 128), 128)
            for m in range(8):
                ref[m, :, pl.ds(at * 128, 128)] = added(
                    keep_ref[start + m, :, cols], got_ref[start + m, :, cols]
                )


def second_sum_kernel(a_keep, a_got, b_keep, b_got, a_mine, a_send, b_mine, b_send):
    for keep, got, mine, send in ((a_keep, a_got, a_mine, a_send), (b_keep, b_got, b_mine, b_send)):
        mine[...] = added(keep[:, :, :128], got[:, :, :128])
        send[...] = added(keep[:, :, 128:], got[:, :, 128:])


def third_sum_kernel(a_mine, a_got, b_mine, b_got, out):
    out[pl.ds(0, 8)] = added(a_mine[...], a_got[...])
    out[pl.ds(8, 8)] = added(b_mine[...], b_got[...])


def fourth_sum_kernel(parts, out):
    total = jnp.sum(parts[...].astype(jnp.float32), axis=0).astype(jnp.bfloat16)
    for k in range(8):
        out[k] = total


def last_sum_kernel(parts, out):
    for x in range(4):
        total = parts[2 * x].astype(jnp.float32) + parts[2 * x + 1].astype(jnp.float32)
        out[0, :, pl.ds(x * 128, 128)] = total[:SLOTS]


def reduce_gradient(place, send, keep):
    bf16 = jnp.bfloat16
    one = [(s, s ^ 2) for s in range(8)]
    three = [(s, s ^ 6) for s in range(8)]
    got = lax.ppermute(send, "dp", [(i, i ^ 1) for i in range(32)])
    a_keep, a_send, b_keep, b_send = small_call(
        first_sum_kernel, "first_sum", (place, keep, got), [((8, PADDED, 256), bf16)] * 4,
        [SMEM, VMEM, VMEM],
    )
    a_got = lax.ppermute(a_send, "space", one)
    b_got = lax.ppermute(b_send, "space", three)
    a_mine, a_send, b_mine, b_send = small_call(
        second_sum_kernel, "second_sum", (a_keep, a_got, b_keep, b_got),
        [((8, PADDED, 128), bf16)] * 4,
    )
    a_got = lax.ppermute(a_send, "space", three)
    b_got = lax.ppermute(b_send, "space", one)
    (parts,) = small_call(
        third_sum_kernel, "third_sum", (a_mine, a_got, b_mine, b_got), [((16, PADDED, 128), bf16)]
    )
    parts = lax.all_to_all(
        parts, "dp", split_axis=0, concat_axis=0, tiled=True,
        axis_index_groups=[[2 * m + c for m in range(16)] for c in range(2)],
    )
    (parts,) = small_call(fourth_sum_kernel, "fourth_sum", (parts,), [((8, PADDED, 128), bf16)])
    parts = lax.all_to_all(parts, "space", split_axis=0, concat_axis=0, tiled=True)
    return small_call(last_sum_kernel, "last_sum", (parts,), [((1, SLOTS, EMB), jnp.float32)])[0]


def on_device(clip_qkv, temporal_qk, proj_weight, caption_tokens, caption_lens, positive):
    dp = lax.axis_index("dp")
    space = lax.axis_index("space")
    x, y = space >> 1, space & 1
    place = jnp.stack([dp >> 4, dp & 1, x, y]).astype(jnp.int32)

    def frames_of(dx, dy):
        owner = ((x + dx) & 3) * 2 + (y ^ dy)
        return lax.dynamic_slice_in_dim(
            clip_qkv[0], owner * 2, 2, axis=0, allow_negative_indices=False
        )

    got = exchange(frames_of)
    lens_row = jnp.broadcast_to(
        caption_lens.astype(jnp.bfloat16)[:, None], (PADDED - SLOTS, EMB)
    )
    caps = gather_captions(jnp.concatenate([caption_tokens[0], lens_row], axis=0), place)
    time = time_weights(temporal_qk[0])
    pieces = [frames_of(0, 0)] + [piece for key in ORDER[1:] for piece in got[key]]
    attended = spatial_attention(pieces)
    sent = dict(zip(ORDER[1:6], attended[1:6]))
    sent[(2, 0)] = (attended[6][0], attended[7][0])
    sent[(2, 1)] = (attended[8][0], attended[9][0])
    got = exchange(lambda dx, dy: sent[(dx, dy)])
    pieces = [attended[0]] + [piece for key in ORDER[1:] for piece in got[key]]
    video, stats, grad = token_part(place, pieces, time, proj_weight, caps)
    stats = lax.all_to_all(stats, "space", split_axis=0, concat_axis=0, tiled=True)
    send, keep, loss = coef_part(place, positive, stats, caps[:, SLOTS, :128], grad)
    caption_grad = reduce_gradient(place, send, keep)
    return video[None], caption_grad, loss.reshape(1)


def solution(mesh):
    return jax.shard_map(
        on_device,
        mesh=mesh,
        in_specs=(
            P("dp", None, "space", None),
            P("dp", None, "space", None),
            P(),
            P("dp", None, None),
            P("dp"),
            P("dp"),
        ),
        out_specs=(P("dp", None, "space", None), P("dp", None, None), P("dp")),
        check_vma=False,
    )
```

```python
import math

import jax
import jax.numpy as jnp
from jax import lax
from jax.experimental import pallas as pl
from jax.experimental.pallas import tpu as pltpu
from jax.sharding import PartitionSpec as P

HEADS = 13
HD = 128
FEATURES = HEADS * HD
EMB = 512
FRAMES = 16
PATCHES = 256
LOCAL = 32
SLOTS = 77
PADDED = 80
CAPTIONS = 32
SHARPNESS = 4.0
LOGIT_SCALE = 10.0
LOG2E = math.log2(math.e)
SCORE_LOG2 = HD ** (-0.5) * LOG2E
SHARP_LOG2 = SHARPNESS * LOG2E
MIB = 1 << 20
VMEM = pl.BlockSpec(memory_space=pltpu.VMEM)
SMEM = pl.BlockSpec(memory_space=pltpu.SMEM)

NEAR = ((0, 1), (1, 0), (3, 0), (1, 1), (3, 1))
FAR = ((2, 0), (2, 1))


def moved(dx, dy):
    return [(s, (s // 2 + dx) % 4 * 2 + (s % 2 ^ dy)) for s in range(8)]


def nt(a, b):
    return lax.dot_general(a, b, (((1,), (1,)), ((), ())), preferred_element_type=jnp.float32)


def exchange(block):
    ways = (1, 3)
    first = {
        (far, f): lax.ppermute(block(*far)[f : f + 1], "space", moved(ways[f], 0))
        for far in FAR
        for f in range(2)
    }
    got = {}
    for dx, dy in NEAR:
        back = ((4 - dx) % 4, dy)
        got[back] = [lax.ppermute(block(dx, dy), "space", moved(dx, dy))]
    for far in FAR:
        got[far] = [
            lax.ppermute(first[(far, f)], "space", moved(ways[f], far[1])) for f in range(2)
        ]
    return got


ORDER = ((0, 0),) + NEAR + FAR


def frame_view(refs, f):
    views = [refs[i].at[f] for i in range(6)]
    return views + [refs[6 + 2 * i + f].at[0] for i in range(2)]


def spatial_kernel(place_ref, *refs):
    ins, out_ref = refs[:10], refs[10]
    x, y = place_ref[2], place_ref[3]
    for f in range(2):
        src = frame_view(ins, f)

        def rows(offset):
            return jnp.concatenate([r[:, pl.ds(offset, HD)] for r in src], axis=0)

        for h in range(HEADS):
            q = rows(h * HD)
            k = rows(FEATURES + h * HD)
            v = rows(2 * FEATURES + h * HD)
            s = nt(q, k)
            m = jnp.max(s, axis=-1, keepdims=True)
            e = jnp.exp2((s - m) * SCORE_LOG2)
            total = jnp.sum(e, axis=-1, keepdims=True)
            o = jnp.dot(e.astype(jnp.bfloat16), v, preferred_element_type=jnp.float32)
            o = (o / total).astype(jnp.bfloat16)
            for i, (dx, dy) in enumerate(ORDER):
                at = ((x + dx) & 3) * 2 + (y ^ dy)
                out_ref[at, f, :, pl.ds(h * HD, HD)] = o[i * LOCAL : (i + 1) * LOCAL]


def spatial_attention(place, pieces):
    return pl.pallas_call(
        spatial_kernel,
        in_specs=[SMEM] + [VMEM] * 10,
        out_specs=VMEM,
        out_shape=jax.ShapeDtypeStruct((8, 2, LOCAL, FEATURES), jnp.bfloat16),
        compiler_params=pltpu.CompilerParams(vmem_limit_bytes=12 * MIB),
        cost_estimate=pl.CostEstimate(
            flops=8 * HEADS * PATCHES * PATCHES * HD,
            bytes_accessed=2 * PATCHES * 4 * FEATURES * 2,
            transcendentals=2 * HEADS * PATCHES * PATCHES,
        ),
        name="spatial_attention",
    )(place, *pieces)


def time_kernel(tqk_ref, out_ref):
    rows = FRAMES * 16
    r = lax.broadcasted_iota(jnp.int32, (rows, rows), 0)
    c = lax.broadcasted_iota(jnp.int32, (rows, rows), 1)
    bias = jnp.where((r & 15) == (c & 15), 0.0, -1e30).astype(jnp.float32)
    for g in range(LOCAL // 16):
        part = pl.ds(g * 16, 16)
        for h in range(HEADS):
            q = tqk_ref[:, part, pl.ds(h * HD, HD)].reshape(rows, HD)
            k = tqk_ref[:, part, pl.ds(FEATURES + h * HD, HD)].reshape(rows, HD)
            s = nt(q, k) + bias
            m = jnp.max(s, axis=-1, keepdims=True)
            e = jnp.exp2((s - m) * SCORE_LOG2)
            total = jnp.sum(e, axis=-1, keepdims=True)
            out_ref[g * HEADS + h] = (e * (1.0 / total)).astype(jnp.bfloat16)


def time_weights(temporal_qk):
    rows = FRAMES * 16
    return pl.pallas_call(
        time_kernel,
        in_specs=[VMEM],
        out_specs=VMEM,
        out_shape=jax.ShapeDtypeStruct((2 * HEADS, rows, rows), jnp.bfloat16),
        compiler_params=pltpu.CompilerParams(vmem_limit_bytes=12 * MIB),
        cost_estimate=pl.CostEstimate(
            flops=4 * HEADS * rows * rows * HD,
            bytes_accessed=7_000_000,
            transcendentals=2 * HEADS * rows * rows,
        ),
        name="time_weights",
    )(temporal_qk)


def gathered_kernel(place_ref, mine_ref, other_ref, out_ref):
    core = place_ref[1]
    for m in range(CAPTIONS // 2):
        out_ref[2 * m + core] = mine_ref[m]
        out_ref[2 * m + 1 - core] = other_ref[m]


def gather_captions(caps, place):
    groups = [[2 * m + c for m in range(16)] for c in range(2)]
    mine = lax.all_gather(caps, "dp", axis=0, axis_index_groups=groups)
    other = lax.ppermute(mine, "dp", [(i, i ^ 1) for i in range(32)])
    return pl.pallas_call(
        gathered_kernel,
        in_specs=[SMEM, VMEM, VMEM],
        out_specs=VMEM,
        out_shape=jax.ShapeDtypeStruct((CAPTIONS, PADDED, EMB), jnp.bfloat16),
        compiler_params=pltpu.CompilerParams(vmem_limit_bytes=10 * MIB),
        cost_estimate=pl.CostEstimate(flops=0, bytes_accessed=5_200_000, transcendentals=0),
        name="gathered",
    )(place, mine, other)


def token_kernel(
    value, time_ref, proj_ref, cap_ref, emb_ref, stats_ref, grad_ref, comb
):
    rows = FRAMES * 16
    for g in range(LOCAL // 16):
        part = pl.ds(g * 16, 16)
        for h in range(HEADS):
            cols = pl.ds(h * HD, HD)
            v = value[:, part, cols].reshape(rows, HD)
            o = jnp.dot(time_ref[g * HEADS + h], v, preferred_element_type=jnp.float32)
            o = (v.astype(jnp.float32) + o).astype(jnp.bfloat16)
            comb[:, part, cols] = o.reshape(FRAMES, 16, HD)
    tokens = FRAMES * LOCAL
    projected = jnp.dot(
        comb[...].reshape(tokens, FEATURES), proj_ref[...], preferred_element_type=jnp.float32
    )
    scale = lax.rsqrt(jnp.mean(projected * projected, axis=-1, keepdims=True) + 1e-06)
    video = (projected * scale).astype(jnp.bfloat16)
    emb_ref[...] = video.reshape(FRAMES, LOCAL, EMB)

    eye = lax.broadcasted_iota(jnp.int32, (PADDED, 128), 0) == lax.broadcasted_iota(
        jnp.int32, (PADDED, 128), 1
    )
    group = 8
    for j0 in range(0, CAPTIONS, group):
        caps = cap_ref[pl.ds(j0, group)].reshape(group * PADDED, EMB)
        sim = nt(caps, video)
        top = jnp.max(sim, axis=-1, keepdims=True)
        w = jnp.exp2((sim - top) * SHARP_LOG2)
        total = jnp.sum(w, axis=-1, keepdims=True)
        for j in range(group):
            rng = slice(j * PADDED, (j + 1) * PADDED)
            top_row = jnp.sum(jnp.where(eye, top[rng], 0.0), axis=0, keepdims=True)
            total_row = jnp.sum(jnp.where(eye, total[rng], 0.0), axis=0, keepdims=True)
            for k in range(8):
                stats_ref[k, 0, pl.ds(j0 + j, 1), :] = top_row
                stats_ref[k, 1, pl.ds(j0 + j, 1), :] = total_row
        grad_ref[pl.ds(j0, group)] = jnp.dot(
            w.astype(jnp.bfloat16), video, preferred_element_type=jnp.float32
        ).reshape(group, PADDED, EMB)


def token_part(spatial, time, proj_weight, caps):
    return pl.pallas_call(
        token_kernel,
        in_specs=[VMEM] * 4,
        out_specs=[VMEM] * 3,
        out_shape=[
            jax.ShapeDtypeStruct((FRAMES, LOCAL, EMB), jnp.bfloat16),
            jax.ShapeDtypeStruct((8, 2, CAPTIONS, 128), jnp.float32),
            jax.ShapeDtypeStruct((CAPTIONS, PADDED, EMB), jnp.float32),
        ],
        scratch_shapes=[pltpu.VMEM((FRAMES, LOCAL, FEATURES), jnp.bfloat16)],
        compiler_params=pltpu.CompilerParams(vmem_limit_bytes=24 * MIB),
        cost_estimate=pl.CostEstimate(
            flops=4_000_000_000, bytes_accessed=16_000_000, transcendentals=1_300_000
        ),
        name="token_part",
    )(spatial, time, proj_weight, caps)


def coef_kernel(place_ref, pos_ref, stats_ref, lens_ref, grad_ref, send_ref, keep_ref, loss_ref, hold):
    tops = stats_ref[:, 0]
    totals = stats_ref[:, 1]
    top = jnp.max(tops, axis=0)
    total = jnp.sum(totals * jnp.exp2((tops - top[None]) * SHARP_LOG2), axis=0)
    soft = top + jnp.log(total) / SHARPNESS
    slot = lax.broadcasted_iota(jnp.int32, (CAPTIONS, 128), 1).astype(jnp.float32)
    lens = lens_ref[...].astype(jnp.float32)
    live = slot < lens
    lens_col = lens[:, :1]
    score = jnp.sum(jnp.where(live, soft, 0.0), axis=-1, keepdims=True) / lens_col
    logits = LOGIT_SCALE * score
    peak = jnp.max(logits, axis=0, keepdims=True)
    log_total = peak + jnp.log(jnp.sum(jnp.exp(logits - peak), axis=0, keepdims=True))
    onehot = lax.broadcasted_iota(jnp.int32, (CAPTIONS, 1), 0) == pos_ref[0]
    loss_ref[...] = log_total - jnp.sum(jnp.where(onehot, logits, 0.0), axis=0, keepdims=True)
    grad_logit = LOGIT_SCALE * (jnp.exp(logits - log_total) - onehot.astype(jnp.float32))
    coef = jnp.where(live, grad_logit / lens_col, 0.0)
    mine = stats_ref[place_ref[2] * 2 + place_ref[3], 0]
    hold[...] = coef * jnp.exp2((mine - soft) * SHARP_LOG2)
    eye = lax.broadcasted_iota(jnp.int32, (PADDED, 128), 0) == lax.broadcasted_iota(
        jnp.int32, (PADDED, 128), 1
    )
    core = place_ref[1]
    for m in range(CAPTIONS // 2):
        for j, ref in ((2 * m + 1 - core, send_ref), (2 * m + core, keep_ref)):
            col = jnp.sum(jnp.where(eye, hold[pl.ds(j, 1), :], 0.0), axis=-1, keepdims=True)
            ref[m] = (grad_ref[j] * col).astype(jnp.bfloat16)


def coef_part(place, pos, stats, lens, grad):
    half = jax.ShapeDtypeStruct((CAPTIONS // 2, PADDED, EMB), jnp.bfloat16)
    return pl.pallas_call(
        coef_kernel,
        in_specs=[SMEM, SMEM, VMEM, VMEM, VMEM],
        out_specs=[VMEM] * 3,
        out_shape=[half, half, jax.ShapeDtypeStruct((1, 1), jnp.float32)],
        scratch_shapes=[pltpu.VMEM((CAPTIONS, 128), jnp.float32)],
        compiler_params=pltpu.CompilerParams(vmem_limit_bytes=16 * MIB),
        cost_estimate=pl.CostEstimate(
            flops=4_000_000, bytes_accessed=8_000_000, transcendentals=100_000
        ),
        name="coef_part",
    )(place, pos, stats, lens, grad)


def small_call(kernel, name, operands, out_shapes, specs=None):
    return pl.pallas_call(
        kernel,
        in_specs=specs or [VMEM] * len(operands),
        out_specs=[VMEM] * len(out_shapes),
        out_shape=[jax.ShapeDtypeStruct(s, d) for s, d in out_shapes],
        compiler_params=pltpu.CompilerParams(vmem_limit_bytes=16 * MIB),
        cost_estimate=pl.CostEstimate(flops=0, bytes_accessed=2_000_000, transcendentals=0),
        name=name,
    )(*operands)


def added(a, b):
    return (a.astype(jnp.float32) + b.astype(jnp.float32)).astype(jnp.bfloat16)


def first_sum_kernel(place_ref, keep_ref, got_ref, a_keep, a_send, b_keep, b_send):
    x = place_ref[2]
    plan = (
        (0, ((a_keep, 0, 0), (a_send, 0, 1), (a_send, 1, 2), (a_keep, 1, 3))),
        (8, ((b_keep, 0, 0), (b_keep, 1, 1), (b_send, 1, 2), (b_send, 0, 3))),
    )
    for start, parts in plan:
        for ref, at, flip in parts:
            cols = pl.ds(pl.multiple_of((x ^ flip) * 128, 128), 128)
            for m in range(8):
                ref[m, :, pl.ds(at * 128, 128)] = added(
                    keep_ref[start + m, :, cols], got_ref[start + m, :, cols]
                )


def second_sum_kernel(a_keep, a_got, b_keep, b_got, a_mine, a_send, b_mine, b_send):
    for keep, got, mine, send in ((a_keep, a_got, a_mine, a_send), (b_keep, b_got, b_mine, b_send)):
        mine[...] = added(keep[:, :, :128], got[:, :, :128])
        send[...] = added(keep[:, :, 128:], got[:, :, 128:])


def third_sum_kernel(a_mine, a_got, b_mine, b_got, out):
    out[pl.ds(0, 8)] = added(a_mine[...], a_got[...])
    out[pl.ds(8, 8)] = added(b_mine[...], b_got[...])


def fourth_sum_kernel(parts, out):
    total = jnp.sum(parts[...].astype(jnp.float32), axis=0).astype(jnp.bfloat16)
    for k in range(8):
        out[k] = total


def last_sum_kernel(parts, out):
    for x in range(4):
        total = parts[2 * x].astype(jnp.float32) + parts[2 * x + 1].astype(jnp.float32)
        out[0, :, pl.ds(x * 128, 128)] = total[:SLOTS]


def reduce_gradient(place, send, keep):
    bf16 = jnp.bfloat16
    one = [(s, s ^ 2) for s in range(8)]
    three = [(s, s ^ 6) for s in range(8)]
    got = lax.ppermute(send, "dp", [(i, i ^ 1) for i in range(32)])
    a_keep, a_send, b_keep, b_send = small_call(
        first_sum_kernel, "first_sum", (place, keep, got), [((8, PADDED, 256), bf16)] * 4,
        [SMEM, VMEM, VMEM],
    )
    a_got = lax.ppermute(a_send, "space", one)
    b_got = lax.ppermute(b_send, "space", three)
    a_mine, a_send, b_mine, b_send = small_call(
        second_sum_kernel, "second_sum", (a_keep, a_got, b_keep, b_got),
        [((8, PADDED, 128), bf16)] * 4,
    )
    a_got = lax.ppermute(a_send, "space", three)
    b_got = lax.ppermute(b_send, "space", one)
    (parts,) = small_call(
        third_sum_kernel, "third_sum", (a_mine, a_got, b_mine, b_got), [((16, PADDED, 128), bf16)]
    )
    parts = lax.all_to_all(
        parts, "dp", split_axis=0, concat_axis=0, tiled=True,
        axis_index_groups=[[2 * m + c for m in range(16)] for c in range(2)],
    )
    (parts,) = small_call(fourth_sum_kernel, "fourth_sum", (parts,), [((8, PADDED, 128), bf16)])
    parts = lax.all_to_all(parts, "space", split_axis=0, concat_axis=0, tiled=True)
    return small_call(last_sum_kernel, "last_sum", (parts,), [((1, SLOTS, EMB), jnp.float32)])[0]


def on_device(clip_qkv, temporal_qk, proj_weight, caption_tokens, caption_lens, positive):
    dp = lax.axis_index("dp")
    space = lax.axis_index("space")
    x, y = space >> 1, space & 1
    place = jnp.stack([dp >> 4, dp & 1, x, y]).astype(jnp.int32)

    def frames_of(dx, dy):
        owner = ((x + dx) & 3) * 2 + (y ^ dy)
        return lax.dynamic_slice_in_dim(
            clip_qkv[0], owner * 2, 2, axis=0, allow_negative_indices=False
        )

    got = exchange(frames_of)
    lens_row = jnp.broadcast_to(
        caption_lens.astype(jnp.bfloat16)[:, None], (PADDED - SLOTS, EMB)
    )
    caps = gather_captions(jnp.concatenate([caption_tokens[0], lens_row], axis=0), place)
    time = time_weights(temporal_qk[0])
    pieces = [frames_of(0, 0)] + [piece for key in ORDER[1:] for piece in got[key]]
    attended = spatial_attention(place, pieces)
    spatial = lax.all_to_all(attended, "space", split_axis=0, concat_axis=0, tiled=True)
    video, stats, grad = token_part(
        spatial.reshape(FRAMES, LOCAL, FEATURES), time, proj_weight, caps
    )
    stats = lax.all_to_all(stats, "space", split_axis=0, concat_axis=0, tiled=True)
    send, keep, loss = coef_part(place, positive, stats, caps[:, SLOTS, :128], grad)
    caption_grad = reduce_gradient(place, send, keep)
    return video[None], caption_grad, loss.reshape(1)


def solution(mesh):
    return jax.shard_map(
        on_device,
        mesh=mesh,
        in_specs=(
            P("dp", None, "space", None),
            P("dp", None, "space", None),
            P(),
            P("dp", None, None),
            P("dp"),
            P("dp"),
        ),
        out_specs=(P("dp", None, "space", None), P("dp", None, None), P("dp")),
        check_vma=False,
    )
```

```python
import math

import jax
import jax.numpy as jnp
from jax import lax
from jax.experimental import pallas as pl
from jax.experimental.pallas import tpu as pltpu
from jax.sharding import PartitionSpec as P

HEADS = 13
HD = 128
FEATURES = HEADS * HD
EMB = 512
FRAMES = 16
PATCHES = 256
LOCAL = 32
SLOTS = 77
PADDED = 80
CAPTIONS = 32
SHARPNESS = 4.0
LOGIT_SCALE = 10.0
LOG2E = math.log2(math.e)
SCORE_LOG2 = HD ** (-0.5) * LOG2E
SHARP_LOG2 = SHARPNESS * LOG2E
MIB = 1 << 20
VMEM = pl.BlockSpec(memory_space=pltpu.VMEM)
SMEM = pl.BlockSpec(memory_space=pltpu.SMEM)

ANY = pl.BlockSpec(memory_space=pltpu.HBM)


def owner(g1, g0, y):
    return (g1 * 2 + (g0 ^ g1)) * 2 + y


QUADS = [[owner(g1, g0, y) for g0 in range(2) for y in range(2)] for g1 in range(2)]
ACROSS = [(s, s ^ 6) for s in range(8)]


def frame_place(frame):
    if frame < 8:
        quad, g1 = divmod(frame, 2)
        return owner(g1, quad // 2, quad % 2), 0
    g1, quad = divmod(frame - 8, 4)
    return owner(g1, quad // 2, quad % 2), 1


def nt(a, b):
    return lax.dot_general(a, b, (((1,), (1,)), ((), ())), preferred_element_type=jnp.float32)


def quad_exchange(blocks):
    return lax.all_to_all(
        blocks, "space", split_axis=0, concat_axis=0, axis_index_groups=QUADS, tiled=True
    )


def bring_frames(clip, g1):
    across = lax.ppermute(
        lax.dynamic_slice_in_dim(clip, 12 - 4 * g1, 4, allow_negative_indices=False),
        "space", ACROSS,
    )
    quad = quad_exchange(clip[:8].reshape(4, 2, LOCAL, 3 * FEATURES))
    turned = lax.dynamic_index_in_dim(
        quad, 1 - g1, axis=1, keepdims=False, allow_negative_indices=False
    )
    turned = lax.ppermute(turned, "space", ACROSS)
    far = quad_exchange(across)
    mine = lax.dynamic_slice_in_dim(clip, 8 + 4 * g1, 4, allow_negative_indices=False)
    mine, _ = lax.optimization_barrier((mine, across[0, 0, :128]))
    near = quad_exchange(mine)
    return quad, turned, near, far


def spatial_kernel(place_ref, quad_ref, turned_ref, near_ref, far_ref, out_ref, buf, res, sems):
    g1 = place_ref[2] >> 1
    arrivals = (
        (quad_ref.at[:, g1], buf.at[0, pl.ds(0, 4)]),
        (turned_ref, buf.at[0, pl.ds(4, 4)]),
        (near_ref, buf.at[1, pl.ds(0, 4)]),
        (far_ref, buf.at[1, pl.ds(4, 4)]),
    )
    loads = [
        pltpu.make_async_copy(src, dst, sems.at[i]) for i, (src, dst) in enumerate(arrivals)
    ]
    for load in loads:
        load.start()
    stores = [
        pltpu.make_async_copy(res.at[f], out_ref.at[:, f], sems.at[4 + f]) for f in range(2)
    ]
    for f in range(2):
        loads[2 * f].wait()
        loads[2 * f + 1].wait()
        for h in range(HEADS):
            q = buf[f, :, :, pl.ds(h * HD, HD)].reshape(PATCHES, HD)
            k = buf[f, :, :, pl.ds(FEATURES + h * HD, HD)].reshape(PATCHES, HD)
            v = buf[f, :, :, pl.ds(2 * FEATURES + h * HD, HD)].reshape(PATCHES, HD)
            s = nt(q, k)
            m = jnp.max(s, axis=-1, keepdims=True)
            e = jnp.exp2((s - m) * SCORE_LOG2)
            total = jnp.sum(e, axis=-1, keepdims=True)
            o = jnp.dot(e.astype(jnp.bfloat16), v, preferred_element_type=jnp.float32)
            o = (o / total).astype(jnp.bfloat16)
            for i in range(8):
                side = g1 if i < 4 else 1 - g1
                at = owner(side, (i & 3) >> 1, i & 1)
                res[f, at, :, pl.ds(h * HD, HD)] = o[i * LOCAL : (i + 1) * LOCAL]
        stores[f].start()
    for store in stores:
        store.wait()


def spatial_attention(place, pieces):
    return pl.pallas_call(
        spatial_kernel,
        in_specs=[SMEM] + [ANY] * 4,
        out_specs=ANY,
        out_shape=jax.ShapeDtypeStruct((8, 2, LOCAL, FEATURES), jnp.bfloat16),
        scratch_shapes=[
            pltpu.VMEM((2, 8, LOCAL, 3 * FEATURES), jnp.bfloat16),
            pltpu.VMEM((2, 8, LOCAL, FEATURES), jnp.bfloat16),
            pltpu.SemaphoreType.DMA((6,)),
        ],
        compiler_params=pltpu.CompilerParams(vmem_limit_bytes=24 * MIB),
        cost_estimate=pl.CostEstimate(
            flops=8 * HEADS * PATCHES * PATCHES * HD,
            bytes_accessed=2 * PATCHES * 4 * FEATURES * 2,
            transcendentals=2 * HEADS * PATCHES * PATCHES,
        ),
        name="spatial_attention",
    )(place, *pieces)


def time_kernel(tqk_ref, out_ref, tqk, weights, load_sem, sems):
    load = pltpu.make_async_copy(tqk_ref, tqk, load_sem)
    load.start()
    load.wait()
    rows = FRAMES * 16
    r = lax.broadcasted_iota(jnp.int32, (rows, rows), 0)
    c = lax.broadcasted_iota(jnp.int32, (rows, rows), 1)
    bias = jnp.where((r & 15) == (c & 15), 0.0, -1e30).astype(jnp.float32)
    stores = []
    for h in range(HEADS):
        for g in range(LOCAL // 16):
            part = pl.ds(g * 16, 16)
            q = tqk[:, part, pl.ds(h * HD, HD)].reshape(rows, HD)
            k = tqk[:, part, pl.ds(FEATURES + h * HD, HD)].reshape(rows, HD)
            s = nt(q, k) + bias
            m = jnp.max(s, axis=-1, keepdims=True)
            e = jnp.exp2((s - m) * SCORE_LOG2)
            total = jnp.sum(e, axis=-1, keepdims=True)
            weights[h, g] = (e * (1.0 / total)).astype(jnp.bfloat16)
        stores.append(pltpu.make_async_copy(weights.at[h], out_ref.at[h], sems.at[h]))
        stores[-1].start()
    for store in stores:
        store.wait()


def time_weights(temporal_qk):
    rows = FRAMES * 16
    return pl.pallas_call(
        time_kernel,
        in_specs=[ANY],
        out_specs=ANY,
        out_shape=jax.ShapeDtypeStruct((HEADS, 2, rows, rows), jnp.bfloat16),
        scratch_shapes=[
            pltpu.VMEM((FRAMES, LOCAL, 2 * FEATURES), jnp.bfloat16),
            pltpu.VMEM((HEADS, 2, rows, rows), jnp.bfloat16),
            pltpu.SemaphoreType.DMA,
            pltpu.SemaphoreType.DMA((HEADS,)),
        ],
        compiler_params=pltpu.CompilerParams(vmem_limit_bytes=24 * MIB),
        cost_estimate=pl.CostEstimate(
            flops=4 * HEADS * rows * rows * HD,
            bytes_accessed=7_000_000,
            transcendentals=2 * HEADS * rows * rows,
        ),
        name="time_weights",
    )(temporal_qk)


def gathered_kernel(place_ref, mine_ref, other_ref, out_ref, sems):
    y_hi, core, z = place_ref[0], place_ref[1], place_ref[4]
    copies = []
    for m in range(CAPTIONS // 2):
        at = (y_hi ^ (m & 1)) * 16
        flips = (m >> 3 & 1) + (m >> 2 & 1) * 2 + (m >> 1 & 1) * 4
        at = at + (z ^ flips) * 2
        for i, (ref, c) in enumerate(((mine_ref, core), (other_ref, 1 - core))):
            copies.append(
                pltpu.make_async_copy(ref.at[m], out_ref.at[at + c], sems.at[2 * m + i])
            )
            copies[-1].start()
    for copy in copies:
        copy.wait()


def flip(value, bit):
    return lax.ppermute(value, "dp", [(i, i ^ bit) for i in range(32)])


def doubled(value, bit):
    return jnp.concatenate([value, flip(value, bit)], axis=0)


def after(value, *others):
    return lax.optimization_barrier((value,) + others)[0]


def gather_captions(caps, place, first, second, third):
    got = doubled(caps, 16)
    got = doubled(after(got, first), 8)
    got = doubled(after(got, second), 4)
    got = doubled(got, 2)
    got = after(got, third)
    other = flip(got, 1)
    return pl.pallas_call(
        gathered_kernel,
        in_specs=[SMEM, ANY, ANY],
        out_specs=ANY,
        out_shape=jax.ShapeDtypeStruct((CAPTIONS, PADDED, EMB), jnp.bfloat16),
        scratch_shapes=[pltpu.SemaphoreType.DMA((CAPTIONS,))],
        compiler_params=pltpu.CompilerParams(vmem_limit_bytes=4 * MIB),
        cost_estimate=pl.CostEstimate(flops=0, bytes_accessed=5_200_000, transcendentals=0),
        name="gathered",
    )(place, got, other)


SPLIT = 7


def token_kernel(
    value_ref, time_ref, proj_ref, cap_ref, emb_ref, stats_ref, w_ref,
    value, time, proj, caps, comb, video, weights, value_sems, time_sems, sems, w_sems,
):
    cut = pl.ds(0, SPLIT * HD), pl.ds(SPLIT * HD, (HEADS - SPLIT) * HD)
    value_loads = [
        pltpu.make_async_copy(value_ref.at[:, :, :, c], value.at[:, :, :, c], value_sems.at[i])
        for i, c in enumerate(cut)
    ]
    time_loads = [
        pltpu.make_async_copy(time_ref.at[h], time.at[h], time_sems.at[h]) for h in range(HEADS)
    ]
    proj_load = pltpu.make_async_copy(proj_ref, proj, sems.at[0])
    cap_load = pltpu.make_async_copy(cap_ref, caps, sems.at[1])
    value_loads[0].start()
    for h in range(SPLIT):
        time_loads[h].start()
    value_loads[1].start()
    for h in range(SPLIT, HEADS):
        time_loads[h].start()
    proj_load.start()
    cap_load.start()
    rows = FRAMES * 16
    for h in range(HEADS):
        if h in (0, SPLIT):
            value_loads[h // SPLIT].wait()
        time_loads[h].wait()
        cols = pl.ds(h * HD, HD)
        for g in range(LOCAL // 16):
            part = pl.ds(g * 16, 16)
            v = jnp.concatenate(
                [value[at, f, part, cols] for at, f in map(frame_place, range(FRAMES))], axis=0
            )
            o = jnp.dot(time[h, g], v, preferred_element_type=jnp.float32)
            o = (v.astype(jnp.float32) + o).astype(jnp.bfloat16)
            comb[:, part, cols] = o.reshape(FRAMES, 16, HD)
    tokens = FRAMES * LOCAL
    proj_load.wait()
    projected = jnp.dot(
        comb[...].reshape(tokens, FEATURES), proj[...], preferred_element_type=jnp.float32
    )
    scale = lax.rsqrt(jnp.mean(projected * projected, axis=-1, keepdims=True) + 1e-06)
    emb = (projected * scale).astype(jnp.bfloat16)
    video[...] = emb.reshape(FRAMES, LOCAL, EMB)
    emb_store = pltpu.make_async_copy(video, emb_ref, sems.at[2])
    emb_store.start()
    cap_load.wait()

    eye = lax.broadcasted_iota(jnp.int32, (PADDED, 128), 0) == lax.broadcasted_iota(
        jnp.int32, (PADDED, 128), 1
    )
    group = 8
    stores = []
    for j0 in range(0, CAPTIONS, group):
        block = pl.ds(j0, group)
        sim = nt(caps[block].reshape(group * PADDED, EMB), emb)
        top = jnp.max(sim, axis=-1, keepdims=True)
        w = jnp.exp2((sim - top) * SHARP_LOG2)
        total = jnp.sum(w, axis=-1, keepdims=True)
        weights[block] = w.astype(jnp.bfloat16).reshape(group, PADDED, EMB)
        stores.append(
            pltpu.make_async_copy(weights.at[block], w_ref.at[block], w_sems.at[j0 // group])
        )
        stores[-1].start()
        for j in range(group):
            rng = slice(j * PADDED, (j + 1) * PADDED)
            top_row = jnp.sum(jnp.where(eye, top[rng], 0.0), axis=0, keepdims=True)
            total_row = jnp.sum(jnp.where(eye, total[rng], 0.0), axis=0, keepdims=True)
            for k in range(8):
                stats_ref[k, 0, pl.ds(j0 + j, 1), :] = top_row
                stats_ref[k, 1, pl.ds(j0 + j, 1), :] = total_row
    emb_store.wait()
    for store in stores:
        store.wait()


def token_part(spatial, time, proj_weight, caps):
    bf16 = jnp.bfloat16
    return pl.pallas_call(
        token_kernel,
        in_specs=[ANY] * 4,
        out_specs=[ANY, VMEM, ANY],
        out_shape=[
            jax.ShapeDtypeStruct((FRAMES, LOCAL, EMB), bf16),
            jax.ShapeDtypeStruct((8, 2, CAPTIONS, 128), jnp.float32),
            jax.ShapeDtypeStruct((CAPTIONS, PADDED, FRAMES * LOCAL), bf16),
        ],
        scratch_shapes=[
            pltpu.VMEM((8, 2, LOCAL, FEATURES), bf16),
            pltpu.VMEM((HEADS, 2, FRAMES * 16, FRAMES * 16), bf16),
            pltpu.VMEM((FEATURES, EMB), bf16),
            pltpu.VMEM((CAPTIONS, PADDED, EMB), bf16),
            pltpu.VMEM((FRAMES, LOCAL, FEATURES), bf16),
            pltpu.VMEM((FRAMES, LOCAL, EMB), bf16),
            pltpu.VMEM((CAPTIONS, PADDED, FRAMES * LOCAL), bf16),
            pltpu.SemaphoreType.DMA((2,)),
            pltpu.SemaphoreType.DMA((HEADS,)),
            pltpu.SemaphoreType.DMA((3,)),
            pltpu.SemaphoreType.DMA((4,)),
        ],
        compiler_params=pltpu.CompilerParams(vmem_limit_bytes=40 * MIB),
        cost_estimate=pl.CostEstimate(
            flops=2_700_000_000, bytes_accessed=13_000_000, transcendentals=1_300_000
        ),
        name="token_part",
    )(spatial, time, proj_weight, caps)


def product_kernel(w_ref, video_ref, out_ref):
    group = w_ref.shape[0]
    video = video_ref[...].reshape(FRAMES * LOCAL, EMB)
    g = jnp.dot(
        w_ref[...].reshape(group * PADDED, FRAMES * LOCAL), video,
        preferred_element_type=jnp.float32,
    )
    out_ref[...] = g.astype(jnp.bfloat16).reshape(group, PADDED, EMB)


def gradient_product(w, video):
    group = 8
    return pl.pallas_call(
        product_kernel,
        grid=(CAPTIONS // group,),
        in_specs=[
            pl.BlockSpec((group, PADDED, FRAMES * LOCAL), lambda i: (i, 0, 0)),
            pl.BlockSpec((FRAMES, LOCAL, EMB), lambda i: (0, 0, 0)),
        ],
        out_specs=pl.BlockSpec((group, PADDED, EMB), lambda i: (i, 0, 0)),
        out_shape=jax.ShapeDtypeStruct((CAPTIONS, PADDED, EMB), jnp.bfloat16),
        compiler_params=pltpu.CompilerParams(vmem_limit_bytes=16 * MIB),
        cost_estimate=pl.CostEstimate(
            flops=1_340_000_000, bytes_accessed=6_000_000, transcendentals=0
        ),
        name="gradient_product",
    )(w, video)


def coef_kernel(place_ref, pos_ref, stats_ref, lens_ref, grad_ref, send_ref, keep_ref, loss_ref, hold):
    @pl.when(pl.program_id(0) == 0)
    def _():
        tops = stats_ref[:, 0]
        totals = stats_ref[:, 1]
        top = jnp.max(tops, axis=0)
        total = jnp.sum(totals * jnp.exp2((tops - top[None]) * SHARP_LOG2), axis=0)
        soft = top + jnp.log(total) / SHARPNESS
        slot = lax.broadcasted_iota(jnp.int32, (CAPTIONS, 128), 1).astype(jnp.float32)
        lens = lens_ref[...].astype(jnp.float32)
        live = slot < lens
        lens_col = lens[:, :1]
        score = jnp.sum(jnp.where(live, soft, 0.0), axis=-1, keepdims=True) / lens_col
        logits = LOGIT_SCALE * score
        peak = jnp.max(logits, axis=0, keepdims=True)
        log_total = peak + jnp.log(jnp.sum(jnp.exp(logits - peak), axis=0, keepdims=True))
        onehot = lax.broadcasted_iota(jnp.int32, (CAPTIONS, 1), 0) == pos_ref[0]
        loss_ref[...] = log_total - jnp.sum(jnp.where(onehot, logits, 0.0), axis=0, keepdims=True)
        grad_logit = LOGIT_SCALE * (jnp.exp(logits - log_total) - onehot.astype(jnp.float32))
        coef = jnp.where(live, grad_logit / lens_col, 0.0)
        mine = stats_ref[place_ref[2] * 2 + place_ref[3], 0]
        hold[...] = coef * jnp.exp2((mine - soft) * SHARP_LOG2)

    eye = lax.broadcasted_iota(jnp.int32, (PADDED, 128), 0) == lax.broadcasted_iota(
        jnp.int32, (PADDED, 128), 1
    )
    core = place_ref[1]
    half = send_ref.shape[0]
    start = pl.program_id(0) * 2 * half
    for m in range(half):
        for j, ref in ((2 * m + 1 - core, send_ref), (2 * m + core, keep_ref)):
            row = hold[pl.ds(start + j, 1), :]
            col = jnp.sum(jnp.where(eye, row, 0.0), axis=-1, keepdims=True)
            ref[m] = (grad_ref[j].astype(jnp.float32) * col).astype(jnp.bfloat16)


def coef_part(place, pos, stats, lens, grad):
    half = jax.ShapeDtypeStruct((CAPTIONS // 2, PADDED, EMB), jnp.bfloat16)
    steps = 4
    some = CAPTIONS // 2 // steps
    return pl.pallas_call(
        coef_kernel,
        grid=(steps,),
        in_specs=[
            SMEM,
            SMEM,
            pl.BlockSpec((8, 2, CAPTIONS, 128), lambda i: (0, 0, 0, 0)),
            pl.BlockSpec((CAPTIONS, 128), lambda i: (0, 0)),
            pl.BlockSpec((2 * some, PADDED, EMB), lambda i: (i, 0, 0)),
        ],
        out_specs=[
            pl.BlockSpec((some, PADDED, EMB), lambda i: (i, 0, 0)),
            pl.BlockSpec((some, PADDED, EMB), lambda i: (i, 0, 0)),
            pl.BlockSpec((1, 1), lambda i: (0, 0)),
        ],
        out_shape=[half, half, jax.ShapeDtypeStruct((1, 1), jnp.float32)],
        scratch_shapes=[pltpu.VMEM((CAPTIONS, 128), jnp.float32)],
        compiler_params=pltpu.CompilerParams(vmem_limit_bytes=16 * MIB),
        cost_estimate=pl.CostEstimate(
            flops=4_000_000, bytes_accessed=6_000_000, transcendentals=100_000
        ),
        name="coef_part",
    )(place, pos, stats, lens, grad)


def small_call(kernel, name, operands, out_shapes, specs=None):
    return pl.pallas_call(
        kernel,
        in_specs=specs or [VMEM] * len(operands),
        out_specs=[VMEM] * len(out_shapes),
        out_shape=[jax.ShapeDtypeStruct(s, d) for s, d in out_shapes],
        compiler_params=pltpu.CompilerParams(vmem_limit_bytes=16 * MIB),
        cost_estimate=pl.CostEstimate(flops=0, bytes_accessed=2_000_000, transcendentals=0),
        name=name,
    )(*operands)


def added(a, b):
    return (a.astype(jnp.float32) + b.astype(jnp.float32)).astype(jnp.bfloat16)


def first_sum_kernel(place_ref, keep_ref, got_ref, a_keep, a_send, b_keep, b_send):
    x = place_ref[2]
    plan = (
        (0, ((a_keep, 0, 0), (a_send, 0, 1), (a_send, 1, 2), (a_keep, 1, 3))),
        (8, ((b_keep, 0, 0), (b_keep, 1, 1), (b_send, 1, 2), (b_send, 0, 3))),
    )
    for start, parts in plan:
        for ref, at, flip in parts:
            cols = pl.ds(pl.multiple_of((x ^ flip) * 128, 128), 128)
            for m in range(8):
                ref[m, :, pl.ds(at * 128, 128)] = added(
                    keep_ref[start + m, :, cols], got_ref[start + m, :, cols]
                )


def second_sum_kernel(a_keep, a_got, b_keep, b_got, a_mine, a_send, b_mine, b_send):
    for keep, got, mine, send in ((a_keep, a_got, a_mine, a_send), (b_keep, b_got, b_mine, b_send)):
        mine[...] = added(keep[:, :, :128], got[:, :, :128])
        send[...] = added(keep[:, :, 128:], got[:, :, 128:])


def third_sum_kernel(a_mine, a_got, b_mine, b_got, out):
    out[pl.ds(0, 8)] = added(a_mine[...], a_got[...])
    out[pl.ds(8, 8)] = added(b_mine[...], b_got[...])


def fourth_sum_kernel(parts, out):
    total = jnp.sum(parts[...].astype(jnp.float32), axis=0).astype(jnp.bfloat16)
    for k in range(8):
        out[k] = total


def last_sum_kernel(parts, out):
    for x in range(4):
        total = parts[2 * x].astype(jnp.float32) + parts[2 * x + 1].astype(jnp.float32)
        out[0, :, pl.ds(x * 128, 128)] = total[:SLOTS]


def reduce_gradient(place, send, keep):
    bf16 = jnp.bfloat16
    one = [(s, s ^ 2) for s in range(8)]
    three = [(s, s ^ 6) for s in range(8)]
    got = lax.ppermute(send, "dp", [(i, i ^ 1) for i in range(32)])
    a_keep, a_send, b_keep, b_send = small_call(
        first_sum_kernel, "first_sum", (place, keep, got), [((8, PADDED, 256), bf16)] * 4,
        [SMEM, VMEM, VMEM],
    )
    a_got = lax.ppermute(a_send, "space", one)
    b_got = lax.ppermute(b_send, "space", three)
    a_mine, a_send, b_mine, b_send = small_call(
        second_sum_kernel, "second_sum", (a_keep, a_got, b_keep, b_got),
        [((8, PADDED, 128), bf16)] * 4,
    )
    a_got = lax.ppermute(a_send, "space", three)
    b_got = lax.ppermute(b_send, "space", one)
    (parts,) = small_call(
        third_sum_kernel, "third_sum", (a_mine, a_got, b_mine, b_got), [((16, PADDED, 128), bf16)]
    )
    parts = lax.all_to_all(
        parts, "dp", split_axis=0, concat_axis=0, tiled=True,
        axis_index_groups=[[2 * m + c for m in range(16)] for c in range(2)],
    )
    (parts,) = small_call(fourth_sum_kernel, "fourth_sum", (parts,), [((8, PADDED, 128), bf16)])
    parts = lax.all_to_all(parts, "space", split_axis=0, concat_axis=0, tiled=True)
    return small_call(last_sum_kernel, "last_sum", (parts,), [((1, SLOTS, EMB), jnp.float32)])[0]


def on_device(clip_qkv, temporal_qk, proj_weight, caption_tokens, caption_lens, positive):
    dp = lax.axis_index("dp")
    space = lax.axis_index("space")
    x, y = space >> 1, space & 1
    place = jnp.stack([dp >> 4, dp & 1, x, y, (dp >> 1) & 7]).astype(jnp.int32)
    lens_row = jnp.broadcast_to(
        caption_lens.astype(jnp.bfloat16)[:, None, None], (1, PADDED - SLOTS, EMB)
    )
    caps = jnp.concatenate([caption_tokens, lens_row], axis=1)
    pieces = bring_frames(clip_qkv[0], space >> 2)
    time = time_weights(temporal_qk[0])
    attended = spatial_attention(place, pieces)
    caps = gather_captions(
        caps, place, time[0, 0, 0, :128], pieces[0][0, 0, 0, :128], attended[0, 0, 0, :128]
    )
    spatial = lax.all_to_all(attended, "space", split_axis=0, concat_axis=0, tiled=True)
    video, stats, weights = token_part(spatial, time, proj_weight, caps)
    stats = lax.all_to_all(stats, "space", split_axis=0, concat_axis=0, tiled=True)
    grad = gradient_product(weights, video)
    send, keep, loss = coef_part(place, positive, stats, caps[:, SLOTS, :128], grad)
    caption_grad = reduce_gradient(place, send, keep)
    return video[None], caption_grad, loss.reshape(1)


def solution(mesh):
    return jax.shard_map(
        on_device,
        mesh=mesh,
        in_specs=(
            P("dp", None, "space", None),
            P("dp", None, "space", None),
            P(),
            P("dp", None, None),
            P("dp"),
            P("dp"),
        ),
        out_specs=(P("dp", None, "space", None), P("dp", None, None), P("dp")),
        check_vma=False,
    )
```

```python
import math

import jax
import jax.numpy as jnp
from jax import lax
from jax.experimental import pallas as pl
from jax.experimental.pallas import tpu as pltpu
from jax.sharding import PartitionSpec as P

HEADS = 13
HD = 128
FEATURES = HEADS * HD
EMB = 512
FRAMES = 16
PATCHES = 256
LOCAL = 32
SLOTS = 77
PADDED = 80
CAPTIONS = 32
SHARPNESS = 4.0
LOGIT_SCALE = 10.0
LOG2E = math.log2(math.e)
SCORE_LOG2 = HD ** (-0.5) * LOG2E
SHARP_LOG2 = SHARPNESS * LOG2E
MIB = 1 << 20
GRANT = pltpu.CompilerParams(vmem_limit_bytes=24 * MIB)
VMEM = pl.BlockSpec(memory_space=pltpu.VMEM)
SMEM = pl.BlockSpec(memory_space=pltpu.SMEM)

FAR_OFF = pl.BlockSpec(memory_space=pltpu.HBM)
ANY = pl.BlockSpec(memory_space=pl.ANY)

def held(value):
    return pltpu.with_memory_space_constraint(value, pltpu.HBM)


def nt(a, b):
    return lax.dot_general(a, b, (((1,), (1,)), ((), ())), preferred_element_type=jnp.float32)


SPLIT = 7


def spatial_kernel(qkv_ref, out_ref):
    for h in range(HEADS):
        q = qkv_ref[:, 0, :, pl.ds(h * HD, HD)].reshape(PATCHES, HD)
        k = qkv_ref[:, 0, :, pl.ds(FEATURES + h * HD, HD)].reshape(PATCHES, HD)
        v = qkv_ref[:, 0, :, pl.ds(2 * FEATURES + h * HD, HD)].reshape(PATCHES, HD)
        s = nt(q, k)
        m = jnp.max(s, axis=-1, keepdims=True)
        e = jnp.exp2((s - m) * SCORE_LOG2)
        total = jnp.sum(e, axis=-1, keepdims=True)
        o = jnp.dot(e.astype(jnp.bfloat16), v, preferred_element_type=jnp.float32)
        o = (o * (1.0 / total)).astype(jnp.bfloat16)
        out_ref[:, 0, :, pl.ds(h * HD, HD)] = o.reshape(8, LOCAL, HD)


def spatial_attention(blocks):
    return pl.pallas_call(
        spatial_kernel,
        grid=(2,),
        in_specs=[pl.BlockSpec((8, 1, LOCAL, 3 * FEATURES), lambda f: (0, f, 0, 0))],
        out_specs=pl.BlockSpec((8, 1, LOCAL, FEATURES), lambda f: (0, f, 0, 0)),
        out_shape=pltpu.HBM((8, 2, LOCAL, FEATURES), jnp.bfloat16),
        compiler_params=GRANT,
        cost_estimate=pl.CostEstimate(
            flops=8 * HEADS * PATCHES * PATCHES * HD,
            bytes_accessed=2 * PATCHES * 4 * FEATURES * 2,
            transcendentals=2 * HEADS * PATCHES * PATCHES,
        ),
        name="spatial_attention",
    )(blocks)


ROWS = FRAMES * 16


def time_kernel(tqk_ref, out_ref, tqk, weights, load_sem, sems):
    load = pltpu.make_async_copy(tqk_ref, tqk, load_sem)
    load.start()
    load.wait()
    r = lax.broadcasted_iota(jnp.int32, (ROWS, ROWS), 0)
    c = lax.broadcasted_iota(jnp.int32, (ROWS, ROWS), 1)
    bias = jnp.where((r & 15) == (c & 15), 0.0, -1e30).astype(jnp.float32)
    stores = []
    for h in range(HEADS):
        for g in range(LOCAL // 16):
            part = pl.ds(g * 16, 16)
            q = tqk[:, part, pl.ds(h * HD, HD)].reshape(ROWS, HD)
            k = tqk[:, part, pl.ds(FEATURES + h * HD, HD)].reshape(ROWS, HD)
            s = nt(q, k) + bias
            m = jnp.max(s, axis=-1, keepdims=True)
            e = jnp.exp2((s - m) * SCORE_LOG2)
            total = jnp.sum(e, axis=-1, keepdims=True)
            weights[h, g] = (e * (1.0 / total)).astype(jnp.bfloat16)
        stores.append(pltpu.make_async_copy(weights.at[h], out_ref.at[h], sems.at[h]))
        stores[-1].start()
    for store in stores:
        store.wait()


def time_weights(temporal_qk):
    return pl.pallas_call(
        time_kernel,
        in_specs=[FAR_OFF],
        out_specs=FAR_OFF,
        out_shape=pltpu.HBM((HEADS, 2, ROWS, ROWS), jnp.bfloat16),
        scratch_shapes=[
            pltpu.VMEM((FRAMES, LOCAL, 2 * FEATURES), jnp.bfloat16),
            pltpu.VMEM((HEADS, 2, ROWS, ROWS), jnp.bfloat16),
            pltpu.SemaphoreType.DMA,
            pltpu.SemaphoreType.DMA((HEADS,)),
        ],
        compiler_params=GRANT,
        cost_estimate=pl.CostEstimate(
            flops=4 * HEADS * ROWS * ROWS * HD,
            bytes_accessed=7_000_000,
            transcendentals=2 * HEADS * ROWS * ROWS,
        ),
        name="time_weights",
    )(held(temporal_qk))


def flip(value, bit):
    return lax.ppermute(value, "dp", [(i, i ^ bit) for i in range(32)])


def join_kernel(*refs):
    refs[-1][0] = refs[0][...]
    refs[-1][1] = refs[1][...]


def doubled(value, bit, *behind):
    both = pl.pallas_call(
        join_kernel,
        in_specs=[VMEM] * 2 + [ANY] * len(behind),
        out_specs=VMEM,
        out_shape=jax.ShapeDtypeStruct((2,) + value.shape, value.dtype),
        compiler_params=pltpu.CompilerParams(vmem_limit_bytes=8 * MIB),
        cost_estimate=pl.CostEstimate(flops=0, bytes_accessed=1_000_000, transcendentals=0),
        name="join",
    )(value, flip(value, bit), *behind)
    return both.reshape((-1,) + value.shape[1:])


def token_kernel(
    place_ref, value, time_ref, proj_ref, mine_ref, other_ref,
    emb_ref, stats_ref, grad_ref, lens_ref,
    proj, mine, comb, video, grads, sems, grad_sems,
):
    proj_load = pltpu.make_async_copy(proj_ref, proj, sems.at[0])
    mine_load = pltpu.make_async_copy(mine_ref, mine, sems.at[1])
    proj_load.start()
    mine_load.start()
    for h in range(HEADS):
        cols = pl.ds(h * HD, HD)
        for g in range(LOCAL // 16):
            part = pl.ds(g * 16, 16)
            v = value[:, :, part, cols].reshape(ROWS, HD)
            o = jnp.dot(time_ref[h, g], v, preferred_element_type=jnp.float32)
            o = (v.astype(jnp.float32) + o).astype(jnp.bfloat16)
            comb[:, part, cols] = o.reshape(FRAMES, 16, HD)
    tokens = FRAMES * LOCAL
    proj_load.wait()
    projected = jnp.dot(
        comb[...].reshape(tokens, FEATURES), proj[...], preferred_element_type=jnp.float32
    )
    scale = lax.rsqrt(jnp.mean(projected * projected, axis=-1, keepdims=True) + 1e-06)
    emb = (projected * scale).astype(jnp.bfloat16)
    video[...] = emb.reshape(FRAMES, LOCAL, EMB)
    emb_store = pltpu.make_async_copy(video, emb_ref, sems.at[2])
    emb_store.start()
    mine_load.wait()

    eye = lax.broadcasted_iota(jnp.int32, (PADDED, 128), 0) == lax.broadcasted_iota(
        jnp.int32, (PADDED, 128), 1
    )
    y_hi, core, z = place_ref[0], place_ref[1], place_ref[4]
    group = 8
    stores = []
    for i, (ref, c) in enumerate(((mine, core), (other_ref, 1 - core))):
        for m0 in range(0, CAPTIONS // 2, group):
            sim = nt(ref[pl.ds(m0, group)].reshape(group * PADDED, EMB), emb)
            top = jnp.max(sim, axis=-1, keepdims=True)
            w = jnp.exp2((sim - top) * SHARP_LOG2)
            total = jnp.sum(w, axis=-1, keepdims=True)
            product = jnp.dot(w.astype(jnp.bfloat16), emb, preferred_element_type=jnp.float32)
            slot = i * CAPTIONS // 2 + m0
            grads[pl.ds(slot, group)] = product.astype(jnp.bfloat16).reshape(group, PADDED, EMB)
            for j in range(group):
                m = m0 + j
                flips = (m >> 3 & 1) + (m >> 2 & 1) * 2 + (m >> 1 & 1) * 4
                at = (y_hi ^ (m & 1)) * 16 + (z ^ flips) * 2 + c
                stores.append(
                    pltpu.make_async_copy(
                        grads.at[slot + j], grad_ref.at[at], grad_sems.at[slot + j]
                    )
                )
                stores[-1].start()
                rng = slice(j * PADDED, (j + 1) * PADDED)
                top_row = jnp.sum(jnp.where(eye, top[rng], 0.0), axis=0, keepdims=True)
                total_row = jnp.sum(jnp.where(eye, total[rng], 0.0), axis=0, keepdims=True)
                for k in range(8):
                    stats_ref[k, 0, pl.ds(at, 1), :] = top_row
                    stats_ref[k, 1, pl.ds(at, 1), :] = total_row
                lens_ref[pl.ds(at, 1), :] = ref[m, SLOTS : SLOTS + 1, :128].astype(jnp.float32)
    emb_store.wait()
    for store in stores:
        store.wait()


def token_part(place, spatial, time, proj_weight, mine, other):
    bf16 = jnp.bfloat16
    return pl.pallas_call(
        token_kernel,
        in_specs=[SMEM, VMEM, VMEM, FAR_OFF, FAR_OFF, VMEM],
        out_specs=[FAR_OFF, VMEM, FAR_OFF, VMEM],
        out_shape=[
            pltpu.HBM((FRAMES, LOCAL, EMB), bf16),
            jax.ShapeDtypeStruct((8, 2, CAPTIONS, 128), jnp.float32),
            pltpu.HBM((CAPTIONS, PADDED, EMB), bf16),
            jax.ShapeDtypeStruct((CAPTIONS, 128), jnp.float32),
        ],
        scratch_shapes=[
            pltpu.VMEM((FEATURES, EMB), bf16),
            pltpu.VMEM((CAPTIONS // 2, PADDED, EMB), bf16),
            pltpu.VMEM((FRAMES, LOCAL, FEATURES), bf16),
            pltpu.VMEM((FRAMES, LOCAL, EMB), bf16),
            pltpu.VMEM((CAPTIONS, PADDED, EMB), bf16),
            pltpu.SemaphoreType.DMA((3,)),
            pltpu.SemaphoreType.DMA((CAPTIONS,)),
        ],
        compiler_params=GRANT,
        cost_estimate=pl.CostEstimate(
            flops=4_500_000_000, bytes_accessed=12_000_000, transcendentals=1_300_000
        ),
        name="token_part",
    )(place, spatial, time, held(proj_weight), held(mine), other)


def coef_kernel(
    place_ref, pos_ref, stats_ref, lens_ref, grad_ref, send_ref, keep_ref, loss_ref, hold, grad, sems
):
    group = 8
    loads = [
        pltpu.make_async_copy(
            grad_ref.at[pl.ds(group * i, group)], grad.at[pl.ds(group * i, group)], sems.at[i]
        )
        for i in range(CAPTIONS // group)
    ]
    for load in loads:
        load.start()
    tops = stats_ref[:, 0]
    totals = stats_ref[:, 1]
    top = jnp.max(tops, axis=0)
    total = jnp.sum(totals * jnp.exp2((tops - top[None]) * SHARP_LOG2), axis=0)
    soft = top + jnp.log(total) / SHARPNESS
    slot = lax.broadcasted_iota(jnp.int32, (CAPTIONS, 128), 1).astype(jnp.float32)
    lens = lens_ref[...]
    live = slot < lens
    lens_col = lens[:, :1]
    score = jnp.sum(jnp.where(live, soft, 0.0), axis=-1, keepdims=True) / lens_col
    logits = LOGIT_SCALE * score
    peak = jnp.max(logits, axis=0, keepdims=True)
    log_total = peak + jnp.log(jnp.sum(jnp.exp(logits - peak), axis=0, keepdims=True))
    onehot = lax.broadcasted_iota(jnp.int32, (CAPTIONS, 1), 0) == pos_ref[0]
    loss_ref[...] = log_total - jnp.sum(jnp.where(onehot, logits, 0.0), axis=0, keepdims=True)
    grad_logit = LOGIT_SCALE * (jnp.exp(logits - log_total) - onehot.astype(jnp.float32))
    coef = jnp.where(live, grad_logit / lens_col, 0.0)
    mine = stats_ref[place_ref[2] * 2 + place_ref[3], 0]
    hold[...] = coef * jnp.exp2((mine - soft) * SHARP_LOG2)

    eye = lax.broadcasted_iota(jnp.int32, (PADDED, 128), 0) == lax.broadcasted_iota(
        jnp.int32, (PADDED, 128), 1
    )
    core = place_ref[1]
    for m in range(CAPTIONS // 2):
        if 2 * m % group == 0:
            loads[2 * m // group].wait()
        for j, ref in ((2 * m + 1 - core, send_ref), (2 * m + core, keep_ref)):
            col = jnp.sum(jnp.where(eye, hold[pl.ds(j, 1), :], 0.0), axis=-1, keepdims=True)
            ref[m] = (grad[j].astype(jnp.float32) * col).astype(jnp.bfloat16)


def coef_part(place, pos, stats, lens, grad):
    half = jax.ShapeDtypeStruct((CAPTIONS // 2, PADDED, EMB), jnp.bfloat16)
    return pl.pallas_call(
        coef_kernel,
        in_specs=[SMEM, SMEM, VMEM, VMEM, FAR_OFF],
        out_specs=[VMEM] * 3,
        out_shape=[half, half, jax.ShapeDtypeStruct((1, 1), jnp.float32)],
        scratch_shapes=[
            pltpu.VMEM((CAPTIONS, 128), jnp.float32),
            pltpu.VMEM((CAPTIONS, PADDED, EMB), jnp.bfloat16),
            pltpu.SemaphoreType.DMA((4,)),
        ],
        compiler_params=pltpu.CompilerParams(vmem_limit_bytes=12 * MIB),
        cost_estimate=pl.CostEstimate(
            flops=4_000_000, bytes_accessed=6_000_000, transcendentals=100_000
        ),
        name="coef_part",
    )(place, pos, stats, lens, held(grad))


def small_call(kernel, name, operands, out_shapes, specs=None):
    return pl.pallas_call(
        kernel,
        in_specs=specs or [VMEM] * len(operands),
        out_specs=[VMEM] * len(out_shapes),
        out_shape=[jax.ShapeDtypeStruct(s, d) for s, d in out_shapes],
        compiler_params=pltpu.CompilerParams(vmem_limit_bytes=16 * MIB),
        cost_estimate=pl.CostEstimate(flops=0, bytes_accessed=2_000_000, transcendentals=0),
        name=name,
    )(*operands)


def added(a, b):
    return (a.astype(jnp.float32) + b.astype(jnp.float32)).astype(jnp.bfloat16)


def first_sum_kernel(place_ref, keep_ref, got_ref, a_keep, a_send, b_keep, b_send):
    x = place_ref[2]
    plan = (
        (0, ((a_keep, 0, 0), (a_send, 0, 1), (a_send, 1, 2), (a_keep, 1, 3))),
        (8, ((b_keep, 0, 0), (b_keep, 1, 1), (b_send, 1, 2), (b_send, 0, 3))),
    )
    for start, parts in plan:
        for ref, at, flip in parts:
            cols = pl.ds(pl.multiple_of((x ^ flip) * 128, 128), 128)
            for m in range(8):
                ref[m, :, pl.ds(at * 128, 128)] = added(
                    keep_ref[start + m, :, cols], got_ref[start + m, :, cols]
                )


def second_sum_kernel(a_keep, a_got, b_keep, b_got, a_mine, a_send, b_mine, b_send):
    for keep, got, mine, send in ((a_keep, a_got, a_mine, a_send), (b_keep, b_got, b_mine, b_send)):
        mine[...] = added(keep[:, :, :128], got[:, :, :128])
        send[...] = added(keep[:, :, 128:], got[:, :, 128:])


def third_sum_kernel(a_mine, a_got, b_mine, b_got, out):
    out[pl.ds(0, 8)] = added(a_mine[...], a_got[...])
    out[pl.ds(8, 8)] = added(b_mine[...], b_got[...])


def owned_sum_kernel(parts, out):
    total = jnp.sum(parts[...].astype(jnp.float32), axis=0).astype(jnp.bfloat16)
    for k in range(8):
        out[k] = total


def last_sum_kernel(parts, out):
    for x in range(4):
        total = parts[2 * x].astype(jnp.float32) + parts[2 * x + 1].astype(jnp.float32)
        out[:, 0, pl.ds(x * 128, 128)] = total[:SLOTS]


def reduce_gradient(place, send, keep):
    bf16 = jnp.bfloat16
    one = [(s, s ^ 2) for s in range(8)]
    three = [(s, s ^ 6) for s in range(8)]
    got = lax.ppermute(send, "dp", [(i, i ^ 1) for i in range(32)])
    a_keep, a_send, b_keep, b_send = small_call(
        first_sum_kernel, "first_sum", (place, keep, got), [((8, PADDED, 256), bf16)] * 4,
        [SMEM, VMEM, VMEM],
    )
    a_got = lax.ppermute(a_send, "space", one)
    b_got = lax.ppermute(b_send, "space", three)
    a_mine, a_send, b_mine, b_send = small_call(
        second_sum_kernel, "second_sum", (a_keep, a_got, b_keep, b_got),
        [((8, PADDED, 128), bf16)] * 4,
    )
    a_got = lax.ppermute(a_send, "space", three)
    b_got = lax.ppermute(b_send, "space", one)
    (parts,) = small_call(
        third_sum_kernel, "third_sum", (a_mine, a_got, b_mine, b_got), [((16, PADDED, 128), bf16)]
    )
    parts = lax.all_to_all(
        parts, "dp", split_axis=0, concat_axis=0, tiled=True,
        axis_index_groups=[[2 * m + c for m in range(16)] for c in range(2)],
    )
    (parts,) = small_call(owned_sum_kernel, "owned_sum", (parts,), [((8, PADDED, 128), bf16)])
    parts = lax.all_to_all(parts, "space", split_axis=0, concat_axis=0, tiled=True)
    (total,) = small_call(last_sum_kernel, "last_sum", (parts,), [((SLOTS, 1, EMB), jnp.float32)])
    return total.reshape(1, SLOTS, EMB)


def on_device(clip_qkv, temporal_qk, proj_weight, caption_tokens, caption_lens, positive):
    dp = lax.axis_index("dp")
    space = lax.axis_index("space")
    x, y = space >> 1, space & 1
    place = jnp.stack([dp >> 4, dp & 1, x, y, (dp >> 1) & 7]).astype(jnp.int32)
    lens_row = jnp.broadcast_to(
        caption_lens.astype(jnp.bfloat16)[:, None, None], (1, PADDED - SLOTS, EMB)
    )
    caps = jnp.concatenate([caption_tokens, lens_row], axis=1)
    blocks = clip_qkv.reshape(8, 2, LOCAL, 3 * FEATURES)
    blocks = lax.all_to_all(blocks, "space", split_axis=0, concat_axis=0, tiled=True)
    time = time_weights(temporal_qk[0])
    caps = doubled(caps, 16)
    caps = doubled(caps, 8)
    caps = doubled(caps, 4)
    caps = doubled(caps, 2)
    other = flip(caps, 1)
    attended = spatial_attention(blocks)
    spatial = lax.all_to_all(held(attended), "space", split_axis=0, concat_axis=0, tiled=True)
    video, stats, grad, lens = token_part(
        place, spatial, time, proj_weight, caps, other
    )
    stats = lax.all_to_all(stats, "space", split_axis=0, concat_axis=0, tiled=True)
    send, keep, loss = coef_part(place, positive, stats, lens, grad)
    caption_grad = reduce_gradient(place, send, keep)
    return video[None], caption_grad, loss.reshape(1)


def solution(mesh):
    return jax.shard_map(
        on_device,
        mesh=mesh,
        in_specs=(
            P("dp", None, "space", None),
            P("dp", None, "space", None),
            P(),
            P("dp", None, None),
            P("dp"),
            P("dp"),
        ),
        out_specs=(P("dp", None, "space", None), P("dp", None, None), P("dp")),
        check_vma=False,
    )
```

```python
import functools
import math

import jax
import jax.numpy as jnp
from jax import lax
from jax.experimental import pallas as pl
from jax.experimental.pallas import tpu as pltpu
from jax.sharding import PartitionSpec as P

HEADS = 13
HD = 128
FEATURES = HEADS * HD
EMB = 512
FRAMES = 16
PATCHES = 256
LOCAL = 32
SLOTS = 77
PADDED = 80
CAPTIONS = 32
SHARPNESS = 4.0
LOGIT_SCALE = 10.0
LOG2E = math.log2(math.e)
SCORE_LOG2 = HD ** (-0.5) * LOG2E
SHARP_LOG2 = SHARPNESS * LOG2E
MIB = 1 << 20
GRANT = pltpu.CompilerParams(vmem_limit_bytes=24 * MIB)
VMEM = pl.BlockSpec(memory_space=pltpu.VMEM)
SMEM = pl.BlockSpec(memory_space=pltpu.SMEM)

FAR_OFF = pl.BlockSpec(memory_space=pltpu.HBM)
ANY = pl.BlockSpec(memory_space=pl.ANY)

def held(value):
    return pltpu.with_memory_space_constraint(value, pltpu.HBM)


def nt(a, b):
    return lax.dot_general(a, b, (((1,), (1,)), ((), ())), preferred_element_type=jnp.float32)


SPLIT = 7


HALF = LOCAL // 2


def spatial_kernel(half, qkv_ref, out_ref):
    part = pl.ds(half * HALF, HALF)
    for h in range(HEADS):
        q = qkv_ref[:, 0, part, pl.ds(h * HD, HD)].reshape(PATCHES // 2, HD)
        k = qkv_ref[:, 0, :, pl.ds(FEATURES + h * HD, HD)].reshape(PATCHES, HD)
        v = qkv_ref[:, 0, :, pl.ds(2 * FEATURES + h * HD, HD)].reshape(PATCHES, HD)
        s = nt(q, k)
        m = jnp.max(s, axis=-1, keepdims=True)
        e = jnp.exp2((s - m) * SCORE_LOG2)
        total = jnp.sum(e, axis=-1, keepdims=True)
        o = jnp.dot(e.astype(jnp.bfloat16), v, preferred_element_type=jnp.float32)
        o = (o * (1.0 / total)).astype(jnp.bfloat16)
        out_ref[:, 0, :, pl.ds(h * HD, HD)] = o.reshape(8, HALF, HD)


def spatial_attention(blocks, half):
    return pl.pallas_call(
        functools.partial(spatial_kernel, half),
        grid=(2,),
        in_specs=[pl.BlockSpec((8, 1, LOCAL, 3 * FEATURES), lambda f: (0, f, 0, 0))],
        out_specs=pl.BlockSpec((8, 1, HALF, FEATURES), lambda f: (0, f, 0, 0)),
        out_shape=pltpu.HBM((8, 2, HALF, FEATURES), jnp.bfloat16),
        compiler_params=GRANT,
        cost_estimate=pl.CostEstimate(
            flops=4 * HEADS * PATCHES * PATCHES * HD,
            bytes_accessed=2 * PATCHES * 4 * FEATURES * 2,
            transcendentals=HEADS * PATCHES * PATCHES,
        ),
        name="spatial_attention",
    )(blocks)


ROWS = FRAMES * 16


def time_kernel(tqk_ref, low_ref, high_ref, tqk, weights, load_sem, sems):
    load = pltpu.make_async_copy(tqk_ref, tqk, load_sem)
    load.start()
    load.wait()
    r = lax.broadcasted_iota(jnp.int32, (ROWS, ROWS), 0)
    c = lax.broadcasted_iota(jnp.int32, (ROWS, ROWS), 1)
    bias = jnp.where((r & 15) == (c & 15), 0.0, -1e30).astype(jnp.float32)
    stores = []
    for g, out_ref in enumerate((low_ref, high_ref)):
        for h in range(HEADS):
            part = pl.ds(g * 16, 16)
            q = tqk[:, part, pl.ds(h * HD, HD)].reshape(ROWS, HD)
            k = tqk[:, part, pl.ds(FEATURES + h * HD, HD)].reshape(ROWS, HD)
            s = nt(q, k) + bias
            m = jnp.max(s, axis=-1, keepdims=True)
            e = jnp.exp2((s - m) * SCORE_LOG2)
            total = jnp.sum(e, axis=-1, keepdims=True)
            weights[g, h] = (e * (1.0 / total)).astype(jnp.bfloat16)
        stores.append(pltpu.make_async_copy(weights.at[g], out_ref, sems.at[g]))
        stores[-1].start()
    for store in stores:
        store.wait()


def time_weights(temporal_qk):
    return pl.pallas_call(
        time_kernel,
        in_specs=[FAR_OFF],
        out_specs=[FAR_OFF] * 2,
        out_shape=[pltpu.HBM((HEADS, ROWS, ROWS), jnp.bfloat16)] * 2,
        scratch_shapes=[
            pltpu.VMEM((FRAMES, LOCAL, 2 * FEATURES), jnp.bfloat16),
            pltpu.VMEM((2, HEADS, ROWS, ROWS), jnp.bfloat16),
            pltpu.SemaphoreType.DMA,
            pltpu.SemaphoreType.DMA((2,)),
        ],
        compiler_params=GRANT,
        cost_estimate=pl.CostEstimate(
            flops=4 * HEADS * ROWS * ROWS * HD,
            bytes_accessed=7_000_000,
            transcendentals=2 * HEADS * ROWS * ROWS,
        ),
        name="time_weights",
    )(held(temporal_qk))


def flip(value, bit):
    return lax.ppermute(value, "dp", [(i, i ^ bit) for i in range(32)])


def join_kernel(*refs):
    refs[-1][0] = refs[0][...]
    refs[-1][1] = refs[1][...]


def flip_y(value):
    pairs = [(i * 8 + s, (i ^ 16) * 8 + (s ^ 1)) for i in range(32) for s in range(8)]
    return lax.ppermute(value, ("dp", "space"), pairs)


def doubled(value, other):
    both = pl.pallas_call(
        join_kernel,
        in_specs=[VMEM] * 2,
        out_specs=VMEM,
        out_shape=jax.ShapeDtypeStruct((2,) + value.shape, value.dtype),
        compiler_params=pltpu.CompilerParams(vmem_limit_bytes=8 * MIB),
        cost_estimate=pl.CostEstimate(flops=0, bytes_accessed=1_000_000, transcendentals=0),
        name="join",
    )(value, other)
    return both.reshape((-1,) + value.shape[1:])


GROUP = 8


def token_kernel(
    half, place_ref, value, time_ref, proj_ref, mine_ref, other_ref, *refs
):
    if half == 0:
        emb_ref, stats_ref, grad_ref, proj, caps, comb, video, grads, sems, grad_sems = refs
    else:
        (
            _, old_stats, old_ref, emb_ref, all_stats_ref, grad_ref, lens_ref,
            proj, caps, comb, video, grads, sems, grad_sems, olds, old_sems, stats_ref,
        ) = refs
        old_loads = [
            pltpu.make_async_copy(
                old_ref.at[pl.ds(i * GROUP, GROUP)], olds.at[pl.ds(i * GROUP, GROUP)], old_sems.at[i]
            )
            for i in range(CAPTIONS // GROUP)
        ]
    proj_load = pltpu.make_async_copy(proj_ref, proj, sems.at[0])
    cap_loads = [
        pltpu.make_async_copy(ref, caps.at[i], sems.at[1 + i])
        for i, ref in enumerate((mine_ref, other_ref))
    ]
    for load in (proj_load, *cap_loads):
        load.start()
    if half == 1:
        for load in old_loads:
            load.start()
    for h in range(HEADS):
        cols = pl.ds(h * HD, HD)
        v = value[:, :, :, cols].reshape(ROWS, HD)
        o = jnp.dot(time_ref[h], v, preferred_element_type=jnp.float32)
        comb[:, cols] = (v.astype(jnp.float32) + o).astype(jnp.bfloat16)
    proj_load.wait()
    projected = jnp.dot(comb[...], proj[...], preferred_element_type=jnp.float32)
    scale = lax.rsqrt(jnp.mean(projected * projected, axis=-1, keepdims=True) + 1e-06)
    emb = (projected * scale).astype(jnp.bfloat16)
    video[...] = emb.reshape(FRAMES, HALF, EMB)
    emb_store = pltpu.make_async_copy(
        video, emb_ref.at[:, pl.ds(half * HALF, HALF)], sems.at[3]
    )
    emb_store.start()

    eye = lax.broadcasted_iota(jnp.int32, (PADDED, 128), 0) == lax.broadcasted_iota(
        jnp.int32, (PADDED, 128), 1
    )

    def as_row(col):
        return jnp.sum(jnp.where(eye, col, 0.0), axis=0, keepdims=True)

    def as_col(row):
        return jnp.sum(jnp.where(eye, row, 0.0), axis=-1, keepdims=True)

    y_hi, core, z = place_ref[0], place_ref[1], place_ref[4]
    stores = []
    for i in range(2):
        cap_loads[i].wait()
        for m0 in range(0, CAPTIONS // 2, GROUP):
            slot = i * CAPTIONS // 2 + m0
            block = pl.ds(slot, GROUP)
            sim = nt(caps[i, pl.ds(m0, GROUP)].reshape(GROUP * PADDED, EMB), emb)
            top = jnp.max(sim, axis=-1, keepdims=True)
            if half == 1:
                old_top, old_total = (
                    jnp.concatenate(
                        [as_col(old_stats[k, slot + j : slot + j + 1, :]) for j in range(GROUP)], axis=0
                    )
                    for k in range(2)
                )
                top = jnp.maximum(top, old_top)
                factor = jnp.exp2((old_top - top) * SHARP_LOG2)
            w = jnp.exp2((sim - top) * SHARP_LOG2)
            total = jnp.sum(w, axis=-1, keepdims=True)
            product = jnp.dot(w.astype(jnp.bfloat16), emb, preferred_element_type=jnp.float32)
            if half == 1:
                total = total + old_total * factor
                old_loads[slot // GROUP].wait()
                old = olds[block].reshape(GROUP * PADDED, EMB).astype(jnp.float32)
                product = product + old * factor
            grads[block] = product.astype(jnp.bfloat16).reshape(GROUP, PADDED, EMB)
            if half == 0:
                stores.append(
                    pltpu.make_async_copy(
                        grads.at[block], grad_ref.at[block], grad_sems.at[slot // GROUP]
                    )
                )
                stores[-1].start()
            for j in range(GROUP):
                m = m0 + j
                rng = slice(j * PADDED, (j + 1) * PADDED)
                if half == 0:
                    at = slot + j
                else:
                    flips = (m >> 3 & 1) + (m >> 2 & 1) * 2 + (m >> 1 & 1) * 4
                    side = core if i == 0 else 1 - core
                    at = (y_hi ^ (m & 1)) * 16 + (z ^ flips) * 2 + side
                    stores.append(
                        pltpu.make_async_copy(
                            grads.at[slot + j], grad_ref.at[at], grad_sems.at[slot + j]
                        )
                    )
                    stores[-1].start()
                    lens_ref[pl.ds(at, 1), :] = caps[i, m, SLOTS : SLOTS + 1, :128].astype(
                        jnp.float32
                    )
                stats_ref[0, pl.ds(at, 1), :] = as_row(top[rng])
                stats_ref[1, pl.ds(at, 1), :] = as_row(total[rng])
    if half == 1:
        for k in range(8):
            all_stats_ref[k] = stats_ref[...]
    emb_store.wait()
    for store in stores:
        store.wait()


def token_part(half, place, value, time, proj_weight, mine, other, before=()):
    bf16, f32 = jnp.bfloat16, jnp.float32
    emb = pltpu.HBM((FRAMES, LOCAL, EMB), bf16)
    grad = pltpu.HBM((CAPTIONS, PADDED, EMB), bf16)
    one = jax.ShapeDtypeStruct((2, CAPTIONS, 128), f32)
    scratch = [
        pltpu.VMEM((FEATURES, EMB), bf16),
        pltpu.VMEM((2, CAPTIONS // 2, PADDED, EMB), bf16),
        pltpu.VMEM((ROWS, FEATURES), bf16),
        pltpu.VMEM((FRAMES, HALF, EMB), bf16),
        pltpu.VMEM((CAPTIONS, PADDED, EMB), bf16),
        pltpu.SemaphoreType.DMA((4,)),
        pltpu.SemaphoreType.DMA((CAPTIONS,)),
    ]
    if half == 0:
        out_shape, out_specs, more_specs, aliases = [emb, one, grad], [FAR_OFF, VMEM, FAR_OFF], [], {}
    else:
        out_shape = [
            emb,
            jax.ShapeDtypeStruct((8, 2, CAPTIONS, 128), f32),
            grad,
            jax.ShapeDtypeStruct((CAPTIONS, 128), f32),
        ]
        out_specs = [FAR_OFF, VMEM, FAR_OFF, VMEM]
        more_specs, aliases = [FAR_OFF, VMEM, FAR_OFF], {6: 0}
        scratch += [
            pltpu.VMEM((CAPTIONS, PADDED, EMB), bf16),
            pltpu.SemaphoreType.DMA((CAPTIONS // GROUP,)),
            pltpu.VMEM((2, CAPTIONS, 128), f32),
        ]
    return pl.pallas_call(
        functools.partial(token_kernel, half),
        in_specs=[SMEM, VMEM, VMEM, FAR_OFF, FAR_OFF, FAR_OFF] + more_specs,
        out_specs=out_specs,
        out_shape=out_shape,
        scratch_shapes=scratch,
        input_output_aliases=aliases,
        compiler_params=pltpu.CompilerParams(vmem_limit_bytes=28 * MIB),
        cost_estimate=pl.CostEstimate(
            flops=2_250_000_000, bytes_accessed=10_000_000, transcendentals=700_000
        ),
        name="token_part",
    )(place, value, time, held(proj_weight), held(mine), held(other), *before)


def coef_kernel(
    place_ref, pos_ref, stats_ref, lens_ref, grad_ref, send_ref, keep_ref, loss_ref, hold, grad, sems
):
    group = 8
    loads = [
        pltpu.make_async_copy(
            grad_ref.at[pl.ds(group * i, group)], grad.at[pl.ds(group * i, group)], sems.at[i]
        )
        for i in range(CAPTIONS // group)
    ]
    for load in loads:
        load.start()
    tops = stats_ref[:, 0]
    totals = stats_ref[:, 1]
    top = jnp.max(tops, axis=0)
    total = jnp.sum(totals * jnp.exp2((tops - top[None]) * SHARP_LOG2), axis=0)
    soft = top + jnp.log(total) / SHARPNESS
    slot = lax.broadcasted_iota(jnp.int32, (CAPTIONS, 128), 1).astype(jnp.float32)
    lens = lens_ref[...]
    live = slot < lens
    lens_col = lens[:, :1]
    score = jnp.sum(jnp.where(live, soft, 0.0), axis=-1, keepdims=True) / lens_col
    logits = LOGIT_SCALE * score
    peak = jnp.max(logits, axis=0, keepdims=True)
    log_total = peak + jnp.log(jnp.sum(jnp.exp(logits - peak), axis=0, keepdims=True))
    onehot = lax.broadcasted_iota(jnp.int32, (CAPTIONS, 1), 0) == pos_ref[0]
    loss_ref[...] = log_total - jnp.sum(jnp.where(onehot, logits, 0.0), axis=0, keepdims=True)
    grad_logit = LOGIT_SCALE * (jnp.exp(logits - log_total) - onehot.astype(jnp.float32))
    coef = jnp.where(live, grad_logit / lens_col, 0.0)
    mine = stats_ref[place_ref[2] * 2 + place_ref[3], 0]
    hold[...] = coef * jnp.exp2((mine - soft) * SHARP_LOG2)

    eye = lax.broadcasted_iota(jnp.int32, (PADDED, 128), 0) == lax.broadcasted_iota(
        jnp.int32, (PADDED, 128), 1
    )
    core = place_ref[1]
    for m in range(CAPTIONS // 2):
        if 2 * m % group == 0:
            loads[2 * m // group].wait()
        for j, ref in ((2 * m + 1 - core, send_ref), (2 * m + core, keep_ref)):
            col = jnp.sum(jnp.where(eye, hold[pl.ds(j, 1), :], 0.0), axis=-1, keepdims=True)
            ref[m] = (grad[j].astype(jnp.float32) * col).astype(jnp.bfloat16)


def coef_part(place, pos, stats, lens, grad):
    half = jax.ShapeDtypeStruct((CAPTIONS // 2, PADDED, EMB), jnp.bfloat16)
    return pl.pallas_call(
        coef_kernel,
        in_specs=[SMEM, SMEM, VMEM, VMEM, FAR_OFF],
        out_specs=[VMEM] * 3,
        out_shape=[half, half, jax.ShapeDtypeStruct((1, 1), jnp.float32)],
        scratch_shapes=[
            pltpu.VMEM((CAPTIONS, 128), jnp.float32),
            pltpu.VMEM((CAPTIONS, PADDED, EMB), jnp.bfloat16),
            pltpu.SemaphoreType.DMA((4,)),
        ],
        compiler_params=pltpu.CompilerParams(vmem_limit_bytes=12 * MIB),
        cost_estimate=pl.CostEstimate(
            flops=4_000_000, bytes_accessed=6_000_000, transcendentals=100_000
        ),
        name="coef_part",
    )(place, pos, stats, lens, held(grad))


def small_call(kernel, name, operands, out_shapes, specs=None):
    return pl.pallas_call(
        kernel,
        in_specs=specs or [VMEM] * len(operands),
        out_specs=[VMEM] * len(out_shapes),
        out_shape=[jax.ShapeDtypeStruct(s, d) for s, d in out_shapes],
        compiler_params=pltpu.CompilerParams(vmem_limit_bytes=16 * MIB),
        cost_estimate=pl.CostEstimate(flops=0, bytes_accessed=2_000_000, transcendentals=0),
        name=name,
    )(*operands)


def added(a, b):
    return (a.astype(jnp.float32) + b.astype(jnp.float32)).astype(jnp.bfloat16)


def first_sum_kernel(place_ref, keep_ref, got_ref, a_keep, a_send, b_keep, b_send):
    x = place_ref[2]
    plan = (
        (0, ((a_keep, 0, 0), (a_send, 0, 1), (a_send, 1, 2), (a_keep, 1, 3))),
        (8, ((b_keep, 0, 0), (b_keep, 1, 1), (b_send, 1, 2), (b_send, 0, 3))),
    )
    for start, parts in plan:
        for ref, at, flip in parts:
            cols = pl.ds(pl.multiple_of((x ^ flip) * 128, 128), 128)
            for m in range(8):
                ref[m, :, pl.ds(at * 128, 128)] = added(
                    keep_ref[start + m, :, cols], got_ref[start + m, :, cols]
                )


def second_sum_kernel(a_keep, a_got, b_keep, b_got, a_mine, a_send, b_mine, b_send):
    for keep, got, mine, send in ((a_keep, a_got, a_mine, a_send), (b_keep, b_got, b_mine, b_send)):
        mine[...] = added(keep[:, :, :128], got[:, :, :128])
        send[...] = added(keep[:, :, 128:], got[:, :, 128:])


def third_sum_kernel(a_mine, a_got, b_mine, b_got, out):
    out[pl.ds(0, 8)] = added(a_mine[...], a_got[...])
    out[pl.ds(8, 8)] = added(b_mine[...], b_got[...])


def owned_sum_kernel(parts, out):
    total = jnp.sum(parts[...].astype(jnp.float32), axis=0).astype(jnp.bfloat16)
    for k in range(8):
        out[k] = total


def last_sum_kernel(parts, out):
    for x in range(4):
        total = parts[2 * x].astype(jnp.float32) + parts[2 * x + 1].astype(jnp.float32)
        out[:, 0, pl.ds(x * 128, 128)] = total[:SLOTS]


def reduce_gradient(place, send, keep):
    bf16 = jnp.bfloat16
    one = [(s, s ^ 2) for s in range(8)]
    three = [(s, s ^ 6) for s in range(8)]
    got = lax.ppermute(send, "dp", [(i, i ^ 1) for i in range(32)])
    a_keep, a_send, b_keep, b_send = small_call(
        first_sum_kernel, "first_sum", (place, keep, got), [((8, PADDED, 256), bf16)] * 4,
        [SMEM, VMEM, VMEM],
    )
    a_got = lax.ppermute(a_send, "space", one)
    b_got = lax.ppermute(b_send, "space", three)
    a_mine, a_send, b_mine, b_send = small_call(
        second_sum_kernel, "second_sum", (a_keep, a_got, b_keep, b_got),
        [((8, PADDED, 128), bf16)] * 4,
    )
    a_got = lax.ppermute(a_send, "space", three)
    b_got = lax.ppermute(b_send, "space", one)
    (parts,) = small_call(
        third_sum_kernel, "third_sum", (a_mine, a_got, b_mine, b_got), [((16, PADDED, 128), bf16)]
    )
    parts = lax.all_to_all(
        parts, "dp", split_axis=0, concat_axis=0, tiled=True,
        axis_index_groups=[[2 * m + c for m in range(16)] for c in range(2)],
    )
    (parts,) = small_call(owned_sum_kernel, "owned_sum", (parts,), [((8, PADDED, 128), bf16)])
    parts = lax.all_to_all(parts, "space", split_axis=0, concat_axis=0, tiled=True)
    (total,) = small_call(last_sum_kernel, "last_sum", (parts,), [((SLOTS, 1, EMB), jnp.float32)])
    return total.reshape(1, SLOTS, EMB)


def on_device(clip_qkv, temporal_qk, proj_weight, caption_tokens, caption_lens, positive):
    dp = lax.axis_index("dp")
    space = lax.axis_index("space")
    x, y = space >> 1, space & 1
    place = jnp.stack([dp >> 4, dp & 1, x, y, (dp >> 1) & 7]).astype(jnp.int32)
    lens_row = jnp.broadcast_to(
        caption_lens.astype(jnp.bfloat16)[:, None, None], (1, PADDED - SLOTS, EMB)
    )
    caps = jnp.concatenate([caption_tokens, lens_row], axis=1)
    blocks = clip_qkv.reshape(8, 2, LOCAL, 3 * FEATURES)
    blocks = lax.all_to_all(blocks, "space", split_axis=0, concat_axis=0, tiled=True)
    time = time_weights(temporal_qk[0])
    caps = doubled(caps, flip_y(caps))
    for bit in (8, 4, 2):
        caps = doubled(caps, flip(caps, bit))
    other = flip(caps, 1)
    values = [
        lax.all_to_all(
            held(spatial_attention(blocks, half)), "space", split_axis=0, concat_axis=0, tiled=True
        )
        for half in range(2)
    ]
    before = token_part(0, place, values[0], time[0], proj_weight, caps, other)
    video, stats, grad, lens = token_part(
        1, place, values[1], time[1], proj_weight, caps, other, before
    )
    stats = lax.all_to_all(stats, "space", split_axis=0, concat_axis=0, tiled=True)
    send, keep, loss = coef_part(place, positive, stats, lens, grad)
    caption_grad = reduce_gradient(place, send, keep)
    return video[None], caption_grad, loss.reshape(1)


def solution(mesh):
    return jax.shard_map(
        on_device,
        mesh=mesh,
        in_specs=(
            P("dp", None, "space", None),
            P("dp", None, "space", None),
            P(),
            P("dp", None, None),
            P("dp"),
            P("dp"),
        ),
        out_specs=(P("dp", None, "space", None), P("dp", None, None), P("dp")),
        check_vma=False,
    )
```

```python
import math

import jax
import jax.numpy as jnp
from jax import lax
from jax.experimental import pallas as pl
from jax.experimental.pallas import tpu as pltpu
from jax.sharding import PartitionSpec as P

HEADS = 13
HD = 128
FEATURES = HEADS * HD
EMB = 512
FRAMES = 16
PATCHES = 256
LOCAL = 32
SLOTS = 77
PADDED = 80
CAPTIONS = 32
SHARPNESS = 4.0
LOGIT_SCALE = 10.0
LOG2E = math.log2(math.e)
SCORE_LOG2 = HD ** (-0.5) * LOG2E
SHARP_LOG2 = SHARPNESS * LOG2E
MIB = 1 << 20
GRANT = pltpu.CompilerParams(vmem_limit_bytes=24 * MIB)
VMEM = pl.BlockSpec(memory_space=pltpu.VMEM)
SMEM = pl.BlockSpec(memory_space=pltpu.SMEM)

FAR_OFF = pl.BlockSpec(memory_space=pltpu.HBM)
ANY = pl.BlockSpec(memory_space=pl.ANY)


def owner(g1, a):
    return (g1 * 2 + ((a >> 1) ^ g1)) * 2 + (a & 1)


def quad_place(place_ref):
    x, y = place_ref[2], place_ref[3]
    return x >> 1, ((x >> 1) ^ (x & 1)) * 2 + y


def held(value):
    return pltpu.with_memory_space_constraint(value, pltpu.HBM)


def nt(a, b):
    return lax.dot_general(a, b, (((1,), (1,)), ((), ())), preferred_element_type=jnp.float32)


SPLIT = 7


ROW = (LOCAL, 3 * FEATURES)
FULL = pltpu.CompilerParams(vmem_limit_bytes=60 * MIB)


def copied(pairs, buf, sems):
    loads = [
        pltpu.make_async_copy(src, buf.at[i], sems.at[0, i]) for i, (src, _) in enumerate(pairs)
    ]
    stores = [
        pltpu.make_async_copy(buf.at[i], dst, sems.at[1, i]) for i, (_, dst) in enumerate(pairs)
    ]
    for load in loads:
        load.start()
    for load, store in zip(loads, stores):
        load.wait()
        store.start()
    for store in stores:
        store.wait()


def copying(kernel, name, operands, shapes, count, params=FULL):
    return pl.pallas_call(
        kernel,
        in_specs=[SMEM] + [ANY] * (len(operands) - 1),
        out_specs=[ANY] * len(shapes),
        out_shape=[jax.ShapeDtypeStruct((n,) + ROW, jnp.bfloat16) for n in shapes],
        scratch_shapes=[
            pltpu.VMEM((count,) + ROW, jnp.bfloat16),
            pltpu.SemaphoreType.DMA((2, count)),
        ],
        compiler_params=params,
        cost_estimate=pl.CostEstimate(flops=0, bytes_accessed=6_000_000, transcendentals=0),
        name=name,
    )(*operands)


def across_kernel(place_ref, clip_ref, out_ref, buf, sems):
    g1, _ = quad_place(place_ref)
    copied([(clip_ref.at[2 * owner(1 - g1, a) + 1], out_ref.at[a]) for a in range(4)], buf, sems)


def quads_kernel(place_ref, clip_ref, one, two, three, buf, sems):
    _, a = quad_place(place_ref)
    pairs = [
        (clip_ref.at[2 * owner(g, a ^ k)], ref.at[g])
        for k, ref in ((1, one), (2, two), (3, three))
        for g in range(2)
    ]
    copied(pairs, buf, sems)


def own_kernel(place_ref, clip_ref, first, seconds, kept, buf, sems):
    g1, a = quad_place(place_ref)
    pairs = [(clip_ref.at[2 * owner(1 - g1, a)], first.at[0])]
    pairs += [(clip_ref.at[2 * owner(g1, a ^ k) + 1], seconds.at[k - 1]) for k in (1, 2, 3)]
    pairs += [(clip_ref.at[2 * owner(g1, a) + f], kept.at[f]) for f in range(2)]
    copied(pairs, buf, sems)


def turn_kernel(place_ref, first_ref, one, two, three, behind_ref, out_ref, buf, sems):
    g1, _ = quad_place(place_ref)
    pairs = [(first_ref.at[0], out_ref.at[0])]
    pairs += [(ref.at[1 - g1], out_ref.at[k]) for k, ref in ((1, one), (2, two), (3, three))]
    copied(pairs, buf, sems)


def spread_kernel(place_ref, seconds_ref, across_ref, one, two, three, buf, sems):
    _, a = quad_place(place_ref)
    pairs = []
    for k, ref in ((1, one), (2, two), (3, three)):
        pairs += [(seconds_ref.at[k - 1], ref.at[0]), (across_ref.at[a ^ k], ref.at[1])]
    copied(pairs, buf, sems)


def swap(value, bits):
    return lax.ppermute(value, "space", [(s, s ^ bits) for s in range(8)])


def bring_frames(clip, place, behind):
    (across,) = copying(across_kernel, "across", (place, clip), (4,), 4)
    across = swap(across, 6)
    quads = copying(quads_kernel, "quads", (place, clip), (2, 2, 2), 6)
    quads = [swap(quad, k) for k, quad in zip((1, 2, 3), quads)]
    first, seconds, kept = copying(own_kernel, "own", (place, clip), (1, 3, 2), 6)
    few = pltpu.CompilerParams(vmem_limit_bytes=8 * MIB)
    (turned,) = copying(turn_kernel, "turn", (place, first, *quads, behind), (4,), 4, few)
    turned = swap(turned, 6)
    pairs = copying(spread_kernel, "spread", (place, seconds, across), (2, 2, 2), 6, few)
    started = pairs[0]
    pairs = [swap(pair, k) for k, pair in zip((1, 2, 3), pairs)]
    return (kept, across, turned, *quads, *pairs), started


def spatial_kernel(place_ref, kept_ref, across_ref, turned_ref, *refs):
    quads, pairs, (_, out_ref, buf, res, sems, store_sems) = refs[:3], refs[3:6], refs[6:]
    g1, a = quad_place(place_ref)
    first = [kept_ref.at[0]] + [ref.at[g1] for ref in quads] + [turned_ref.at[k] for k in range(4)]
    second = [kept_ref.at[1]] + [ref.at[0] for ref in pairs]
    second += [across_ref.at[a]] + [ref.at[1] for ref in pairs]
    loads = [
        [pltpu.make_async_copy(src, buf.at[f, i], sems.at[f, i]) for i, src in enumerate(sources)]
        for f, sources in enumerate((first, second))
    ]
    for f in range(2):
        for load in loads[f]:
            load.start()
    stores = [
        pltpu.make_async_copy(res.at[f], out_ref.at[:, f], store_sems.at[f]) for f in range(2)
    ]
    for f in range(2):
        for load in loads[f]:
            load.wait()
        for h in range(HEADS):
            q = buf[f, :, :, pl.ds(h * HD, HD)].reshape(PATCHES, HD)
            k = buf[f, :, :, pl.ds(FEATURES + h * HD, HD)].reshape(PATCHES, HD)
            v = buf[f, :, :, pl.ds(2 * FEATURES + h * HD, HD)].reshape(PATCHES, HD)
            s = nt(q, k)
            m = jnp.max(s, axis=-1, keepdims=True)
            e = jnp.exp2((s - m) * SCORE_LOG2)
            total = jnp.sum(e, axis=-1, keepdims=True)
            o = jnp.dot(e.astype(jnp.bfloat16), v, preferred_element_type=jnp.float32)
            o = (o * (1.0 / total)).astype(jnp.bfloat16)
            for i in range(8):
                at = owner(g1 if i < 4 else 1 - g1, a ^ (i & 3))
                res[f, at, :, pl.ds(h * HD, HD)] = o[i * LOCAL : (i + 1) * LOCAL]
        stores[f].start()
    for store in stores:
        store.wait()


def spatial_attention(place, pieces, behind):
    return pl.pallas_call(
        spatial_kernel,
        in_specs=[SMEM] + [ANY] * (len(pieces) + 1),
        out_specs=ANY,
        out_shape=jax.ShapeDtypeStruct((8, 2, LOCAL, FEATURES), jnp.bfloat16),
        scratch_shapes=[
            pltpu.VMEM((2, 8) + ROW, jnp.bfloat16),
            pltpu.VMEM((2, 8, LOCAL, FEATURES), jnp.bfloat16),
            pltpu.SemaphoreType.DMA((2, 8)),
            pltpu.SemaphoreType.DMA((2,)),
        ],
        compiler_params=GRANT,
        cost_estimate=pl.CostEstimate(
            flops=8 * HEADS * PATCHES * PATCHES * HD,
            bytes_accessed=2 * PATCHES * 4 * FEATURES * 2,
            transcendentals=2 * HEADS * PATCHES * PATCHES,
        ),
        name="spatial_attention",
    )(place, *pieces, behind)


ROWS = FRAMES * 16


def time_kernel(tqk_ref, behind_ref, out_ref, mark_ref, tqk, weights, load_sem, sems):
    load = pltpu.make_async_copy(tqk_ref, tqk, load_sem)
    load.start()
    load.wait()
    mark_ref[...] = jnp.zeros_like(mark_ref)
    r = lax.broadcasted_iota(jnp.int32, (ROWS, ROWS), 0)
    c = lax.broadcasted_iota(jnp.int32, (ROWS, ROWS), 1)
    bias = jnp.where((r & 15) == (c & 15), 0.0, -1e30).astype(jnp.float32)
    stores = []
    for h in range(HEADS):
        for g in range(LOCAL // 16):
            part = pl.ds(g * 16, 16)
            q = tqk[:, part, pl.ds(h * HD, HD)].reshape(ROWS, HD)
            k = tqk[:, part, pl.ds(FEATURES + h * HD, HD)].reshape(ROWS, HD)
            s = nt(q, k) + bias
            m = jnp.max(s, axis=-1, keepdims=True)
            e = jnp.exp2((s - m) * SCORE_LOG2)
            total = jnp.sum(e, axis=-1, keepdims=True)
            weights[h, g] = (e * (1.0 / total)).astype(jnp.bfloat16)
        stores.append(pltpu.make_async_copy(weights.at[h], out_ref.at[h], sems.at[h]))
        stores[-1].start()
    for store in stores:
        store.wait()


def time_weights(temporal_qk, behind):
    return pl.pallas_call(
        time_kernel,
        in_specs=[ANY] * 2,
        out_specs=[ANY, VMEM],
        out_shape=[
            jax.ShapeDtypeStruct((HEADS, 2, ROWS, ROWS), jnp.bfloat16),
            jax.ShapeDtypeStruct((8, 128), jnp.float32),
        ],
        scratch_shapes=[
            pltpu.VMEM((FRAMES, LOCAL, 2 * FEATURES), jnp.bfloat16),
            pltpu.VMEM((HEADS, 2, ROWS, ROWS), jnp.bfloat16),
            pltpu.SemaphoreType.DMA,
            pltpu.SemaphoreType.DMA((HEADS,)),
        ],
        compiler_params=GRANT,
        cost_estimate=pl.CostEstimate(
            flops=4 * HEADS * ROWS * ROWS * HD,
            bytes_accessed=7_000_000,
            transcendentals=2 * HEADS * ROWS * ROWS,
        ),
        name="time_weights",
    )(temporal_qk, behind)


def flip(value, bit):
    return lax.ppermute(value, "dp", [(i, i ^ bit) for i in range(32)])


def join_kernel(*refs):
    refs[-1][0] = refs[0][...]
    refs[-1][1] = refs[1][...]


def flip_y(value):
    pairs = [(i * 8 + s, (i ^ 16) * 8 + (s ^ 1)) for i in range(32) for s in range(8)]
    return lax.ppermute(value, ("dp", "space"), pairs)


def doubled(value, other, *behind):
    both = pl.pallas_call(
        join_kernel,
        in_specs=[VMEM] * 2 + [ANY] * len(behind),
        out_specs=VMEM,
        out_shape=jax.ShapeDtypeStruct((2,) + value.shape, value.dtype),
        compiler_params=pltpu.CompilerParams(vmem_limit_bytes=8 * MIB),
        cost_estimate=pl.CostEstimate(flops=0, bytes_accessed=1_000_000, transcendentals=0),
        name="join",
    )(value, other, *behind)
    return both.reshape((-1,) + value.shape[1:])


def token_kernel(
    place_ref, value, time_ref, proj_ref, mine_ref, other_ref,
    emb_ref, all_stats_ref, grad_ref, lens_ref,
    proj, mine, comb, video, grads, stats_ref, sems, grad_sems,
):
    proj_load = pltpu.make_async_copy(proj_ref, proj, sems.at[0])
    mine_load = pltpu.make_async_copy(mine_ref, mine, sems.at[1])
    proj_load.start()
    mine_load.start()
    for h in range(HEADS):
        cols = pl.ds(h * HD, HD)
        for g in range(LOCAL // 16):
            part = pl.ds(g * 16, 16)
            v = value[:, :, part, cols].reshape(ROWS, HD)
            o = jnp.dot(time_ref[h, g], v, preferred_element_type=jnp.float32)
            o = (v.astype(jnp.float32) + o).astype(jnp.bfloat16)
            comb[:, part, cols] = o.reshape(FRAMES, 16, HD)
    tokens = FRAMES * LOCAL
    proj_load.wait()
    projected = jnp.dot(
        comb[...].reshape(tokens, FEATURES), proj[...], preferred_element_type=jnp.float32
    )
    scale = lax.rsqrt(jnp.mean(projected * projected, axis=-1, keepdims=True) + 1e-06)
    emb = (projected * scale).astype(jnp.bfloat16)
    video[...] = emb.reshape(FRAMES, LOCAL, EMB)
    emb_store = pltpu.make_async_copy(video, emb_ref, sems.at[2])
    emb_store.start()
    mine_load.wait()

    eye = lax.broadcasted_iota(jnp.int32, (PADDED, 128), 0) == lax.broadcasted_iota(
        jnp.int32, (PADDED, 128), 1
    )
    y_hi, core, z = place_ref[0], place_ref[1], place_ref[4]
    group = 8
    stores = []
    for i, (ref, c) in enumerate(((mine, core), (other_ref, 1 - core))):
        for m0 in range(0, CAPTIONS // 2, group):
            sim = nt(ref[pl.ds(m0, group)].reshape(group * PADDED, EMB), emb)
            top = jnp.max(sim, axis=-1, keepdims=True)
            w = jnp.exp2((sim - top) * SHARP_LOG2)
            total = jnp.sum(w, axis=-1, keepdims=True)
            product = jnp.dot(w.astype(jnp.bfloat16), emb, preferred_element_type=jnp.float32)
            slot = i * CAPTIONS // 2 + m0
            grads[pl.ds(slot, group)] = product.astype(jnp.bfloat16).reshape(group, PADDED, EMB)
            for j in range(group):
                m = m0 + j
                flips = (m >> 3 & 1) + (m >> 2 & 1) * 2 + (m >> 1 & 1) * 4
                at = (y_hi ^ (m & 1)) * 16 + (z ^ flips) * 2 + c
                stores.append(
                    pltpu.make_async_copy(
                        grads.at[slot + j], grad_ref.at[at], grad_sems.at[slot + j]
                    )
                )
                stores[-1].start()
                rng = slice(j * PADDED, (j + 1) * PADDED)
                top_row = jnp.sum(jnp.where(eye, top[rng], 0.0), axis=0, keepdims=True)
                total_row = jnp.sum(jnp.where(eye, total[rng], 0.0), axis=0, keepdims=True)
                stats_ref[0, pl.ds(at, 1), :] = top_row
                stats_ref[1, pl.ds(at, 1), :] = total_row
                lens_ref[pl.ds(at, 1), :] = ref[m, SLOTS : SLOTS + 1, :128].astype(jnp.float32)
    for k in range(8):
        all_stats_ref[k] = stats_ref[...]
    emb_store.wait()
    for store in stores:
        store.wait()


def token_part(place, spatial, time, proj_weight, mine, other):
    bf16 = jnp.bfloat16
    return pl.pallas_call(
        token_kernel,
        in_specs=[SMEM, VMEM, VMEM, FAR_OFF, FAR_OFF, VMEM],
        out_specs=[FAR_OFF, VMEM, FAR_OFF, VMEM],
        out_shape=[
            pltpu.HBM((FRAMES, LOCAL, EMB), bf16),
            jax.ShapeDtypeStruct((8, 2, CAPTIONS, 128), jnp.float32),
            pltpu.HBM((CAPTIONS, PADDED, EMB), bf16),
            jax.ShapeDtypeStruct((CAPTIONS, 128), jnp.float32),
        ],
        scratch_shapes=[
            pltpu.VMEM((FEATURES, EMB), bf16),
            pltpu.VMEM((CAPTIONS // 2, PADDED, EMB), bf16),
            pltpu.VMEM((FRAMES, LOCAL, FEATURES), bf16),
            pltpu.VMEM((FRAMES, LOCAL, EMB), bf16),
            pltpu.VMEM((CAPTIONS, PADDED, EMB), bf16),
            pltpu.VMEM((2, CAPTIONS, 128), jnp.float32),
            pltpu.SemaphoreType.DMA((3,)),
            pltpu.SemaphoreType.DMA((CAPTIONS,)),
        ],
        compiler_params=GRANT,
        cost_estimate=pl.CostEstimate(
            flops=4_500_000_000, bytes_accessed=12_000_000, transcendentals=1_300_000
        ),
        name="token_part",
    )(place, spatial, time, held(proj_weight), held(mine), other)


def coef_kernel(
    place_ref, pos_ref, stats_ref, lens_ref, grad_ref, send_ref, keep_ref, loss_ref, hold, grad, sems
):
    group = 8
    loads = [
        pltpu.make_async_copy(
            grad_ref.at[pl.ds(group * i, group)], grad.at[pl.ds(group * i, group)], sems.at[i]
        )
        for i in range(CAPTIONS // group)
    ]
    for load in loads:
        load.start()
    tops = stats_ref[:, 0]
    totals = stats_ref[:, 1]
    top = jnp.max(tops, axis=0)
    total = jnp.sum(totals * jnp.exp2((tops - top[None]) * SHARP_LOG2), axis=0)
    soft = top + jnp.log(total) / SHARPNESS
    slot = lax.broadcasted_iota(jnp.int32, (CAPTIONS, 128), 1).astype(jnp.float32)
    lens = lens_ref[...]
    live = slot < lens
    lens_col = lens[:, :1]
    score = jnp.sum(jnp.where(live, soft, 0.0), axis=-1, keepdims=True) / lens_col
    logits = LOGIT_SCALE * score
    peak = jnp.max(logits, axis=0, keepdims=True)
    log_total = peak + jnp.log(jnp.sum(jnp.exp(logits - peak), axis=0, keepdims=True))
    onehot = lax.broadcasted_iota(jnp.int32, (CAPTIONS, 1), 0) == pos_ref[0]
    loss_ref[...] = log_total - jnp.sum(jnp.where(onehot, logits, 0.0), axis=0, keepdims=True)
    grad_logit = LOGIT_SCALE * (jnp.exp(logits - log_total) - onehot.astype(jnp.float32))
    coef = jnp.where(live, grad_logit / lens_col, 0.0)
    mine = stats_ref[place_ref[2] * 2 + place_ref[3], 0]
    hold[...] = coef * jnp.exp2((mine - soft) * SHARP_LOG2)

    eye = lax.broadcasted_iota(jnp.int32, (PADDED, 128), 0) == lax.broadcasted_iota(
        jnp.int32, (PADDED, 128), 1
    )
    core = place_ref[1]
    for m in range(CAPTIONS // 2):
        if 2 * m % group == 0:
            loads[2 * m // group].wait()
        for j, ref in ((2 * m + 1 - core, send_ref), (2 * m + core, keep_ref)):
            col = jnp.sum(jnp.where(eye, hold[pl.ds(j, 1), :], 0.0), axis=-1, keepdims=True)
            ref[m] = (grad[j].astype(jnp.float32) * col).astype(jnp.bfloat16)


def coef_part(place, pos, stats, lens, grad):
    half = jax.ShapeDtypeStruct((CAPTIONS // 2, PADDED, EMB), jnp.bfloat16)
    return pl.pallas_call(
        coef_kernel,
        in_specs=[SMEM, SMEM, VMEM, VMEM, FAR_OFF],
        out_specs=[VMEM] * 3,
        out_shape=[half, half, jax.ShapeDtypeStruct((1, 1), jnp.float32)],
        scratch_shapes=[
            pltpu.VMEM((CAPTIONS, 128), jnp.float32),
            pltpu.VMEM((CAPTIONS, PADDED, EMB), jnp.bfloat16),
            pltpu.SemaphoreType.DMA((4,)),
        ],
        compiler_params=pltpu.CompilerParams(vmem_limit_bytes=12 * MIB),
        cost_estimate=pl.CostEstimate(
            flops=4_000_000, bytes_accessed=6_000_000, transcendentals=100_000
        ),
        name="coef_part",
    )(place, pos, stats, lens, held(grad))


def small_call(kernel, name, operands, out_shapes, specs=None):
    return pl.pallas_call(
        kernel,
        in_specs=specs or [VMEM] * len(operands),
        out_specs=[VMEM] * len(out_shapes),
        out_shape=[jax.ShapeDtypeStruct(s, d) for s, d in out_shapes],
        compiler_params=pltpu.CompilerParams(vmem_limit_bytes=16 * MIB),
        cost_estimate=pl.CostEstimate(flops=0, bytes_accessed=2_000_000, transcendentals=0),
        name=name,
    )(*operands)


def added(a, b):
    return (a.astype(jnp.float32) + b.astype(jnp.float32)).astype(jnp.bfloat16)


def first_sum_kernel(place_ref, keep_ref, got_ref, a_keep, a_send, b_keep, b_send):
    x = place_ref[2]
    plan = (
        (0, ((a_keep, 0, 0), (a_send, 0, 1), (a_send, 1, 2), (a_keep, 1, 3))),
        (8, ((b_keep, 0, 0), (b_keep, 1, 1), (b_send, 1, 2), (b_send, 0, 3))),
    )
    for start, parts in plan:
        for ref, at, flip in parts:
            cols = pl.ds(pl.multiple_of((x ^ flip) * 128, 128), 128)
            for m in range(8):
                ref[m, :, pl.ds(at * 128, 128)] = added(
                    keep_ref[start + m, :, cols], got_ref[start + m, :, cols]
                )


def second_sum_kernel(a_keep, a_got, b_keep, b_got, a_mine, a_send, b_mine, b_send):
    for keep, got, mine, send in ((a_keep, a_got, a_mine, a_send), (b_keep, b_got, b_mine, b_send)):
        mine[...] = added(keep[:, :, :128], got[:, :, :128])
        send[...] = added(keep[:, :, 128:], got[:, :, 128:])


def third_sum_kernel(a_mine, a_got, b_mine, b_got, out):
    out[pl.ds(0, 8)] = added(a_mine[...], a_got[...])
    out[pl.ds(8, 8)] = added(b_mine[...], b_got[...])


def owned_sum_kernel(parts, out):
    total = jnp.sum(parts[...].astype(jnp.float32), axis=0).astype(jnp.bfloat16)
    for k in range(8):
        out[k] = total


def last_sum_kernel(parts, out):
    for x in range(4):
        total = parts[2 * x].astype(jnp.float32) + parts[2 * x + 1].astype(jnp.float32)
        out[:, 0, pl.ds(x * 128, 128)] = total[:SLOTS]


def reduce_gradient(place, send, keep):
    bf16 = jnp.bfloat16
    one = [(s, s ^ 2) for s in range(8)]
    three = [(s, s ^ 6) for s in range(8)]
    got = lax.ppermute(send, "dp", [(i, i ^ 1) for i in range(32)])
    a_keep, a_send, b_keep, b_send = small_call(
        first_sum_kernel, "first_sum", (place, keep, got), [((8, PADDED, 256), bf16)] * 4,
        [SMEM, VMEM, VMEM],
    )
    a_got = lax.ppermute(a_send, "space", one)
    b_got = lax.ppermute(b_send, "space", three)
    a_mine, a_send, b_mine, b_send = small_call(
        second_sum_kernel, "second_sum", (a_keep, a_got, b_keep, b_got),
        [((8, PADDED, 128), bf16)] * 4,
    )
    a_got = lax.ppermute(a_send, "space", three)
    b_got = lax.ppermute(b_send, "space", one)
    (parts,) = small_call(
        third_sum_kernel, "third_sum", (a_mine, a_got, b_mine, b_got), [((16, PADDED, 128), bf16)]
    )
    parts = lax.all_to_all(
        parts, "dp", split_axis=0, concat_axis=0, tiled=True,
        axis_index_groups=[[2 * m + c for m in range(16)] for c in range(2)],
    )
    (parts,) = small_call(owned_sum_kernel, "owned_sum", (parts,), [((8, PADDED, 128), bf16)])
    parts = lax.all_to_all(parts, "space", split_axis=0, concat_axis=0, tiled=True)
    (total,) = small_call(last_sum_kernel, "last_sum", (parts,), [((SLOTS, 1, EMB), jnp.float32)])
    return total.reshape(1, SLOTS, EMB)


def on_device(clip_qkv, temporal_qk, proj_weight, caption_tokens, caption_lens, positive):
    dp = lax.axis_index("dp")
    space = lax.axis_index("space")
    x, y = space >> 1, space & 1
    place = jnp.stack([dp >> 4, dp & 1, x, y, (dp >> 1) & 7]).astype(jnp.int32)
    lens_row = jnp.broadcast_to(
        caption_lens.astype(jnp.bfloat16)[:, None, None], (1, PADDED - SLOTS, EMB)
    )
    caps = jnp.concatenate([caption_tokens, lens_row], axis=1)
    caps = doubled(caps, flip_y(caps))
    caps = doubled(caps, flip(caps, 8))
    pieces, started = bring_frames(clip_qkv[0], place, caps)
    time, done = time_weights(temporal_qk[0], started)
    attended = spatial_attention(place, pieces, done)
    caps = doubled(caps, flip(caps, 4), attended)
    caps = doubled(caps, flip(caps, 2))
    other = flip(caps, 1)
    spatial = lax.all_to_all(attended, "space", split_axis=0, concat_axis=0, tiled=True)
    video, stats, grad, lens = token_part(
        place, spatial, time, proj_weight, caps, other
    )
    stats = lax.all_to_all(stats, "space", split_axis=0, concat_axis=0, tiled=True)
    send, keep, loss = coef_part(place, positive, stats, lens, grad)
    caption_grad = reduce_gradient(place, send, keep)
    return video[None], caption_grad, loss.reshape(1)


def solution(mesh):
    return jax.shard_map(
        on_device,
        mesh=mesh,
        in_specs=(
            P("dp", None, "space", None),
            P("dp", None, "space", None),
            P(),
            P("dp", None, None),
            P("dp"),
            P("dp"),
        ),
        out_specs=(P("dp", None, "space", None), P("dp", None, None), P("dp")),
        check_vma=False,
    )
```

```python
import math

import jax
import jax.numpy as jnp
from jax import lax
from jax.experimental import pallas as pl
from jax.experimental.pallas import tpu as pltpu
from jax.sharding import PartitionSpec as P

HEADS = 13
HD = 128
FEATURES = HEADS * HD
EMB = 512
FRAMES = 16
PATCHES = 256
LOCAL = 32
SLOTS = 77
PADDED = 80
CAPTIONS = 32
SHARPNESS = 4.0
LOGIT_SCALE = 10.0
LOG2E = math.log2(math.e)
SCORE_LOG2 = HD ** (-0.5) * LOG2E
SHARP_LOG2 = SHARPNESS * LOG2E
MIB = 1 << 20
GRANT = pltpu.CompilerParams(vmem_limit_bytes=24 * MIB)
VMEM = pl.BlockSpec(memory_space=pltpu.VMEM)
SMEM = pl.BlockSpec(memory_space=pltpu.SMEM)

FAR_OFF = pl.BlockSpec(memory_space=pltpu.HBM)
ANY = pl.BlockSpec(memory_space=pl.ANY)


def owner(g1, a):
    return (g1 * 2 + ((a >> 1) ^ g1)) * 2 + (a & 1)


def place():
    dp, space = lax.axis_index("dp"), lax.axis_index("space")
    return dp >> 4, dp & 1, space >> 1, space & 1, (dp >> 1) & 7


def quad_place():
    _, _, x, y, _ = place()
    return x >> 1, ((x >> 1) ^ (x & 1)) * 2 + y


def held(value):
    return pltpu.with_memory_space_constraint(value, pltpu.HBM)


def nt(a, b):
    return lax.dot_general(a, b, (((1,), (1,)), ((), ())), preferred_element_type=jnp.float32)


SPLIT = 7


ROW = (LOCAL, 3 * FEATURES)
FULL = pltpu.CompilerParams(vmem_limit_bytes=60 * MIB)


def copied(pairs, buf, sems):
    loads = [
        pltpu.make_async_copy(src, buf.at[i], sems.at[0, i]) for i, (src, _) in enumerate(pairs)
    ]
    stores = [
        pltpu.make_async_copy(buf.at[i], dst, sems.at[1, i]) for i, (_, dst) in enumerate(pairs)
    ]
    for load in loads:
        load.start()
    for load, store in zip(loads, stores):
        load.wait()
        store.start()
    for store in stores:
        store.wait()


def copying(kernel, name, operands, shapes, count, params=FULL):
    return pl.pallas_call(
        kernel,
        in_specs=[ANY] * len(operands),
        out_specs=[ANY] * len(shapes),
        out_shape=[jax.ShapeDtypeStruct((n,) + ROW, jnp.bfloat16) for n in shapes],
        scratch_shapes=[
            pltpu.VMEM((count,) + ROW, jnp.bfloat16),
            pltpu.SemaphoreType.DMA((2, count)),
        ],
        compiler_params=params,
        cost_estimate=pl.CostEstimate(flops=0, bytes_accessed=6_000_000, transcendentals=0),
        name=name,
    )(*operands)


def relay_kernel(clip_ref, one, two, three, buf, sems):
    g1, a = quad_place()
    refs = ((1, one), (2, two), (3, three))
    copied([(clip_ref.at[2 * owner(1 - g1, a ^ k)], ref.at[0]) for k, ref in refs], buf, sems)


def across_kernel(clip_ref, out_ref, buf, sems):
    g1, _ = quad_place()
    copied([(clip_ref.at[2 * owner(1 - g1, a) + 1], out_ref.at[a]) for a in range(4)], buf, sems)


def quads_kernel(clip_ref, one, two, three, buf, sems):
    g1, a = quad_place()
    pairs = [
        (clip_ref.at[2 * owner(g1, a ^ k) + f], ref.at[f])
        for k, ref in ((1, one), (2, two), (3, three))
        for f in range(2)
    ]
    copied(pairs, buf, sems)


def own_kernel(clip_ref, first, kept, buf, sems):
    g1, a = quad_place()
    pairs = [(clip_ref.at[2 * owner(1 - g1, a)], first.at[0])]
    pairs += [(clip_ref.at[2 * owner(g1, a) + f], kept.at[f]) for f in range(2)]
    copied(pairs, buf, sems)


def turn_kernel(first_ref, one, two, three, behind_ref, out_ref, buf, sems):
    refs = (first_ref, one, two, three)
    copied([(ref.at[0], out_ref.at[k]) for k, ref in enumerate(refs)], buf, sems)


def spread_kernel(across_ref, behind_ref, one, two, three, buf, sems):
    _, a = quad_place()
    refs = ((1, one), (2, two), (3, three))
    copied([(across_ref.at[a ^ k], ref.at[0]) for k, ref in refs], buf, sems)


def swap(value, bits):
    return lax.ppermute(value, "space", [(s, s ^ bits) for s in range(8)])


def swap_quad(values):
    return [swap(value, k) for k, value in zip((1, 2, 3), values)]


def bring_frames(clip, behind):
    relays = swap_quad(copying(relay_kernel, "relay", (clip,), (1, 1, 1), 3))
    (across,) = copying(across_kernel, "across", (clip,), (4,), 4)
    across = swap(across, 6)
    quads = copying(quads_kernel, "quads", (clip,), (2, 2, 2), 6)
    prepared = quads[0]
    quads = swap_quad(quads)
    first, kept = copying(own_kernel, "own", (clip,), (1, 2), 3)
    few = pltpu.CompilerParams(vmem_limit_bytes=8 * MIB)
    (turned,) = copying(turn_kernel, "turn", (first, *relays, prepared), (4,), 4, few)
    turned = swap(turned, 6)
    spread = copying(spread_kernel, "spread", (across, behind), (1, 1, 1), 3, few)
    return (kept, across, turned, *quads, *swap_quad(spread)), spread[0]


def spatial_kernel(kept_ref, across_ref, turned_ref, *refs):
    quads, spread, (_, out_ref, buf, res, sems, store_sems) = refs[:3], refs[3:6], refs[6:]
    g1, a = quad_place()
    first = [ref.at[0] for ref in (kept_ref, *quads)] + [turned_ref.at[k] for k in range(4)]
    second = [ref.at[1] for ref in (kept_ref, *quads)]
    second += [across_ref.at[a]] + [ref.at[0] for ref in spread]
    loads = [
        [pltpu.make_async_copy(src, buf.at[f, i], sems.at[f, i]) for i, src in enumerate(sources)]
        for f, sources in enumerate((first, second))
    ]
    for f in range(2):
        for load in loads[f]:
            load.start()
    stores = [
        pltpu.make_async_copy(res.at[f], out_ref.at[:, f], store_sems.at[f]) for f in range(2)
    ]
    for f in range(2):
        for load in loads[f]:
            load.wait()
        for h in range(HEADS):
            q = buf[f, :, :, pl.ds(h * HD, HD)].reshape(PATCHES, HD)
            k = buf[f, :, :, pl.ds(FEATURES + h * HD, HD)].reshape(PATCHES, HD)
            v = buf[f, :, :, pl.ds(2 * FEATURES + h * HD, HD)].reshape(PATCHES, HD)
            s = nt(q, k)
            m = jnp.max(s, axis=-1, keepdims=True)
            e = jnp.exp2((s - m) * SCORE_LOG2)
            total = jnp.sum(e, axis=-1, keepdims=True)
            o = jnp.dot(e.astype(jnp.bfloat16), v, preferred_element_type=jnp.float32)
            o = (o * (1.0 / total)).astype(jnp.bfloat16)
            for i in range(8):
                at = owner(g1 if i < 4 else 1 - g1, a ^ (i & 3))
                res[f, at, :, pl.ds(h * HD, HD)] = o[i * LOCAL : (i + 1) * LOCAL]
        stores[f].start()
    for store in stores:
        store.wait()


def spatial_attention(pieces, behind):
    return pl.pallas_call(
        spatial_kernel,
        in_specs=[ANY] * (len(pieces) + 1),
        out_specs=ANY,
        out_shape=jax.ShapeDtypeStruct((8, 2, LOCAL, FEATURES), jnp.bfloat16),
        scratch_shapes=[
            pltpu.VMEM((2, 8) + ROW, jnp.bfloat16),
            pltpu.VMEM((2, 8, LOCAL, FEATURES), jnp.bfloat16),
            pltpu.SemaphoreType.DMA((2, 8)),
            pltpu.SemaphoreType.DMA((2,)),
        ],
        compiler_params=GRANT,
        cost_estimate=pl.CostEstimate(
            flops=8 * HEADS * PATCHES * PATCHES * HD,
            bytes_accessed=2 * PATCHES * 4 * FEATURES * 2,
            transcendentals=2 * HEADS * PATCHES * PATCHES,
        ),
        name="spatial_attention",
    )(*pieces, behind)


ROWS = FRAMES * 16


def time_kernel(tqk_ref, behind_ref, out_ref, mark_ref, tqk, weights, load_sem, sems):
    load = pltpu.make_async_copy(tqk_ref, tqk, load_sem)
    load.start()
    load.wait()
    mark_ref[...] = jnp.zeros_like(mark_ref)
    r = lax.broadcasted_iota(jnp.int32, (ROWS, ROWS), 0)
    c = lax.broadcasted_iota(jnp.int32, (ROWS, ROWS), 1)
    bias = jnp.where((r & 15) == (c & 15), 0.0, -1e30).astype(jnp.float32)
    stores = []
    for h in range(HEADS):
        for g in range(LOCAL // 16):
            part = pl.ds(g * 16, 16)
            q = tqk[:, part, pl.ds(h * HD, HD)].reshape(ROWS, HD)
            k = tqk[:, part, pl.ds(FEATURES + h * HD, HD)].reshape(ROWS, HD)
            s = nt(q, k) + bias
            m = jnp.max(s, axis=-1, keepdims=True)
            e = jnp.exp2((s - m) * SCORE_LOG2)
            total = jnp.sum(e, axis=-1, keepdims=True)
            weights[h, g] = (e * (1.0 / total)).astype(jnp.bfloat16)
        stores.append(pltpu.make_async_copy(weights.at[h], out_ref.at[h], sems.at[h]))
        stores[-1].start()
    for store in stores:
        store.wait()


def time_weights(temporal_qk, behind):
    return pl.pallas_call(
        time_kernel,
        in_specs=[ANY] * 2,
        out_specs=[ANY, VMEM],
        out_shape=[
            jax.ShapeDtypeStruct((HEADS, 2, ROWS, ROWS), jnp.bfloat16),
            jax.ShapeDtypeStruct((8, 128), jnp.float32),
        ],
        scratch_shapes=[
            pltpu.VMEM((FRAMES, LOCAL, 2 * FEATURES), jnp.bfloat16),
            pltpu.VMEM((HEADS, 2, ROWS, ROWS), jnp.bfloat16),
            pltpu.SemaphoreType.DMA,
            pltpu.SemaphoreType.DMA((HEADS,)),
        ],
        compiler_params=GRANT,
        cost_estimate=pl.CostEstimate(
            flops=4 * HEADS * ROWS * ROWS * HD,
            bytes_accessed=7_000_000,
            transcendentals=2 * HEADS * ROWS * ROWS,
        ),
        name="time_weights",
    )(temporal_qk, behind)


def flip(value, bit):
    return lax.ppermute(value, "dp", [(i, i ^ bit) for i in range(32)])


def join_kernel(*refs):
    refs[-1][0] = refs[0][...]
    refs[-1][1] = refs[1][...]


def flip_y(value):
    pairs = [(i * 8 + s, (i ^ 16) * 8 + (s ^ 1)) for i in range(32) for s in range(8)]
    return lax.ppermute(value, ("dp", "space"), pairs)


def doubled(value, other, *behind):
    both = pl.pallas_call(
        join_kernel,
        in_specs=[VMEM] * 2 + [ANY] * len(behind),
        out_specs=VMEM,
        out_shape=jax.ShapeDtypeStruct((2,) + value.shape, value.dtype),
        compiler_params=pltpu.CompilerParams(vmem_limit_bytes=8 * MIB),
        cost_estimate=pl.CostEstimate(flops=0, bytes_accessed=1_000_000, transcendentals=0),
        name="join",
    )(value, other, *behind)
    return both.reshape((-1,) + value.shape[1:])


def token_kernel(
    value_ref, time_ref, proj_ref, mine_ref, other_ref,
    emb_ref, all_stats_ref, grad_ref, lens_ref,
    value, time, proj, mine, comb, video, grads, stats_ref, sems, time_sems, grad_sems,
):
    value_load = pltpu.make_async_copy(value_ref, value, sems.at[3])
    value_load.start()
    time_loads = [
        pltpu.make_async_copy(time_ref.at[h], time.at[h], time_sems.at[h]) for h in range(HEADS)
    ]
    for load in time_loads:
        load.start()
    proj_load = pltpu.make_async_copy(proj_ref, proj, sems.at[0])
    mine_load = pltpu.make_async_copy(mine_ref, mine, sems.at[1])
    proj_load.start()
    mine_load.start()
    value_load.wait()
    for h in range(HEADS):
        time_loads[h].wait()
        cols = pl.ds(h * HD, HD)
        for g in range(LOCAL // 16):
            part = pl.ds(g * 16, 16)
            v = value[:, :, part, cols].reshape(ROWS, HD)
            o = jnp.dot(time[h, g], v, preferred_element_type=jnp.float32)
            o = (v.astype(jnp.float32) + o).astype(jnp.bfloat16)
            comb[:, part, cols] = o.reshape(FRAMES, 16, HD)
    tokens = FRAMES * LOCAL
    proj_load.wait()
    projected = jnp.dot(
        comb[...].reshape(tokens, FEATURES), proj[...], preferred_element_type=jnp.float32
    )
    scale = lax.rsqrt(jnp.mean(projected * projected, axis=-1, keepdims=True) + 1e-06)
    emb = (projected * scale).astype(jnp.bfloat16)
    video[...] = emb.reshape(FRAMES, LOCAL, EMB)
    emb_store = pltpu.make_async_copy(video, emb_ref, sems.at[2])
    emb_store.start()
    mine_load.wait()

    eye = lax.broadcasted_iota(jnp.int32, (PADDED, 128), 0) == lax.broadcasted_iota(
        jnp.int32, (PADDED, 128), 1
    )
    y_hi, core, _, _, z = place()
    group = 8
    stores = []
    for i, (ref, c) in enumerate(((mine, core), (other_ref, 1 - core))):
        for m0 in range(0, CAPTIONS // 2, group):
            sim = nt(ref[pl.ds(m0, group)].reshape(group * PADDED, EMB), emb)
            top = jnp.max(sim, axis=-1, keepdims=True)
            w = jnp.exp2((sim - top) * SHARP_LOG2)
            total = jnp.sum(w, axis=-1, keepdims=True)
            product = jnp.dot(w.astype(jnp.bfloat16), emb, preferred_element_type=jnp.float32)
            slot = i * CAPTIONS // 2 + m0
            grads[pl.ds(slot, group)] = product.astype(jnp.bfloat16).reshape(group, PADDED, EMB)
            for j in range(group):
                m = m0 + j
                flips = (m >> 3 & 1) + (m >> 2 & 1) * 2 + (m >> 1 & 1) * 4
                at = (y_hi ^ (m & 1)) * 16 + (z ^ flips) * 2 + c
                stores.append(
                    pltpu.make_async_copy(
                        grads.at[slot + j], grad_ref.at[at], grad_sems.at[slot + j]
                    )
                )
                stores[-1].start()
                rng = slice(j * PADDED, (j + 1) * PADDED)
                top_row = jnp.sum(jnp.where(eye, top[rng], 0.0), axis=0, keepdims=True)
                total_row = jnp.sum(jnp.where(eye, total[rng], 0.0), axis=0, keepdims=True)
                stats_ref[0, pl.ds(at, 1), :] = top_row
                stats_ref[1, pl.ds(at, 1), :] = total_row
                lens_ref[pl.ds(at, 1), :] = ref[m, SLOTS : SLOTS + 1, :128].astype(jnp.float32)
    for k in range(8):
        all_stats_ref[k] = stats_ref[...]
    emb_store.wait()
    for store in stores:
        store.wait()


def token_part(spatial, time, proj_weight, mine, other):
    bf16 = jnp.bfloat16
    return pl.pallas_call(
        token_kernel,
        in_specs=[ANY, ANY, ANY, ANY, VMEM],
        out_specs=[ANY, VMEM, ANY, VMEM],
        out_shape=[
            jax.ShapeDtypeStruct((FRAMES, LOCAL, EMB), bf16),
            jax.ShapeDtypeStruct((8, 2, CAPTIONS, 128), jnp.float32),
            jax.ShapeDtypeStruct((CAPTIONS, PADDED, EMB), bf16),
            jax.ShapeDtypeStruct((CAPTIONS, 128), jnp.float32),
        ],
        scratch_shapes=[
            pltpu.VMEM((8, 2, LOCAL, FEATURES), bf16),
            pltpu.VMEM((HEADS, 2, ROWS, ROWS), bf16),
            pltpu.VMEM((FEATURES, EMB), bf16),
            pltpu.VMEM((CAPTIONS // 2, PADDED, EMB), bf16),
            pltpu.VMEM((FRAMES, LOCAL, FEATURES), bf16),
            pltpu.VMEM((FRAMES, LOCAL, EMB), bf16),
            pltpu.VMEM((CAPTIONS, PADDED, EMB), bf16),
            pltpu.VMEM((2, CAPTIONS, 128), jnp.float32),
            pltpu.SemaphoreType.DMA((4,)),
            pltpu.SemaphoreType.DMA((HEADS,)),
            pltpu.SemaphoreType.DMA((CAPTIONS,)),
        ],
        compiler_params=pltpu.CompilerParams(vmem_limit_bytes=48 * MIB),
        cost_estimate=pl.CostEstimate(
            flops=4_500_000_000, bytes_accessed=12_000_000, transcendentals=1_300_000
        ),
        name="token_part",
    )(spatial, time, proj_weight, mine, other)


def coef_kernel(
    pos_ref, stats_ref, lens_ref, grad_ref, send_ref, keep_ref, loss_ref, hold, grad, sems
):
    group = 8
    loads = [
        pltpu.make_async_copy(
            grad_ref.at[pl.ds(group * i, group)], grad.at[pl.ds(group * i, group)], sems.at[i]
        )
        for i in range(CAPTIONS // group)
    ]
    for load in loads:
        load.start()
    tops = stats_ref[:, 0]
    totals = stats_ref[:, 1]
    top = jnp.max(tops, axis=0)
    total = jnp.sum(totals * jnp.exp2((tops - top[None]) * SHARP_LOG2), axis=0)
    soft = top + jnp.log(total) / SHARPNESS
    slot = lax.broadcasted_iota(jnp.int32, (CAPTIONS, 128), 1).astype(jnp.float32)
    lens = lens_ref[...]
    live = slot < lens
    lens_col = lens[:, :1]
    score = jnp.sum(jnp.where(live, soft, 0.0), axis=-1, keepdims=True) / lens_col
    logits = LOGIT_SCALE * score
    peak = jnp.max(logits, axis=0, keepdims=True)
    log_total = peak + jnp.log(jnp.sum(jnp.exp(logits - peak), axis=0, keepdims=True))
    onehot = lax.broadcasted_iota(jnp.int32, (CAPTIONS, 1), 0) == pos_ref[0]
    loss_ref[...] = log_total - jnp.sum(jnp.where(onehot, logits, 0.0), axis=0, keepdims=True)
    grad_logit = LOGIT_SCALE * (jnp.exp(logits - log_total) - onehot.astype(jnp.float32))
    coef = jnp.where(live, grad_logit / lens_col, 0.0)
    mine = stats_ref[lax.axis_index("space"), 0]
    hold[...] = coef * jnp.exp2((mine - soft) * SHARP_LOG2)

    eye = lax.broadcasted_iota(jnp.int32, (PADDED, 128), 0) == lax.broadcasted_iota(
        jnp.int32, (PADDED, 128), 1
    )
    core = lax.axis_index("dp") & 1
    for m in range(CAPTIONS // 2):
        if 2 * m % group == 0:
            loads[2 * m // group].wait()
        for j, ref in ((2 * m + 1 - core, send_ref), (2 * m + core, keep_ref)):
            col = jnp.sum(jnp.where(eye, hold[pl.ds(j, 1), :], 0.0), axis=-1, keepdims=True)
            ref[m] = (grad[j].astype(jnp.float32) * col).astype(jnp.bfloat16)


def coef_part(pos, stats, lens, grad):
    half = jax.ShapeDtypeStruct((CAPTIONS // 2, PADDED, EMB), jnp.bfloat16)
    return pl.pallas_call(
        coef_kernel,
        in_specs=[SMEM, VMEM, VMEM, ANY],
        out_specs=[VMEM] * 3,
        out_shape=[half, half, jax.ShapeDtypeStruct((1, 1), jnp.float32)],
        scratch_shapes=[
            pltpu.VMEM((CAPTIONS, 128), jnp.float32),
            pltpu.VMEM((CAPTIONS, PADDED, EMB), jnp.bfloat16),
            pltpu.SemaphoreType.DMA((4,)),
        ],
        compiler_params=pltpu.CompilerParams(vmem_limit_bytes=12 * MIB),
        cost_estimate=pl.CostEstimate(
            flops=4_000_000, bytes_accessed=6_000_000, transcendentals=100_000
        ),
        name="coef_part",
    )(pos, stats, lens, grad)


def small_call(kernel, name, operands, out_shapes, specs=None):
    return pl.pallas_call(
        kernel,
        in_specs=specs or [VMEM] * len(operands),
        out_specs=[VMEM] * len(out_shapes),
        out_shape=[jax.ShapeDtypeStruct(s, d) for s, d in out_shapes],
        compiler_params=pltpu.CompilerParams(vmem_limit_bytes=16 * MIB),
        cost_estimate=pl.CostEstimate(flops=0, bytes_accessed=2_000_000, transcendentals=0),
        name=name,
    )(*operands)


def added(a, b):
    return (a.astype(jnp.float32) + b.astype(jnp.float32)).astype(jnp.bfloat16)


def first_sum_kernel(keep_ref, got_ref, a_keep, a_send, b_keep, b_send):
    x = lax.axis_index("space") >> 1
    plan = (
        (0, ((a_keep, 0, 0), (a_send, 0, 1), (a_send, 1, 2), (a_keep, 1, 3))),
        (8, ((b_keep, 0, 0), (b_keep, 1, 1), (b_send, 1, 2), (b_send, 0, 3))),
    )
    for start, parts in plan:
        for ref, at, flip in parts:
            cols = pl.ds(pl.multiple_of((x ^ flip) * 128, 128), 128)
            for m in range(8):
                ref[m, :, pl.ds(at * 128, 128)] = added(
                    keep_ref[start + m, :, cols], got_ref[start + m, :, cols]
                )


def second_sum_kernel(a_keep, a_got, b_keep, b_got, a_mine, a_send, b_mine, b_send):
    for keep, got, mine, send in ((a_keep, a_got, a_mine, a_send), (b_keep, b_got, b_mine, b_send)):
        mine[...] = added(keep[:, :, :128], got[:, :, :128])
        send[...] = added(keep[:, :, 128:], got[:, :, 128:])


def third_sum_kernel(a_mine, a_got, b_mine, b_got, out):
    out[pl.ds(0, 8)] = added(a_mine[...], a_got[...])
    out[pl.ds(8, 8)] = added(b_mine[...], b_got[...])


def owned_sum_kernel(parts, out):
    total = jnp.sum(parts[...].astype(jnp.float32), axis=0).astype(jnp.bfloat16)
    for k in range(8):
        out[k] = total


def last_sum_kernel(parts, out):
    for x in range(4):
        total = parts[2 * x].astype(jnp.float32) + parts[2 * x + 1].astype(jnp.float32)
        out[:, 0, pl.ds(x * 128, 128)] = total[:SLOTS]


def reduce_gradient(send, keep):
    bf16 = jnp.bfloat16
    one = [(s, s ^ 2) for s in range(8)]
    three = [(s, s ^ 6) for s in range(8)]
    got = lax.ppermute(send, "dp", [(i, i ^ 1) for i in range(32)])
    a_keep, a_send, b_keep, b_send = small_call(
        first_sum_kernel, "first_sum", (keep, got), [((8, PADDED, 256), bf16)] * 4
    )
    a_got = lax.ppermute(a_send, "space", one)
    b_got = lax.ppermute(b_send, "space", three)
    a_mine, a_send, b_mine, b_send = small_call(
        second_sum_kernel, "second_sum", (a_keep, a_got, b_keep, b_got),
        [((8, PADDED, 128), bf16)] * 4,
    )
    a_got = lax.ppermute(a_send, "space", three)
    b_got = lax.ppermute(b_send, "space", one)
    (parts,) = small_call(
        third_sum_kernel, "third_sum", (a_mine, a_got, b_mine, b_got), [((16, PADDED, 128), bf16)]
    )
    parts = lax.all_to_all(
        parts, "dp", split_axis=0, concat_axis=0, tiled=True,
        axis_index_groups=[[2 * m + c for m in range(16)] for c in range(2)],
    )
    (parts,) = small_call(owned_sum_kernel, "owned_sum", (parts,), [((8, PADDED, 128), bf16)])
    parts = lax.all_to_all(parts, "space", split_axis=0, concat_axis=0, tiled=True)
    (total,) = small_call(last_sum_kernel, "last_sum", (parts,), [((SLOTS, 1, EMB), jnp.float32)])
    return total.reshape(1, SLOTS, EMB)


def on_device(clip_qkv, temporal_qk, proj_weight, caption_tokens, caption_lens, positive):
    lens_row = jnp.broadcast_to(
        caption_lens.astype(jnp.bfloat16)[:, None, None], (1, PADDED - SLOTS, EMB)
    )
    caps = jnp.concatenate([caption_tokens, lens_row], axis=1)
    caps = doubled(caps, flip_y(caps))
    caps = doubled(caps, flip(caps, 8))
    pieces, started = bring_frames(clip_qkv[0], caps)
    time, done = time_weights(temporal_qk[0], started)
    caps = doubled(caps, flip(caps, 4), done)
    caps = doubled(caps, flip(caps, 2))
    other = flip(caps, 1)
    attended = spatial_attention(pieces, done)
    spatial = lax.all_to_all(attended, "space", split_axis=0, concat_axis=0, tiled=True)
    video, stats, grad, lens = token_part(spatial, time, proj_weight, caps, other)
    stats = lax.all_to_all(stats, "space", split_axis=0, concat_axis=0, tiled=True)
    send, keep, loss = coef_part(positive, stats, lens, grad)
    caption_grad = reduce_gradient(send, keep)
    return video[None], caption_grad, loss.reshape(1)


def solution(mesh):
    return jax.shard_map(
        on_device,
        mesh=mesh,
        in_specs=(
            P("dp", None, "space", None),
            P("dp", None, "space", None),
            P(),
            P("dp", None, None),
            P("dp"),
            P("dp"),
        ),
        out_specs=(P("dp", None, "space", None), P("dp", None, None), P("dp")),
        check_vma=False,
    )
```

```python
import functools
import math

import jax
import jax.numpy as jnp
from jax import lax
from jax.experimental import pallas as pl
from jax.experimental.pallas import tpu as pltpu
from jax.sharding import PartitionSpec as P

HEADS = 13
HD = 128
FEATURES = HEADS * HD
EMB = 512
FRAMES = 16
PATCHES = 256
LOCAL = 32
SLOTS = 77
PADDED = 80
CAPTIONS = 32
SHARPNESS = 4.0
LOGIT_SCALE = 10.0
LOG2E = math.log2(math.e)
SCORE_LOG2 = HD ** (-0.5) * LOG2E
SHARP_LOG2 = SHARPNESS * LOG2E
MIB = 1 << 20
GRANT = pltpu.CompilerParams(vmem_limit_bytes=24 * MIB)
VMEM = pl.BlockSpec(memory_space=pltpu.VMEM)
SMEM = pl.BlockSpec(memory_space=pltpu.SMEM)

FAR_OFF = pl.BlockSpec(memory_space=pltpu.HBM)
ANY = pl.BlockSpec(memory_space=pl.ANY)


def owner(g1, a):
    return (g1 * 2 + ((a >> 1) ^ g1)) * 2 + (a & 1)


def place():
    dp, space = lax.axis_index("dp"), lax.axis_index("space")
    return dp >> 4, dp & 1, space >> 1, space & 1, (dp >> 1) & 7


def quad_place():
    _, _, x, y, _ = place()
    return x >> 1, ((x >> 1) ^ (x & 1)) * 2 + y


def held(value):
    return pltpu.with_memory_space_constraint(value, pltpu.HBM)


def nt(a, b):
    return lax.dot_general(a, b, (((1,), (1,)), ((), ())), preferred_element_type=jnp.float32)


SPLIT = 7


ROW = (LOCAL, 3 * FEATURES)
FULL = pltpu.CompilerParams(vmem_limit_bytes=60 * MIB)


def copied(pairs, buf, sems):
    loads = [
        pltpu.make_async_copy(src, buf.at[i], sems.at[0, i]) for i, (src, _) in enumerate(pairs)
    ]
    stores = [
        pltpu.make_async_copy(buf.at[i], dst, sems.at[1, i]) for i, (_, dst) in enumerate(pairs)
    ]
    for load in loads:
        load.start()
    for load, store in zip(loads, stores):
        load.wait()
        store.start()
    for store in stores:
        store.wait()


def copying(kernel, name, operands, shapes, count, params=FULL):
    return pl.pallas_call(
        kernel,
        in_specs=[ANY] * len(operands),
        out_specs=[ANY] * len(shapes),
        out_shape=[jax.ShapeDtypeStruct((n,) + ROW, jnp.bfloat16) for n in shapes],
        scratch_shapes=[
            pltpu.VMEM((count,) + ROW, jnp.bfloat16),
            pltpu.SemaphoreType.DMA((2, count)),
        ],
        compiler_params=params,
        cost_estimate=pl.CostEstimate(flops=0, bytes_accessed=6_000_000, transcendentals=0),
        name=name,
    )(*operands)


def depart_kernel(clip_ref, one, two, three, across_ref, buf, sems):
    g1, a = quad_place()
    pairs = [
        (clip_ref.at[2 * owner(g, a ^ k)], ref.at[g])
        for k, ref in ((1, one), (2, two), (3, three))
        for g in range(2)
    ]
    pairs += [(clip_ref.at[2 * owner(1 - g1, b) + 1], across_ref.at[b]) for b in range(4)]
    copied(pairs, buf, sems)


def own_kernel(clip_ref, first, seconds, kept, buf, sems):
    g1, a = quad_place()
    pairs = [(clip_ref.at[2 * owner(1 - g1, a)], first.at[0])]
    pairs += [(clip_ref.at[2 * owner(g1, a ^ k) + 1], seconds.at[k - 1]) for k in (1, 2, 3)]
    pairs += [(clip_ref.at[2 * owner(g1, a) + f], kept.at[f]) for f in range(2)]
    copied(pairs, buf, sems)


def turn_kernel(first_ref, one, two, three, behind_ref, out_ref, buf, sems):
    g1, _ = quad_place()
    pairs = [(first_ref.at[0], out_ref.at[0])]
    pairs += [(ref.at[1 - g1], out_ref.at[k]) for k, ref in ((1, one), (2, two), (3, three))]
    copied(pairs, buf, sems)


def spread_kernel(seconds_ref, across_ref, one, two, three, buf, sems):
    _, a = quad_place()
    pairs = []
    for k, ref in ((1, one), (2, two), (3, three)):
        pairs += [(seconds_ref.at[k - 1], ref.at[0]), (across_ref.at[a ^ k], ref.at[1])]
    copied(pairs, buf, sems)


def swap(value, bits):
    return lax.ppermute(value, "space", [(s, s ^ bits) for s in range(8)])


def bring_frames(clip, behind):
    *quads, across = copying(depart_kernel, "depart", (clip,), (2, 2, 2, 4), 10)
    across = swap(across, 6)
    quads = [swap(quad, k) for k, quad in zip((1, 2, 3), quads)]
    first, seconds, kept = copying(own_kernel, "own", (clip,), (1, 3, 2), 6)
    few = pltpu.CompilerParams(vmem_limit_bytes=8 * MIB)
    (turned,) = copying(turn_kernel, "turn", (first, *quads, behind), (4,), 4, few)
    turned = swap(turned, 6)
    pairs = copying(spread_kernel, "spread", (seconds, across), (2, 2, 2), 6, few)
    started = pairs[0]
    pairs = [swap(pair, k) for k, pair in zip((1, 2, 3), pairs)]
    return (kept, across, turned, *quads, *pairs), started


def spatial_kernel(kept_ref, across_ref, turned_ref, *refs):
    quads, pairs, (_, out_ref, buf, res, sems, store_sems) = refs[:3], refs[3:6], refs[6:]
    g1, a = quad_place()
    first = [kept_ref.at[0]] + [ref.at[g1] for ref in quads] + [turned_ref.at[k] for k in range(4)]
    second = [kept_ref.at[1]] + [ref.at[0] for ref in pairs]
    second += [across_ref.at[a]] + [ref.at[1] for ref in pairs]
    loads = [
        [pltpu.make_async_copy(src, buf.at[f, i], sems.at[f, i]) for i, src in enumerate(sources)]
        for f, sources in enumerate((first, second))
    ]
    for f in range(2):
        for load in loads[f]:
            load.start()
    stores = [
        pltpu.make_async_copy(res.at[f], out_ref.at[:, f], store_sems.at[f]) for f in range(2)
    ]
    for f in range(2):
        for load in loads[f]:
            load.wait()
        for h in range(HEADS):
            q = buf[f, :, :, pl.ds(h * HD, HD)].reshape(PATCHES, HD)
            k = buf[f, :, :, pl.ds(FEATURES + h * HD, HD)].reshape(PATCHES, HD)
            v = buf[f, :, :, pl.ds(2 * FEATURES + h * HD, HD)].reshape(PATCHES, HD)
            s = nt(q, k)
            m = jnp.max(s, axis=-1, keepdims=True)
            e = jnp.exp2((s - m) * SCORE_LOG2)
            total = jnp.sum(e, axis=-1, keepdims=True)
            o = jnp.dot(e.astype(jnp.bfloat16), v, preferred_element_type=jnp.float32)
            o = (o * (1.0 / total)).astype(jnp.bfloat16)
            for i in range(8):
                at = owner(g1 if i < 4 else 1 - g1, a ^ (i & 3))
                res[f, at, :, pl.ds(h * HD, HD)] = o[i * LOCAL : (i + 1) * LOCAL]
        stores[f].start()
    for store in stores:
        store.wait()


def spatial_attention(pieces, behind):
    return pl.pallas_call(
        spatial_kernel,
        in_specs=[ANY] * (len(pieces) + 1),
        out_specs=ANY,
        out_shape=jax.ShapeDtypeStruct((8, 2, LOCAL, FEATURES), jnp.bfloat16),
        scratch_shapes=[
            pltpu.VMEM((2, 8) + ROW, jnp.bfloat16),
            pltpu.VMEM((2, 8, LOCAL, FEATURES), jnp.bfloat16),
            pltpu.SemaphoreType.DMA((2, 8)),
            pltpu.SemaphoreType.DMA((2,)),
        ],
        compiler_params=GRANT,
        cost_estimate=pl.CostEstimate(
            flops=8 * HEADS * PATCHES * PATCHES * HD,
            bytes_accessed=2 * PATCHES * 4 * FEATURES * 2,
            transcendentals=2 * HEADS * PATCHES * PATCHES,
        ),
        name="spatial_attention",
    )(*pieces, behind)


ROWS = FRAMES * 16


def time_kernel(tqk_ref, behind_ref, out_ref, mark_ref, tqk, weights, load_sem, sems):
    load = pltpu.make_async_copy(tqk_ref, tqk, load_sem)
    load.start()
    load.wait()
    mark_ref[...] = jnp.zeros_like(mark_ref)
    r = lax.broadcasted_iota(jnp.int32, (ROWS, ROWS), 0)
    c = lax.broadcasted_iota(jnp.int32, (ROWS, ROWS), 1)
    bias = jnp.where((r & 15) == (c & 15), 0.0, -1e30).astype(jnp.float32)
    stores = []
    for h in range(HEADS):
        for g in range(LOCAL // 16):
            part = pl.ds(g * 16, 16)
            q = tqk[:, part, pl.ds(h * HD, HD)].reshape(ROWS, HD)
            k = tqk[:, part, pl.ds(FEATURES + h * HD, HD)].reshape(ROWS, HD)
            s = nt(q, k) + bias
            m = jnp.max(s, axis=-1, keepdims=True)
            e = jnp.exp2((s - m) * SCORE_LOG2)
            total = jnp.sum(e, axis=-1, keepdims=True)
            weights[h, g] = (e * (1.0 / total)).astype(jnp.bfloat16)
        stores.append(pltpu.make_async_copy(weights.at[h], out_ref.at[h], sems.at[h]))
        stores[-1].start()
    for store in stores:
        store.wait()


def time_weights(temporal_qk, behind):
    return pl.pallas_call(
        time_kernel,
        in_specs=[ANY] * 2,
        out_specs=[ANY, VMEM],
        out_shape=[
            jax.ShapeDtypeStruct((HEADS, 2, ROWS, ROWS), jnp.bfloat16),
            jax.ShapeDtypeStruct((8, 128), jnp.float32),
        ],
        scratch_shapes=[
            pltpu.VMEM((FRAMES, LOCAL, 2 * FEATURES), jnp.bfloat16),
            pltpu.VMEM((HEADS, 2, ROWS, ROWS), jnp.bfloat16),
            pltpu.SemaphoreType.DMA,
            pltpu.SemaphoreType.DMA((HEADS,)),
        ],
        compiler_params=GRANT,
        cost_estimate=pl.CostEstimate(
            flops=4 * HEADS * ROWS * ROWS * HD,
            bytes_accessed=7_000_000,
            transcendentals=2 * HEADS * ROWS * ROWS,
        ),
        name="time_weights",
    )(temporal_qk, behind)


def flip(value, bit):
    return lax.ppermute(value, "dp", [(i, i ^ bit) for i in range(32)])


def join_kernel(*refs):
    refs[-1][0] = refs[0][...]
    refs[-1][1] = refs[1][...]


def flip_y(value):
    pairs = [(i * 8 + s, (i ^ 16) * 8 + (s ^ 1)) for i in range(32) for s in range(8)]
    return lax.ppermute(value, ("dp", "space"), pairs)


def doubled(value, other, *behind):
    both = pl.pallas_call(
        join_kernel,
        in_specs=[VMEM] * 2 + [ANY] * len(behind),
        out_specs=VMEM,
        out_shape=jax.ShapeDtypeStruct((2,) + value.shape, value.dtype),
        compiler_params=pltpu.CompilerParams(vmem_limit_bytes=8 * MIB),
        cost_estimate=pl.CostEstimate(flops=0, bytes_accessed=1_000_000, transcendentals=0),
        name="join",
    )(value, other, *behind)
    return both.reshape((-1,) + value.shape[1:])


def token_kernel(
    value, time_ref, proj_ref, mine_ref, other_ref,
    emb_ref, all_stats_ref, grad_ref, lens_ref,
    proj, mine, comb, video, grads, stats_ref, sems, grad_sems,
):
    proj_load = pltpu.make_async_copy(proj_ref, proj, sems.at[0])
    mine_load = pltpu.make_async_copy(mine_ref, mine, sems.at[1])
    proj_load.start()
    mine_load.start()
    for h in range(HEADS):
        cols = pl.ds(h * HD, HD)
        for g in range(LOCAL // 16):
            part = pl.ds(g * 16, 16)
            v = value[:, :, part, cols].reshape(ROWS, HD)
            o = jnp.dot(time_ref[h, g], v, preferred_element_type=jnp.float32)
            o = (v.astype(jnp.float32) + o).astype(jnp.bfloat16)
            comb[:, part, cols] = o.reshape(FRAMES, 16, HD)
    tokens = FRAMES * LOCAL
    proj_load.wait()
    projected = jnp.dot(
        comb[...].reshape(tokens, FEATURES), proj[...], preferred_element_type=jnp.float32
    )
    scale = lax.rsqrt(jnp.mean(projected * projected, axis=-1, keepdims=True) + 1e-06)
    emb = (projected * scale).astype(jnp.bfloat16)
    video[...] = emb.reshape(FRAMES, LOCAL, EMB)
    emb_store = pltpu.make_async_copy(video, emb_ref, sems.at[2])
    emb_store.start()
    mine_load.wait()

    eye = lax.broadcasted_iota(jnp.int32, (PADDED, 128), 0) == lax.broadcasted_iota(
        jnp.int32, (PADDED, 128), 1
    )
    y_hi, core, _, _, z = place()
    group = 8
    stores = []
    for i, (ref, c) in enumerate(((mine, core), (other_ref, 1 - core))):
        for m0 in range(0, CAPTIONS // 2, group):
            sim = nt(ref[pl.ds(m0, group)].reshape(group * PADDED, EMB), emb)
            top = jnp.max(sim, axis=-1, keepdims=True)
            w = jnp.exp2((sim - top) * SHARP_LOG2)
            total = jnp.sum(w, axis=-1, keepdims=True)
            product = jnp.dot(w.astype(jnp.bfloat16), emb, preferred_element_type=jnp.float32)
            slot = i * CAPTIONS // 2 + m0
            grads[pl.ds(slot, group)] = product.astype(jnp.bfloat16).reshape(group, PADDED, EMB)
            for j in range(group):
                m = m0 + j
                flips = (m >> 3 & 1) + (m >> 2 & 1) * 2 + (m >> 1 & 1) * 4
                at = (y_hi ^ (m & 1)) * 16 + (z ^ flips) * 2 + c
                stores.append(
                    pltpu.make_async_copy(
                        grads.at[slot + j], grad_ref.at[at], grad_sems.at[slot + j]
                    )
                )
                stores[-1].start()
                rng = slice(j * PADDED, (j + 1) * PADDED)
                top_row = jnp.sum(jnp.where(eye, top[rng], 0.0), axis=0, keepdims=True)
                total_row = jnp.sum(jnp.where(eye, total[rng], 0.0), axis=0, keepdims=True)
                stats_ref[0, pl.ds(at, 1), :] = top_row
                stats_ref[1, pl.ds(at, 1), :] = total_row
                lens_ref[pl.ds(at, 1), :] = ref[m, SLOTS : SLOTS + 1, :128].astype(jnp.float32)
    for k in range(8):
        all_stats_ref[k] = stats_ref[...]
    emb_store.wait()
    for store in stores:
        store.wait()


def token_part(spatial, time, proj_weight, mine, other):
    bf16 = jnp.bfloat16
    return pl.pallas_call(
        token_kernel,
        in_specs=[VMEM, VMEM, FAR_OFF, FAR_OFF, VMEM],
        out_specs=[FAR_OFF, VMEM, FAR_OFF, VMEM],
        out_shape=[
            pltpu.HBM((FRAMES, LOCAL, EMB), bf16),
            jax.ShapeDtypeStruct((8, 2, CAPTIONS, 128), jnp.float32),
            pltpu.HBM((CAPTIONS, PADDED, EMB), bf16),
            jax.ShapeDtypeStruct((CAPTIONS, 128), jnp.float32),
        ],
        scratch_shapes=[
            pltpu.VMEM((FEATURES, EMB), bf16),
            pltpu.VMEM((CAPTIONS // 2, PADDED, EMB), bf16),
            pltpu.VMEM((FRAMES, LOCAL, FEATURES), bf16),
            pltpu.VMEM((FRAMES, LOCAL, EMB), bf16),
            pltpu.VMEM((CAPTIONS, PADDED, EMB), bf16),
            pltpu.VMEM((2, CAPTIONS, 128), jnp.float32),
            pltpu.SemaphoreType.DMA((3,)),
            pltpu.SemaphoreType.DMA((CAPTIONS,)),
        ],
        compiler_params=GRANT,
        cost_estimate=pl.CostEstimate(
            flops=4_500_000_000, bytes_accessed=12_000_000, transcendentals=1_300_000
        ),
        name="token_part",
    )(spatial, time, held(proj_weight), held(mine), other)


def coef_kernel(
    pos_ref, stats_ref, lens_ref, grad_ref, send_ref, keep_ref, loss_ref, hold, grad, sems
):
    group = 8
    loads = [
        pltpu.make_async_copy(
            grad_ref.at[pl.ds(group * i, group)], grad.at[pl.ds(group * i, group)], sems.at[i]
        )
        for i in range(CAPTIONS // group)
    ]
    for load in loads:
        load.start()
    tops = stats_ref[:, 0]
    totals = stats_ref[:, 1]
    top = jnp.max(tops, axis=0)
    total = jnp.sum(totals * jnp.exp2((tops - top[None]) * SHARP_LOG2), axis=0)
    soft = top + jnp.log(total) / SHARPNESS
    slot = lax.broadcasted_iota(jnp.int32, (CAPTIONS, 128), 1).astype(jnp.float32)
    lens = lens_ref[...]
    live = slot < lens
    lens_col = lens[:, :1]
    score = jnp.sum(jnp.where(live, soft, 0.0), axis=-1, keepdims=True) / lens_col
    logits = LOGIT_SCALE * score
    peak = jnp.max(logits, axis=0, keepdims=True)
    log_total = peak + jnp.log(jnp.sum(jnp.exp(logits - peak), axis=0, keepdims=True))
    onehot = lax.broadcasted_iota(jnp.int32, (CAPTIONS, 1), 0) == pos_ref[0]
    loss_ref[...] = log_total - jnp.sum(jnp.where(onehot, logits, 0.0), axis=0, keepdims=True)
    grad_logit = LOGIT_SCALE * (jnp.exp(logits - log_total) - onehot.astype(jnp.float32))
    coef = jnp.where(live, grad_logit / lens_col, 0.0)
    mine = stats_ref[lax.axis_index("space"), 0]
    hold[...] = coef * jnp.exp2((mine - soft) * SHARP_LOG2)

    eye = lax.broadcasted_iota(jnp.int32, (PADDED, 128), 0) == lax.broadcasted_iota(
        jnp.int32, (PADDED, 128), 1
    )
    core = lax.axis_index("dp") & 1
    for m in range(CAPTIONS // 2):
        if 2 * m % group == 0:
            loads[2 * m // group].wait()
        for j, ref in ((2 * m + 1 - core, send_ref), (2 * m + core, keep_ref)):
            col = jnp.sum(jnp.where(eye, hold[pl.ds(j, 1), :], 0.0), axis=-1, keepdims=True)
            ref[m] = (grad[j].astype(jnp.float32) * col).astype(jnp.bfloat16)


def coef_part(pos, stats, lens, grad):
    half = jax.ShapeDtypeStruct((CAPTIONS // 2, PADDED, EMB), jnp.bfloat16)
    return pl.pallas_call(
        coef_kernel,
        in_specs=[SMEM, VMEM, VMEM, FAR_OFF],
        out_specs=[VMEM] * 3,
        out_shape=[half, half, jax.ShapeDtypeStruct((1, 1), jnp.float32)],
        scratch_shapes=[
            pltpu.VMEM((CAPTIONS, 128), jnp.float32),
            pltpu.VMEM((CAPTIONS, PADDED, EMB), jnp.bfloat16),
            pltpu.SemaphoreType.DMA((4,)),
        ],
        compiler_params=pltpu.CompilerParams(vmem_limit_bytes=12 * MIB),
        cost_estimate=pl.CostEstimate(
            flops=4_000_000, bytes_accessed=6_000_000, transcendentals=100_000
        ),
        name="coef_part",
    )(pos, stats, lens, held(grad))


def small_call(kernel, name, operands, out_shapes, specs=None):
    return pl.pallas_call(
        kernel,
        in_specs=specs or [VMEM] * len(operands),
        out_specs=[VMEM] * len(out_shapes),
        out_shape=[jax.ShapeDtypeStruct(s, d) for s, d in out_shapes],
        compiler_params=pltpu.CompilerParams(vmem_limit_bytes=16 * MIB),
        cost_estimate=pl.CostEstimate(flops=0, bytes_accessed=2_000_000, transcendentals=0),
        name=name,
    )(*operands)


def added(a, b):
    return (a.astype(jnp.float32) + b.astype(jnp.float32)).astype(jnp.bfloat16)


def first_sum_kernel(keep_ref, got_ref, a_keep, a_send, b_keep, b_send):
    x = lax.axis_index("space") >> 1
    plan = (
        (0, ((a_keep, 0, 0), (a_send, 0, 1), (a_send, 1, 2), (a_keep, 1, 3))),
        (4, ((b_keep, 0, 0), (b_keep, 1, 1), (b_send, 1, 2), (b_send, 0, 3))),
    )
    for start, parts in plan:
        for ref, at, flipped in parts:
            cols = pl.ds(pl.multiple_of((x ^ flipped) * 128, 128), 128)
            for m in range(8):
                source = m // 4 * 8 + start + m % 4
                ref[m, :, pl.ds(at * 128, 128)] = added(
                    keep_ref[source, :, cols], got_ref[source, :, cols]
                )


def second_sum_kernel(a_keep, a_got, b_keep, b_got, a_mine, a_send, b_mine, b_send):
    a_mine[...] = added(a_keep[:, :, :128], a_got[:, :, :128])
    a_send[...] = added(a_keep[:, :, 128:], a_got[:, :, 128:])
    y_hi = lax.axis_index("dp") >> 4
    for ref, side in ((b_mine, y_hi), (b_send, 1 - y_hi)):
        some = pl.ds(side * 4, 4)
        ref[...] = added(b_keep[some], b_got[some])


def third_sum_kernel(a_keep, a_got, b_keep, b_got, a_mine, a_send, b_mine, b_send):
    y_hi = lax.axis_index("dp") >> 4
    for ref, side in ((a_mine, y_hi), (a_send, 1 - y_hi)):
        some = pl.ds(side * 4, 4)
        ref[...] = added(a_keep[some], a_got[some])
    b_mine[...] = added(b_keep[:, :, :128], b_got[:, :, :128])
    b_send[...] = added(b_keep[:, :, 128:], b_got[:, :, 128:])


def fourth_sum_kernel(a_mine, a_got, b_mine, b_got, out):
    out[pl.ds(0, 4)] = added(a_mine[...], a_got[...])
    out[pl.ds(4, 4)] = added(b_mine[...], b_got[...])


def owned_sum_kernel(parts, out):
    total = jnp.sum(parts[...].astype(jnp.float32), axis=0).astype(jnp.bfloat16)
    for k in range(8):
        out[k] = total


def last_sum_kernel(parts, out):
    for x in range(4):
        total = parts[2 * x].astype(jnp.float32) + parts[2 * x + 1].astype(jnp.float32)
        out[:, 0, pl.ds(x * 128, 128)] = total[:SLOTS]


def reduce_gradient(send, keep):
    bf16 = jnp.bfloat16
    got = lax.ppermute(send, "dp", [(i, i ^ 1) for i in range(32)])
    a_keep, a_send, b_keep, b_send = small_call(
        first_sum_kernel, "first_sum", (keep, got), [((8, PADDED, 256), bf16)] * 4
    )
    a_keep, a_send, b_keep, b_send = small_call(
        second_sum_kernel, "second_sum", (a_keep, swap(a_send, 2), b_keep, swap(b_send, 6)),
        [((8, PADDED, 128), bf16)] * 2 + [((4, PADDED, 256), bf16)] * 2,
    )
    a_keep, a_send, b_keep, b_send = small_call(
        third_sum_kernel, "third_sum", (a_keep, swap(a_send, 6), b_keep, flip_y(b_send)),
        [((4, PADDED, 128), bf16)] * 4,
    )
    (parts,) = small_call(
        fourth_sum_kernel, "fourth_sum", (a_keep, flip_y(a_send), b_keep, swap(b_send, 2)),
        [((8, PADDED, 128), bf16)],
    )
    parts = lax.all_to_all(
        parts, "dp", split_axis=0, concat_axis=0, tiled=True,
        axis_index_groups=[[y * 16 + z * 2 + c for z in range(8)] for y in range(2) for c in range(2)],
    )
    (parts,) = small_call(owned_sum_kernel, "owned_sum", (parts,), [((8, PADDED, 128), bf16)])
    parts = lax.all_to_all(parts, "space", split_axis=0, concat_axis=0, tiled=True)
    (total,) = small_call(last_sum_kernel, "last_sum", (parts,), [((SLOTS, 1, EMB), jnp.float32)])
    return total.reshape(1, SLOTS, EMB)


def on_device(clip_qkv, temporal_qk, proj_weight, caption_tokens, caption_lens, positive):
    lens_row = jnp.broadcast_to(
        caption_lens.astype(jnp.bfloat16)[:, None, None], (1, PADDED - SLOTS, EMB)
    )
    caps = jnp.concatenate([caption_tokens, lens_row], axis=1)
    caps = doubled(caps, flip_y(caps))
    far = flip(caps, 8)
    pieces, started = bring_frames(clip_qkv[0], far)
    caps = doubled(caps, far, started)
    time, done = time_weights(temporal_qk[0], started)
    caps = doubled(caps, flip(caps, 4), done)
    caps = doubled(caps, flip(caps, 2))
    other = flip(caps, 1)
    attended = spatial_attention(pieces, done)
    spatial = lax.all_to_all(attended, "space", split_axis=0, concat_axis=0, tiled=True)
    video, stats, grad, lens = token_part(spatial, time, proj_weight, caps, other)
    stats = lax.all_to_all(stats, "space", split_axis=0, concat_axis=0, tiled=True)
    send, keep, loss = coef_part(positive, stats, lens, grad)
    caption_grad = reduce_gradient(send, keep)
    return video[None], caption_grad, loss.reshape(1)


def solution(mesh):
    return jax.shard_map(
        on_device,
        mesh=mesh,
        in_specs=(
            P("dp", None, "space", None),
            P("dp", None, "space", None),
            P(),
            P("dp", None, None),
            P("dp"),
            P("dp"),
        ),
        out_specs=(P("dp", None, "space", None), P("dp", None, None), P("dp")),
        check_vma=False,
    )
```

```python
import functools
import math

import jax
import jax.numpy as jnp
from jax import lax
from jax.experimental import pallas as pl
from jax.experimental.pallas import tpu as pltpu
from jax.sharding import PartitionSpec as P

HEADS = 13
HD = 128
FEATURES = HEADS * HD
EMB = 512
FRAMES = 16
PATCHES = 256
LOCAL = 32
SLOTS = 77
PADDED = 80
CAPTIONS = 32
SHARPNESS = 4.0
LOGIT_SCALE = 10.0
LOG2E = math.log2(math.e)
SCORE_LOG2 = HD ** (-0.5) * LOG2E
SHARP_LOG2 = SHARPNESS * LOG2E
MIB = 1 << 20
GRANT = pltpu.CompilerParams(vmem_limit_bytes=24 * MIB)
VMEM = pl.BlockSpec(memory_space=pltpu.VMEM)
SMEM = pl.BlockSpec(memory_space=pltpu.SMEM)

FAR_OFF = pl.BlockSpec(memory_space=pltpu.HBM)
ANY = pl.BlockSpec(memory_space=pl.ANY)


def owner(g1, a):
    return (g1 * 2 + ((a >> 1) ^ g1)) * 2 + (a & 1)


def place():
    dp, space = lax.axis_index("dp"), lax.axis_index("space")
    return dp >> 4, dp & 1, space >> 1, space & 1, (dp >> 1) & 7


def quad_place():
    _, _, x, y, _ = place()
    return x >> 1, ((x >> 1) ^ (x & 1)) * 2 + y


def held(value):
    return pltpu.with_memory_space_constraint(value, pltpu.HBM)


def nt(a, b):
    return lax.dot_general(a, b, (((1,), (1,)), ((), ())), preferred_element_type=jnp.float32)


SPLIT = 7


ROW = (LOCAL, 3 * FEATURES)
FULL = pltpu.CompilerParams(vmem_limit_bytes=60 * MIB)


def copied(pairs, buf, sems):
    loads = [
        pltpu.make_async_copy(src, buf.at[i], sems.at[0, i]) for i, (src, _) in enumerate(pairs)
    ]
    stores = [
        pltpu.make_async_copy(buf.at[i], dst, sems.at[1, i]) for i, (_, dst) in enumerate(pairs)
    ]
    for load in loads:
        load.start()
    for load, store in zip(loads, stores):
        load.wait()
        store.start()
    for store in stores:
        store.wait()


def copying(kernel, name, operands, shapes, count, params=FULL):
    return pl.pallas_call(
        kernel,
        in_specs=[ANY] * len(operands),
        out_specs=[ANY] * len(shapes),
        out_shape=[jax.ShapeDtypeStruct((n,) + ROW, jnp.bfloat16) for n in shapes],
        scratch_shapes=[
            pltpu.VMEM((count,) + ROW, jnp.bfloat16),
            pltpu.SemaphoreType.DMA((2, count)),
        ],
        compiler_params=params,
        cost_estimate=pl.CostEstimate(flops=0, bytes_accessed=6_000_000, transcendentals=0),
        name=name,
    )(*operands)


def depart_kernel(clip_ref, one, two, three, across_ref, buf, sems):
    g1, a = quad_place()
    pairs = [
        (clip_ref.at[2 * owner(g, a ^ k)], ref.at[g])
        for k, ref in ((1, one), (2, two), (3, three))
        for g in range(2)
    ]
    pairs += [(clip_ref.at[2 * owner(1 - g1, b) + 1], across_ref.at[b]) for b in range(4)]
    copied(pairs, buf, sems)


def own_kernel(clip_ref, first, seconds, kept, buf, sems):
    g1, a = quad_place()
    pairs = [(clip_ref.at[2 * owner(1 - g1, a)], first.at[0])]
    pairs += [(clip_ref.at[2 * owner(g1, a ^ k) + 1], seconds.at[k - 1]) for k in (1, 2, 3)]
    pairs += [(clip_ref.at[2 * owner(g1, a) + f], kept.at[f]) for f in range(2)]
    copied(pairs, buf, sems)


def turn_kernel(first_ref, one, two, three, behind_ref, out_ref, buf, sems):
    g1, _ = quad_place()
    pairs = [(first_ref.at[0], out_ref.at[0])]
    pairs += [(ref.at[1 - g1], out_ref.at[k]) for k, ref in ((1, one), (2, two), (3, three))]
    copied(pairs, buf, sems)


def spread_kernel(seconds_ref, across_ref, one, two, three, buf, sems):
    _, a = quad_place()
    pairs = []
    for k, ref in ((1, one), (2, two), (3, three)):
        pairs += [(seconds_ref.at[k - 1], ref.at[0]), (across_ref.at[a ^ k], ref.at[1])]
    copied(pairs, buf, sems)


def swap(value, bits):
    return lax.ppermute(value, "space", [(s, s ^ bits) for s in range(8)])


def bring_frames(clip, behind):
    *quads, across = copying(depart_kernel, "depart", (clip,), (2, 2, 2, 4), 10)
    across = swap(across, 6)
    quads = [swap(quad, k) for k, quad in zip((1, 2, 3), quads)]
    first, seconds, kept = copying(own_kernel, "own", (clip,), (1, 3, 2), 6)
    few = pltpu.CompilerParams(vmem_limit_bytes=8 * MIB)
    (turned,) = copying(turn_kernel, "turn", (first, *quads, behind), (4,), 4, few)
    turned = swap(turned, 6)
    pairs = copying(spread_kernel, "spread", (seconds, across), (2, 2, 2), 6, few)
    started = pairs[0]
    pairs = [swap(pair, k) for k, pair in zip((1, 2, 3), pairs)]
    return (kept, across, turned, *quads, *pairs), started


def spatial_kernel(kept_ref, across_ref, turned_ref, *refs):
    quads, pairs, (_, out_ref, buf, res, sems, store_sems) = refs[:3], refs[3:6], refs[6:]
    g1, a = quad_place()
    first = [kept_ref.at[0]] + [ref.at[g1] for ref in quads] + [turned_ref.at[k] for k in range(4)]
    second = [kept_ref.at[1]] + [ref.at[0] for ref in pairs]
    second += [across_ref.at[a]] + [ref.at[1] for ref in pairs]
    loads = [
        [pltpu.make_async_copy(src, buf.at[f, i], sems.at[f, i]) for i, src in enumerate(sources)]
        for f, sources in enumerate((first, second))
    ]
    for f in range(2):
        for load in loads[f]:
            load.start()
    stores = [
        pltpu.make_async_copy(res.at[f], out_ref.at[:, f], store_sems.at[f]) for f in range(2)
    ]
    for f in range(2):
        for load in loads[f]:
            load.wait()
        for h in range(HEADS):
            q = buf[f, :, :, pl.ds(h * HD, HD)].reshape(PATCHES, HD)
            k = buf[f, :, :, pl.ds(FEATURES + h * HD, HD)].reshape(PATCHES, HD)
            v = buf[f, :, :, pl.ds(2 * FEATURES + h * HD, HD)].reshape(PATCHES, HD)
            s = nt(q, k)
            m = jnp.max(s, axis=-1, keepdims=True)
            e = jnp.exp2((s - m) * SCORE_LOG2)
            total = jnp.sum(e, axis=-1, keepdims=True)
            o = jnp.dot(e.astype(jnp.bfloat16), v, preferred_element_type=jnp.float32)
            o = (o * (1.0 / total)).astype(jnp.bfloat16)
            for i in range(8):
                at = owner(g1 if i < 4 else 1 - g1, a ^ (i & 3))
                res[f, at, :, pl.ds(h * HD, HD)] = o[i * LOCAL : (i + 1) * LOCAL]
        stores[f].start()
    for store in stores:
        store.wait()


def spatial_attention(pieces, behind):
    return pl.pallas_call(
        spatial_kernel,
        in_specs=[ANY] * (len(pieces) + 1),
        out_specs=ANY,
        out_shape=jax.ShapeDtypeStruct((8, 2, LOCAL, FEATURES), jnp.bfloat16),
        scratch_shapes=[
            pltpu.VMEM((2, 8) + ROW, jnp.bfloat16),
            pltpu.VMEM((2, 8, LOCAL, FEATURES), jnp.bfloat16),
            pltpu.SemaphoreType.DMA((2, 8)),
            pltpu.SemaphoreType.DMA((2,)),
        ],
        compiler_params=GRANT,
        cost_estimate=pl.CostEstimate(
            flops=8 * HEADS * PATCHES * PATCHES * HD,
            bytes_accessed=2 * PATCHES * 4 * FEATURES * 2,
            transcendentals=2 * HEADS * PATCHES * PATCHES,
        ),
        name="spatial_attention",
    )(*pieces, behind)


ROWS = FRAMES * 16


def time_kernel(tqk_ref, behind_ref, out_ref, mark_ref, tqk, weights, load_sem, sems):
    load = pltpu.make_async_copy(tqk_ref, tqk, load_sem)
    load.start()
    load.wait()
    mark_ref[...] = jnp.zeros_like(mark_ref)
    r = lax.broadcasted_iota(jnp.int32, (ROWS, ROWS), 0)
    c = lax.broadcasted_iota(jnp.int32, (ROWS, ROWS), 1)
    bias = jnp.where((r & 15) == (c & 15), 0.0, -1e30).astype(jnp.float32)
    stores = []
    for h in range(HEADS):
        for g in range(LOCAL // 16):
            part = pl.ds(g * 16, 16)
            q = tqk[:, part, pl.ds(h * HD, HD)].reshape(ROWS, HD)
            k = tqk[:, part, pl.ds(FEATURES + h * HD, HD)].reshape(ROWS, HD)
            s = nt(q, k) + bias
            m = jnp.max(s, axis=-1, keepdims=True)
            e = jnp.exp2((s - m) * SCORE_LOG2)
            total = jnp.sum(e, axis=-1, keepdims=True)
            weights[h, g] = (e * (1.0 / total)).astype(jnp.bfloat16)
        stores.append(pltpu.make_async_copy(weights.at[h], out_ref.at[h], sems.at[h]))
        stores[-1].start()
    for store in stores:
        store.wait()


def time_weights(temporal_qk, behind):
    return pl.pallas_call(
        time_kernel,
        in_specs=[ANY] * 2,
        out_specs=[ANY, VMEM],
        out_shape=[
            jax.ShapeDtypeStruct((HEADS, 2, ROWS, ROWS), jnp.bfloat16),
            jax.ShapeDtypeStruct((8, 128), jnp.float32),
        ],
        scratch_shapes=[
            pltpu.VMEM((FRAMES, LOCAL, 2 * FEATURES), jnp.bfloat16),
            pltpu.VMEM((HEADS, 2, ROWS, ROWS), jnp.bfloat16),
            pltpu.SemaphoreType.DMA,
            pltpu.SemaphoreType.DMA((HEADS,)),
        ],
        compiler_params=GRANT,
        cost_estimate=pl.CostEstimate(
            flops=4 * HEADS * ROWS * ROWS * HD,
            bytes_accessed=7_000_000,
            transcendentals=2 * HEADS * ROWS * ROWS,
        ),
        name="time_weights",
    )(temporal_qk, behind)


def flip(value, bit):
    return lax.ppermute(value, "dp", [(i, i ^ bit) for i in range(32)])


def join_kernel(*refs):
    refs[-1][0] = refs[0][...]
    refs[-1][1] = refs[1][...]


def flip_y(value):
    pairs = [(i * 8 + s, (i ^ 16) * 8 + (s ^ 1)) for i in range(32) for s in range(8)]
    return lax.ppermute(value, ("dp", "space"), pairs)


def doubled(value, other, *behind):
    both = pl.pallas_call(
        join_kernel,
        in_specs=[VMEM] * 2 + [ANY] * len(behind),
        out_specs=VMEM,
        out_shape=jax.ShapeDtypeStruct((2,) + value.shape, value.dtype),
        compiler_params=pltpu.CompilerParams(vmem_limit_bytes=8 * MIB),
        cost_estimate=pl.CostEstimate(flops=0, bytes_accessed=1_000_000, transcendentals=0),
        name="join",
    )(value, other, *behind)
    return both.reshape((-1,) + value.shape[1:])


def token_kernel(
    value, time_ref, proj_ref, mine_ref, other_ref,
    emb_ref, all_stats_ref, grad_ref, lens_ref,
    proj, mine, comb, video, grads, stats_ref, sems, grad_sems,
):
    proj_load = pltpu.make_async_copy(proj_ref, proj, sems.at[0])
    mine_load = pltpu.make_async_copy(mine_ref, mine, sems.at[1])
    proj_load.start()
    mine_load.start()
    for h in range(HEADS):
        cols = pl.ds(h * HD, HD)
        for g in range(LOCAL // 16):
            part = pl.ds(g * 16, 16)
            v = value[:, :, part, cols].reshape(ROWS, HD)
            o = jnp.dot(time_ref[h, g], v, preferred_element_type=jnp.float32)
            o = (v.astype(jnp.float32) + o).astype(jnp.bfloat16)
            comb[:, part, cols] = o.reshape(FRAMES, 16, HD)
    tokens = FRAMES * LOCAL
    proj_load.wait()
    projected = jnp.dot(
        comb[...].reshape(tokens, FEATURES), proj[...], preferred_element_type=jnp.float32
    )
    scale = lax.rsqrt(jnp.mean(projected * projected, axis=-1, keepdims=True) + 1e-06)
    emb = (projected * scale).astype(jnp.bfloat16)
    video[...] = emb.reshape(FRAMES, LOCAL, EMB)
    emb_store = pltpu.make_async_copy(video, emb_ref, sems.at[2])
    emb_store.start()
    mine_load.wait()

    eye = lax.broadcasted_iota(jnp.int32, (PADDED, 128), 0) == lax.broadcasted_iota(
        jnp.int32, (PADDED, 128), 1
    )
    y_hi, core, _, _, z = place()
    group = 8
    stores = []
    for i, (ref, c) in enumerate(((mine, core), (other_ref, 1 - core))):
        for m0 in range(0, CAPTIONS // 2, group):
            sim = nt(ref[pl.ds(m0, group)].reshape(group * PADDED, EMB), emb)
            top = jnp.max(sim, axis=-1, keepdims=True)
            w = jnp.exp2((sim - top) * SHARP_LOG2)
            total = jnp.sum(w, axis=-1, keepdims=True)
            product = jnp.dot(w.astype(jnp.bfloat16), emb, preferred_element_type=jnp.float32)
            slot = i * CAPTIONS // 2 + m0
            grads[pl.ds(slot, group)] = product.astype(jnp.bfloat16).reshape(group, PADDED, EMB)
            for j in range(group):
                m = m0 + j
                flips = (m >> 3 & 1) + (m >> 2 & 1) * 2 + (m >> 1 & 1) * 4
                at = (y_hi ^ (m & 1)) * 16 + (z ^ flips) * 2 + c
                stores.append(
                    pltpu.make_async_copy(
                        grads.at[slot + j], grad_ref.at[at], grad_sems.at[slot + j]
                    )
                )
                stores[-1].start()
                rng = slice(j * PADDED, (j + 1) * PADDED)
                top_row = jnp.sum(jnp.where(eye, top[rng], 0.0), axis=0, keepdims=True)
                total_row = jnp.sum(jnp.where(eye, total[rng], 0.0), axis=0, keepdims=True)
                stats_ref[0, pl.ds(at, 1), :] = top_row
                stats_ref[1, pl.ds(at, 1), :] = total_row
                lens_ref[pl.ds(at, 1), :] = ref[m, SLOTS : SLOTS + 1, :128].astype(jnp.float32)
    for k in range(8):
        all_stats_ref[k] = stats_ref[...]
    emb_store.wait()
    for store in stores:
        store.wait()


def token_part(spatial, time, proj_weight, mine, other):
    bf16 = jnp.bfloat16
    return pl.pallas_call(
        token_kernel,
        in_specs=[VMEM, VMEM, FAR_OFF, FAR_OFF, VMEM],
        out_specs=[FAR_OFF, VMEM, FAR_OFF, VMEM],
        out_shape=[
            pltpu.HBM((FRAMES, LOCAL, EMB), bf16),
            jax.ShapeDtypeStruct((8, 2, CAPTIONS, 128), jnp.float32),
            pltpu.HBM((CAPTIONS, PADDED, EMB), bf16),
            jax.ShapeDtypeStruct((CAPTIONS, 128), jnp.float32),
        ],
        scratch_shapes=[
            pltpu.VMEM((FEATURES, EMB), bf16),
            pltpu.VMEM((CAPTIONS // 2, PADDED, EMB), bf16),
            pltpu.VMEM((FRAMES, LOCAL, FEATURES), bf16),
            pltpu.VMEM((FRAMES, LOCAL, EMB), bf16),
            pltpu.VMEM((CAPTIONS, PADDED, EMB), bf16),
            pltpu.VMEM((2, CAPTIONS, 128), jnp.float32),
            pltpu.SemaphoreType.DMA((3,)),
            pltpu.SemaphoreType.DMA((CAPTIONS,)),
        ],
        compiler_params=GRANT,
        cost_estimate=pl.CostEstimate(
            flops=4_500_000_000, bytes_accessed=12_000_000, transcendentals=1_300_000
        ),
        name="token_part",
    )(spatial, time, held(proj_weight), held(mine), other)


def coef_kernel(
    pos_ref, stats_ref, lens_ref, grad_ref, send_ref, keep_ref, loss_ref, hold, grad, sems
):
    group = 8
    loads = [
        pltpu.make_async_copy(
            grad_ref.at[pl.ds(group * i, group)], grad.at[pl.ds(group * i, group)], sems.at[i]
        )
        for i in range(CAPTIONS // group)
    ]
    for load in loads:
        load.start()
    tops = stats_ref[:, 0]
    totals = stats_ref[:, 1]
    top = jnp.max(tops, axis=0)
    total = jnp.sum(totals * jnp.exp2((tops - top[None]) * SHARP_LOG2), axis=0)
    soft = top + jnp.log(total) / SHARPNESS
    slot = lax.broadcasted_iota(jnp.int32, (CAPTIONS, 128), 1).astype(jnp.float32)
    lens = lens_ref[...]
    live = slot < lens
    lens_col = lens[:, :1]
    score = jnp.sum(jnp.where(live, soft, 0.0), axis=-1, keepdims=True) / lens_col
    logits = LOGIT_SCALE * score
    peak = jnp.max(logits, axis=0, keepdims=True)
    log_total = peak + jnp.log(jnp.sum(jnp.exp(logits - peak), axis=0, keepdims=True))
    onehot = lax.broadcasted_iota(jnp.int32, (CAPTIONS, 1), 0) == pos_ref[0]
    loss_ref[...] = log_total - jnp.sum(jnp.where(onehot, logits, 0.0), axis=0, keepdims=True)
    grad_logit = LOGIT_SCALE * (jnp.exp(logits - log_total) - onehot.astype(jnp.float32))
    coef = jnp.where(live, grad_logit / lens_col, 0.0)
    mine = stats_ref[lax.axis_index("space"), 0]
    hold[...] = coef * jnp.exp2((mine - soft) * SHARP_LOG2)

    eye = lax.broadcasted_iota(jnp.int32, (PADDED, 128), 0) == lax.broadcasted_iota(
        jnp.int32, (PADDED, 128), 1
    )
    core = lax.axis_index("dp") & 1
    for m in range(CAPTIONS // 2):
        if 2 * m % group == 0:
            loads[2 * m // group].wait()
        for j, ref in ((2 * m + 1 - core, send_ref), (2 * m + core, keep_ref)):
            col = jnp.sum(jnp.where(eye, hold[pl.ds(j, 1), :], 0.0), axis=-1, keepdims=True)
            ref[m] = (grad[j].astype(jnp.float32) * col).astype(jnp.bfloat16)


def coef_part(pos, stats, lens, grad):
    half = jax.ShapeDtypeStruct((CAPTIONS // 2, PADDED, EMB), jnp.bfloat16)
    return pl.pallas_call(
        coef_kernel,
        in_specs=[SMEM, VMEM, VMEM, FAR_OFF],
        out_specs=[VMEM] * 3,
        out_shape=[half, half, jax.ShapeDtypeStruct((1, 1), jnp.float32)],
        scratch_shapes=[
            pltpu.VMEM((CAPTIONS, 128), jnp.float32),
            pltpu.VMEM((CAPTIONS, PADDED, EMB), jnp.bfloat16),
            pltpu.SemaphoreType.DMA((4,)),
        ],
        compiler_params=pltpu.CompilerParams(vmem_limit_bytes=12 * MIB),
        cost_estimate=pl.CostEstimate(
            flops=4_000_000, bytes_accessed=6_000_000, transcendentals=100_000
        ),
        name="coef_part",
    )(pos, stats, lens, held(grad))


def small_call(kernel, name, operands, out_shapes, specs=None):
    return pl.pallas_call(
        kernel,
        in_specs=specs or [VMEM] * len(operands),
        out_specs=[VMEM] * len(out_shapes),
        out_shape=[jax.ShapeDtypeStruct(s, d) for s, d in out_shapes],
        compiler_params=pltpu.CompilerParams(vmem_limit_bytes=16 * MIB),
        cost_estimate=pl.CostEstimate(flops=0, bytes_accessed=2_000_000, transcendentals=0),
        name=name,
    )(*operands)


def added(a, b):
    return (a.astype(jnp.float32) + b.astype(jnp.float32)).astype(jnp.bfloat16)


def first_sum_kernel(keep_ref, got_ref, a_keep, a_send, b_keep, b_send):
    x = lax.axis_index("space") >> 1
    plan = (
        (0, ((a_keep, 0, 0), (a_send, 0, 1), (a_send, 1, 2), (a_keep, 1, 3))),
        (8, ((b_keep, 0, 0), (b_keep, 1, 1), (b_send, 1, 2), (b_send, 0, 3))),
    )
    for start, parts in plan:
        for ref, at, flip in parts:
            cols = pl.ds(pl.multiple_of((x ^ flip) * 128, 128), 128)
            for m in range(8):
                ref[m, :, pl.ds(at * 128, 128)] = added(
                    keep_ref[start + m, :, cols], got_ref[start + m, :, cols]
                )


def second_sum_kernel(a_keep, a_got, b_keep, b_got, a_mine, a_send, b_mine, b_send):
    for keep, got, mine, send in ((a_keep, a_got, a_mine, a_send), (b_keep, b_got, b_mine, b_send)):
        mine[...] = added(keep[:, :, :128], got[:, :, :128])
        send[...] = added(keep[:, :, 128:], got[:, :, 128:])


def third_sum_kernel(a_mine, a_got, b_mine, b_got, out):
    out[pl.ds(0, 8)] = added(a_mine[...], a_got[...])
    out[pl.ds(8, 8)] = added(b_mine[...], b_got[...])


def owned_sum_kernel(parts, out):
    total = jnp.sum(parts[...].astype(jnp.float32), axis=0).astype(jnp.bfloat16)
    for k in range(8):
        out[k] = total


def last_sum_kernel(parts, out):
    for x in range(4):
        total = parts[2 * x].astype(jnp.float32) + parts[2 * x + 1].astype(jnp.float32)
        out[:, 0, pl.ds(x * 128, 128)] = total[:SLOTS]


def reduce_gradient(send, keep):
    bf16 = jnp.bfloat16
    one = [(s, s ^ 2) for s in range(8)]
    three = [(s, s ^ 6) for s in range(8)]
    got = lax.ppermute(send, "dp", [(i, i ^ 1) for i in range(32)])
    a_keep, a_send, b_keep, b_send = small_call(
        first_sum_kernel, "first_sum", (keep, got), [((8, PADDED, 256), bf16)] * 4
    )
    a_got = lax.ppermute(a_send, "space", one)
    b_got = lax.ppermute(b_send, "space", three)
    a_mine, a_send, b_mine, b_send = small_call(
        second_sum_kernel, "second_sum", (a_keep, a_got, b_keep, b_got),
        [((8, PADDED, 128), bf16)] * 4,
    )
    a_got = lax.ppermute(a_send, "space", three)
    b_got = lax.ppermute(b_send, "space", one)
    (parts,) = small_call(
        third_sum_kernel, "third_sum", (a_mine, a_got, b_mine, b_got), [((16, PADDED, 128), bf16)]
    )
    parts = lax.all_to_all(
        parts, "dp", split_axis=0, concat_axis=0, tiled=True,
        axis_index_groups=[[2 * m + c for m in range(16)] for c in range(2)],
    )
    (parts,) = small_call(owned_sum_kernel, "owned_sum", (parts,), [((8, PADDED, 128), bf16)])
    parts = lax.all_to_all(parts, "space", split_axis=0, concat_axis=0, tiled=True)
    (total,) = small_call(last_sum_kernel, "last_sum", (parts,), [((SLOTS, 1, EMB), jnp.float32)])
    return total.reshape(1, SLOTS, EMB)


def on_device(clip_qkv, temporal_qk, proj_weight, caption_tokens, caption_lens, positive):
    lens_row = jnp.broadcast_to(
        caption_lens.astype(jnp.bfloat16)[:, None, None], (1, PADDED - SLOTS, EMB)
    )
    caps = jnp.concatenate([caption_tokens, lens_row], axis=1)
    caps = doubled(caps, flip_y(caps))
    far = flip(caps, 8)
    pieces, started = bring_frames(clip_qkv[0], far)
    time, done = time_weights(temporal_qk[0], started)
    caps = doubled(caps, far, done)
    caps = doubled(caps, flip(caps, 4))
    caps = doubled(caps, flip(caps, 2))
    other = flip(caps, 1)
    attended = spatial_attention(pieces, done)
    spatial = lax.all_to_all(attended, "space", split_axis=0, concat_axis=0, tiled=True)
    video, stats, grad, lens = token_part(spatial, time, proj_weight, caps, other)
    stats = lax.all_to_all(stats, "space", split_axis=0, concat_axis=0, tiled=True)
    send, keep, loss = coef_part(positive, stats, lens, grad)
    caption_grad = reduce_gradient(send, keep)
    return video[None], caption_grad, loss.reshape(1)


def solution(mesh):
    return jax.shard_map(
        on_device,
        mesh=mesh,
        in_specs=(
            P("dp", None, "space", None),
            P("dp", None, "space", None),
            P(),
            P("dp", None, None),
            P("dp"),
            P("dp"),
        ),
        out_specs=(P("dp", None, "space", None), P("dp", None, None), P("dp")),
        check_vma=False,
    )
```

```python
import functools
import math

import jax
import jax.numpy as jnp
from jax import lax
from jax.experimental import pallas as pl
from jax.experimental.pallas import tpu as pltpu
from jax.sharding import PartitionSpec as P

HEADS = 13
HD = 128
FEATURES = HEADS * HD
EMB = 512
FRAMES = 16
PATCHES = 256
LOCAL = 32
SLOTS = 77
PADDED = 80
CAPTIONS = 32
SHARPNESS = 4.0
LOGIT_SCALE = 10.0
LOG2E = math.log2(math.e)
SCORE_LOG2 = HD ** (-0.5) * LOG2E
SHARP_LOG2 = SHARPNESS * LOG2E
MIB = 1 << 20
GRANT = pltpu.CompilerParams(vmem_limit_bytes=24 * MIB)
VMEM = pl.BlockSpec(memory_space=pltpu.VMEM)
SMEM = pl.BlockSpec(memory_space=pltpu.SMEM)

FAR_OFF = pl.BlockSpec(memory_space=pltpu.HBM)
ANY = pl.BlockSpec(memory_space=pl.ANY)


def owner(g1, a):
    return (g1 * 2 + ((a >> 1) ^ g1)) * 2 + (a & 1)


def place():
    dp, space = lax.axis_index("dp"), lax.axis_index("space")
    return dp >> 4, dp & 1, space >> 1, space & 1, (dp >> 1) & 7


def quad_place():
    _, _, x, y, _ = place()
    return x >> 1, ((x >> 1) ^ (x & 1)) * 2 + y


def held(value):
    return pltpu.with_memory_space_constraint(value, pltpu.HBM)


def nt(a, b):
    return lax.dot_general(a, b, (((1,), (1,)), ((), ())), preferred_element_type=jnp.float32)


SPLIT = 7


ROW = (LOCAL, 3 * FEATURES)
FULL = pltpu.CompilerParams(vmem_limit_bytes=60 * MIB)


def copied(pairs, buf, sems):
    loads = [
        pltpu.make_async_copy(src, buf.at[i], sems.at[0, i]) for i, (src, _) in enumerate(pairs)
    ]
    stores = [
        pltpu.make_async_copy(buf.at[i], dst, sems.at[1, i]) for i, (_, dst) in enumerate(pairs)
    ]
    for load in loads:
        load.start()
    for load, store in zip(loads, stores):
        load.wait()
        store.start()
    for store in stores:
        store.wait()


def copying(kernel, name, operands, shapes, count, params=FULL):
    return pl.pallas_call(
        kernel,
        in_specs=[ANY] * len(operands),
        out_specs=[ANY] * len(shapes),
        out_shape=[jax.ShapeDtypeStruct((n,) + ROW, jnp.bfloat16) for n in shapes],
        scratch_shapes=[
            pltpu.VMEM((count,) + ROW, jnp.bfloat16),
            pltpu.SemaphoreType.DMA((2, count)),
        ],
        compiler_params=params,
        cost_estimate=pl.CostEstimate(flops=0, bytes_accessed=6_000_000, transcendentals=0),
        name=name,
    )(*operands)


def depart_kernel(clip_ref, one, two, three, across_ref, buf, sems):
    g1, a = quad_place()
    pairs = [
        (clip_ref.at[2 * owner(g, a ^ k)], ref.at[g])
        for k, ref in ((1, one), (2, two), (3, three))
        for g in range(2)
    ]
    pairs += [(clip_ref.at[2 * owner(1 - g1, b) + 1], across_ref.at[b]) for b in range(4)]
    copied(pairs, buf, sems)


def own_kernel(clip_ref, first, seconds, kept, buf, sems):
    g1, a = quad_place()
    pairs = [(clip_ref.at[2 * owner(1 - g1, a)], first.at[0])]
    pairs += [(clip_ref.at[2 * owner(g1, a ^ k) + 1], seconds.at[k - 1]) for k in (1, 2, 3)]
    pairs += [(clip_ref.at[2 * owner(g1, a) + f], kept.at[f]) for f in range(2)]
    copied(pairs, buf, sems)


def turn_kernel(first_ref, one, two, three, behind_ref, started_ref, out_ref, buf, sems):
    g1, _ = quad_place()
    pairs = [(first_ref.at[0], out_ref.at[0])]
    pairs += [(ref.at[1 - g1], out_ref.at[k]) for k, ref in ((1, one), (2, two), (3, three))]
    copied(pairs, buf, sems)


def spread_kernel(seconds_ref, across_ref, one, two, three, buf, sems):
    _, a = quad_place()
    pairs = []
    for k, ref in ((1, one), (2, two), (3, three)):
        pairs += [(seconds_ref.at[k - 1], ref.at[0]), (across_ref.at[a ^ k], ref.at[1])]
    copied(pairs, buf, sems)


def swap(value, bits):
    return lax.ppermute(value, "space", [(s, s ^ bits) for s in range(8)])


def bring_frames(clip, behind):
    *quads, across = copying(depart_kernel, "depart", (clip,), (2, 2, 2, 4), 10)
    across = swap(across, 6)
    quads = [swap(quad, k) for k, quad in zip((1, 2, 3), quads)]
    first, seconds, kept = copying(own_kernel, "own", (clip,), (1, 3, 2), 6)
    few = pltpu.CompilerParams(vmem_limit_bytes=8 * MIB)
    pairs = copying(spread_kernel, "spread", (seconds, across), (2, 2, 2), 6, few)
    started = pairs[0]
    pairs = [swap(pair, k) for k, pair in zip((1, 2, 3), pairs)]
    (turned,) = copying(turn_kernel, "turn", (first, *quads, behind, started), (4,), 4, few)
    turned = swap(turned, 6)
    return (kept, across, turned, *quads, *pairs), started


def spatial_kernel(kept_ref, across_ref, turned_ref, *refs):
    quads, pairs, (_, out_ref, buf, res, sems, store_sems) = refs[:3], refs[3:6], refs[6:]
    g1, a = quad_place()
    first = [kept_ref.at[0]] + [ref.at[g1] for ref in quads] + [turned_ref.at[k] for k in range(4)]
    second = [kept_ref.at[1]] + [ref.at[0] for ref in pairs]
    second += [across_ref.at[a]] + [ref.at[1] for ref in pairs]
    loads = [
        [pltpu.make_async_copy(src, buf.at[f, i], sems.at[f, i]) for i, src in enumerate(sources)]
        for f, sources in enumerate((first, second))
    ]
    for f in range(2):
        for load in loads[f]:
            load.start()
    stores = [
        pltpu.make_async_copy(res.at[f], out_ref.at[:, f], store_sems.at[f]) for f in range(2)
    ]
    for f in range(2):
        for load in loads[f]:
            load.wait()
        for h in range(HEADS):
            q = buf[f, :, :, pl.ds(h * HD, HD)].reshape(PATCHES, HD)
            k = buf[f, :, :, pl.ds(FEATURES + h * HD, HD)].reshape(PATCHES, HD)
            v = buf[f, :, :, pl.ds(2 * FEATURES + h * HD, HD)].reshape(PATCHES, HD)
            s = nt(q, k)
            m = jnp.max(s, axis=-1, keepdims=True)
            e = jnp.exp2((s - m) * SCORE_LOG2)
            total = jnp.sum(e, axis=-1, keepdims=True)
            o = jnp.dot(e.astype(jnp.bfloat16), v, preferred_element_type=jnp.float32)
            o = (o * (1.0 / total)).astype(jnp.bfloat16)
            for i in range(8):
                at = owner(g1 if i < 4 else 1 - g1, a ^ (i & 3))
                res[f, at, :, pl.ds(h * HD, HD)] = o[i * LOCAL : (i + 1) * LOCAL]
        stores[f].start()
    for store in stores:
        store.wait()


def spatial_attention(pieces, behind):
    return pl.pallas_call(
        spatial_kernel,
        in_specs=[ANY] * (len(pieces) + 1),
        out_specs=ANY,
        out_shape=jax.ShapeDtypeStruct((8, 2, LOCAL, FEATURES), jnp.bfloat16),
        scratch_shapes=[
            pltpu.VMEM((2, 8) + ROW, jnp.bfloat16),
            pltpu.VMEM((2, 8, LOCAL, FEATURES), jnp.bfloat16),
            pltpu.SemaphoreType.DMA((2, 8)),
            pltpu.SemaphoreType.DMA((2,)),
        ],
        compiler_params=GRANT,
        cost_estimate=pl.CostEstimate(
            flops=8 * HEADS * PATCHES * PATCHES * HD,
            bytes_accessed=2 * PATCHES * 4 * FEATURES * 2,
            transcendentals=2 * HEADS * PATCHES * PATCHES,
        ),
        name="spatial_attention",
    )(*pieces, behind)


ROWS = FRAMES * 16


def time_kernel(tqk_ref, behind_ref, out_ref, mark_ref, tqk, weights, load_sem, sems):
    load = pltpu.make_async_copy(tqk_ref, tqk, load_sem)
    load.start()
    load.wait()
    mark_ref[...] = jnp.zeros_like(mark_ref)
    r = lax.broadcasted_iota(jnp.int32, (ROWS, ROWS), 0)
    c = lax.broadcasted_iota(jnp.int32, (ROWS, ROWS), 1)
    bias = jnp.where((r & 15) == (c & 15), 0.0, -1e30).astype(jnp.float32)
    stores = []
    for h in range(HEADS):
        for g in range(LOCAL // 16):
            part = pl.ds(g * 16, 16)
            q = tqk[:, part, pl.ds(h * HD, HD)].reshape(ROWS, HD)
            k = tqk[:, part, pl.ds(FEATURES + h * HD, HD)].reshape(ROWS, HD)
            s = nt(q, k) + bias
            m = jnp.max(s, axis=-1, keepdims=True)
            e = jnp.exp2((s - m) * SCORE_LOG2)
            total = jnp.sum(e, axis=-1, keepdims=True)
            weights[h, g] = (e * (1.0 / total)).astype(jnp.bfloat16)
        stores.append(pltpu.make_async_copy(weights.at[h], out_ref.at[h], sems.at[h]))
        stores[-1].start()
    for store in stores:
        store.wait()


def time_weights(temporal_qk, behind):
    return pl.pallas_call(
        time_kernel,
        in_specs=[ANY] * 2,
        out_specs=[ANY, VMEM],
        out_shape=[
            jax.ShapeDtypeStruct((HEADS, 2, ROWS, ROWS), jnp.bfloat16),
            jax.ShapeDtypeStruct((8, 128), jnp.float32),
        ],
        scratch_shapes=[
            pltpu.VMEM((FRAMES, LOCAL, 2 * FEATURES), jnp.bfloat16),
            pltpu.VMEM((HEADS, 2, ROWS, ROWS), jnp.bfloat16),
            pltpu.SemaphoreType.DMA,
            pltpu.SemaphoreType.DMA((HEADS,)),
        ],
        compiler_params=GRANT,
        cost_estimate=pl.CostEstimate(
            flops=4 * HEADS * ROWS * ROWS * HD,
            bytes_accessed=7_000_000,
            transcendentals=2 * HEADS * ROWS * ROWS,
        ),
        name="time_weights",
    )(temporal_qk, behind)


def flip(value, bit):
    return lax.ppermute(value, "dp", [(i, i ^ bit) for i in range(32)])


def join_kernel(*refs):
    refs[-1][0] = refs[0][...]
    refs[-1][1] = refs[1][...]


def flip_y(value):
    pairs = [(i * 8 + s, (i ^ 16) * 8 + (s ^ 1)) for i in range(32) for s in range(8)]
    return lax.ppermute(value, ("dp", "space"), pairs)


def doubled(value, other, *behind):
    both = pl.pallas_call(
        join_kernel,
        in_specs=[VMEM] * 2 + [ANY] * len(behind),
        out_specs=VMEM,
        out_shape=jax.ShapeDtypeStruct((2,) + value.shape, value.dtype),
        compiler_params=pltpu.CompilerParams(vmem_limit_bytes=8 * MIB),
        cost_estimate=pl.CostEstimate(flops=0, bytes_accessed=1_000_000, transcendentals=0),
        name="join",
    )(value, other, *behind)
    return both.reshape((-1,) + value.shape[1:])


def token_kernel(
    value, time_ref, proj_ref, mine_ref, other_ref,
    emb_ref, all_stats_ref, grad_ref, lens_ref,
    proj, mine, comb, video, grads, stats_ref, sems, grad_sems,
):
    proj_load = pltpu.make_async_copy(proj_ref, proj, sems.at[0])
    mine_load = pltpu.make_async_copy(mine_ref, mine, sems.at[1])
    proj_load.start()
    mine_load.start()
    for h in range(HEADS):
        cols = pl.ds(h * HD, HD)
        for g in range(LOCAL // 16):
            part = pl.ds(g * 16, 16)
            v = value[:, :, part, cols].reshape(ROWS, HD)
            o = jnp.dot(time_ref[h, g], v, preferred_element_type=jnp.float32)
            o = (v.astype(jnp.float32) + o).astype(jnp.bfloat16)
            comb[:, part, cols] = o.reshape(FRAMES, 16, HD)
    tokens = FRAMES * LOCAL
    proj_load.wait()
    projected = jnp.dot(
        comb[...].reshape(tokens, FEATURES), proj[...], preferred_element_type=jnp.float32
    )
    scale = lax.rsqrt(jnp.mean(projected * projected, axis=-1, keepdims=True) + 1e-06)
    emb = (projected * scale).astype(jnp.bfloat16)
    video[...] = emb.reshape(FRAMES, LOCAL, EMB)
    emb_store = pltpu.make_async_copy(video, emb_ref, sems.at[2])
    emb_store.start()
    mine_load.wait()

    eye = lax.broadcasted_iota(jnp.int32, (PADDED, 128), 0) == lax.broadcasted_iota(
        jnp.int32, (PADDED, 128), 1
    )
    y_hi, core, _, _, z = place()
    group = 8
    stores = []
    for i, (ref, c) in enumerate(((mine, core), (other_ref, 1 - core))):
        for m0 in range(0, CAPTIONS // 2, group):
            sim = nt(ref[pl.ds(m0, group)].reshape(group * PADDED, EMB), emb)
            top = jnp.max(sim, axis=-1, keepdims=True)
            w = jnp.exp2((sim - top) * SHARP_LOG2)
            total = jnp.sum(w, axis=-1, keepdims=True)
            product = jnp.dot(w.astype(jnp.bfloat16), emb, preferred_element_type=jnp.float32)
            slot = i * CAPTIONS // 2 + m0
            grads[pl.ds(slot, group)] = product.astype(jnp.bfloat16).reshape(group, PADDED, EMB)
            for j in range(group):
                m = m0 + j
                flips = (m >> 3 & 1) + (m >> 2 & 1) * 2 + (m >> 1 & 1) * 4
                at = (y_hi ^ (m & 1)) * 16 + (z ^ flips) * 2 + c
                stores.append(
                    pltpu.make_async_copy(
                        grads.at[slot + j], grad_ref.at[at], grad_sems.at[slot + j]
                    )
                )
                stores[-1].start()
                rng = slice(j * PADDED, (j + 1) * PADDED)
                top_row = jnp.sum(jnp.where(eye, top[rng], 0.0), axis=0, keepdims=True)
                total_row = jnp.sum(jnp.where(eye, total[rng], 0.0), axis=0, keepdims=True)
                stats_ref[0, pl.ds(at, 1), :] = top_row
                stats_ref[1, pl.ds(at, 1), :] = total_row
                lens_ref[pl.ds(at, 1), :] = ref[m, SLOTS : SLOTS + 1, :128].astype(jnp.float32)
    for k in range(8):
        all_stats_ref[k] = stats_ref[...]
    emb_store.wait()
    for store in stores:
        store.wait()


def token_part(spatial, time, proj_weight, mine, other):
    bf16 = jnp.bfloat16
    return pl.pallas_call(
        token_kernel,
        in_specs=[VMEM, VMEM, FAR_OFF, FAR_OFF, VMEM],
        out_specs=[FAR_OFF, VMEM, FAR_OFF, VMEM],
        out_shape=[
            pltpu.HBM((FRAMES, LOCAL, EMB), bf16),
            jax.ShapeDtypeStruct((8, 2, CAPTIONS, 128), jnp.float32),
            pltpu.HBM((CAPTIONS, PADDED, EMB), bf16),
            jax.ShapeDtypeStruct((CAPTIONS, 128), jnp.float32),
        ],
        scratch_shapes=[
            pltpu.VMEM((FEATURES, EMB), bf16),
            pltpu.VMEM((CAPTIONS // 2, PADDED, EMB), bf16),
            pltpu.VMEM((FRAMES, LOCAL, FEATURES), bf16),
            pltpu.VMEM((FRAMES, LOCAL, EMB), bf16),
            pltpu.VMEM((CAPTIONS, PADDED, EMB), bf16),
            pltpu.VMEM((2, CAPTIONS, 128), jnp.float32),
            pltpu.SemaphoreType.DMA((3,)),
            pltpu.SemaphoreType.DMA((CAPTIONS,)),
        ],
        compiler_params=GRANT,
        cost_estimate=pl.CostEstimate(
            flops=4_500_000_000, bytes_accessed=12_000_000, transcendentals=1_300_000
        ),
        name="token_part",
    )(spatial, time, held(proj_weight), held(mine), other)


def coef_kernel(
    pos_ref, stats_ref, lens_ref, grad_ref, send_ref, keep_ref, loss_ref, hold, grad, sems
):
    group = 8
    loads = [
        pltpu.make_async_copy(
            grad_ref.at[pl.ds(group * i, group)], grad.at[pl.ds(group * i, group)], sems.at[i]
        )
        for i in range(CAPTIONS // group)
    ]
    for load in loads:
        load.start()
    tops = stats_ref[:, 0]
    totals = stats_ref[:, 1]
    top = jnp.max(tops, axis=0)
    total = jnp.sum(totals * jnp.exp2((tops - top[None]) * SHARP_LOG2), axis=0)
    soft = top + jnp.log(total) / SHARPNESS
    slot = lax.broadcasted_iota(jnp.int32, (CAPTIONS, 128), 1).astype(jnp.float32)
    lens = lens_ref[...]
    live = slot < lens
    lens_col = lens[:, :1]
    score = jnp.sum(jnp.where(live, soft, 0.0), axis=-1, keepdims=True) / lens_col
    logits = LOGIT_SCALE * score
    peak = jnp.max(logits, axis=0, keepdims=True)
    log_total = peak + jnp.log(jnp.sum(jnp.exp(logits - peak), axis=0, keepdims=True))
    onehot = lax.broadcasted_iota(jnp.int32, (CAPTIONS, 1), 0) == pos_ref[0]
    loss_ref[...] = log_total - jnp.sum(jnp.where(onehot, logits, 0.0), axis=0, keepdims=True)
    grad_logit = LOGIT_SCALE * (jnp.exp(logits - log_total) - onehot.astype(jnp.float32))
    coef = jnp.where(live, grad_logit / lens_col, 0.0)
    mine = stats_ref[lax.axis_index("space"), 0]
    hold[...] = coef * jnp.exp2((mine - soft) * SHARP_LOG2)

    eye = lax.broadcasted_iota(jnp.int32, (PADDED, 128), 0) == lax.broadcasted_iota(
        jnp.int32, (PADDED, 128), 1
    )
    core = lax.axis_index("dp") & 1
    for m in range(CAPTIONS // 2):
        if 2 * m % group == 0:
            loads[2 * m // group].wait()
        for j, ref in ((2 * m + 1 - core, send_ref), (2 * m + core, keep_ref)):
            col = jnp.sum(jnp.where(eye, hold[pl.ds(j, 1), :], 0.0), axis=-1, keepdims=True)
            ref[m] = (grad[j].astype(jnp.float32) * col).astype(jnp.bfloat16)


def coef_part(pos, stats, lens, grad):
    half = jax.ShapeDtypeStruct((CAPTIONS // 2, PADDED, EMB), jnp.bfloat16)
    return pl.pallas_call(
        coef_kernel,
        in_specs=[SMEM, VMEM, VMEM, FAR_OFF],
        out_specs=[VMEM] * 3,
        out_shape=[half, half, jax.ShapeDtypeStruct((1, 1), jnp.float32)],
        scratch_shapes=[
            pltpu.VMEM((CAPTIONS, 128), jnp.float32),
            pltpu.VMEM((CAPTIONS, PADDED, EMB), jnp.bfloat16),
            pltpu.SemaphoreType.DMA((4,)),
        ],
        compiler_params=pltpu.CompilerParams(vmem_limit_bytes=12 * MIB),
        cost_estimate=pl.CostEstimate(
            flops=4_000_000, bytes_accessed=6_000_000, transcendentals=100_000
        ),
        name="coef_part",
    )(pos, stats, lens, held(grad))


def small_call(kernel, name, operands, out_shapes, specs=None):
    return pl.pallas_call(
        kernel,
        in_specs=specs or [VMEM] * len(operands),
        out_specs=[VMEM] * len(out_shapes),
        out_shape=[jax.ShapeDtypeStruct(s, d) for s, d in out_shapes],
        compiler_params=pltpu.CompilerParams(vmem_limit_bytes=16 * MIB),
        cost_estimate=pl.CostEstimate(flops=0, bytes_accessed=2_000_000, transcendentals=0),
        name=name,
    )(*operands)


def added(a, b):
    return (a.astype(jnp.float32) + b.astype(jnp.float32)).astype(jnp.bfloat16)


def first_sum_kernel(keep_ref, got_ref, a_keep, a_send, b_keep, b_send):
    x = lax.axis_index("space") >> 1
    plan = (
        (0, ((a_keep, 0, 0), (a_send, 0, 1), (a_send, 1, 2), (a_keep, 1, 3))),
        (8, ((b_keep, 0, 0), (b_keep, 1, 1), (b_send, 1, 2), (b_send, 0, 3))),
    )
    for start, parts in plan:
        for ref, at, flip in parts:
            cols = pl.ds(pl.multiple_of((x ^ flip) * 128, 128), 128)
            for m in range(8):
                ref[m, :, pl.ds(at * 128, 128)] = added(
                    keep_ref[start + m, :, cols], got_ref[start + m, :, cols]
                )


def second_sum_kernel(a_keep, a_got, b_keep, b_got, a_mine, a_send, b_mine, b_send):
    for keep, got, mine, send in ((a_keep, a_got, a_mine, a_send), (b_keep, b_got, b_mine, b_send)):
        mine[...] = added(keep[:, :, :128], got[:, :, :128])
        send[...] = added(keep[:, :, 128:], got[:, :, 128:])


def third_sum_kernel(a_mine, a_got, b_mine, b_got, out):
    out[pl.ds(0, 8)] = added(a_mine[...], a_got[...])
    out[pl.ds(8, 8)] = added(b_mine[...], b_got[...])


def owned_sum_kernel(parts, out):
    total = jnp.sum(parts[...].astype(jnp.float32), axis=0).astype(jnp.bfloat16)
    for k in range(8):
        out[k] = total


def last_sum_kernel(parts, out):
    for x in range(4):
        total = parts[2 * x].astype(jnp.float32) + parts[2 * x + 1].astype(jnp.float32)
        out[:, 0, pl.ds(x * 128, 128)] = total[:SLOTS]


def reduce_gradient(send, keep):
    bf16 = jnp.bfloat16
    one = [(s, s ^ 2) for s in range(8)]
    three = [(s, s ^ 6) for s in range(8)]
    got = lax.ppermute(send, "dp", [(i, i ^ 1) for i in range(32)])
    a_keep, a_send, b_keep, b_send = small_call(
        first_sum_kernel, "first_sum", (keep, got), [((8, PADDED, 256), bf16)] * 4
    )
    a_got = lax.ppermute(a_send, "space", one)
    b_got = lax.ppermute(b_send, "space", three)
    a_mine, a_send, b_mine, b_send = small_call(
        second_sum_kernel, "second_sum", (a_keep, a_got, b_keep, b_got),
        [((8, PADDED, 128), bf16)] * 4,
    )
    a_got = lax.ppermute(a_send, "space", three)
    b_got = lax.ppermute(b_send, "space", one)
    (parts,) = small_call(
        third_sum_kernel, "third_sum", (a_mine, a_got, b_mine, b_got), [((16, PADDED, 128), bf16)]
    )
    parts = lax.all_to_all(
        parts, "dp", split_axis=0, concat_axis=0, tiled=True,
        axis_index_groups=[[2 * m + c for m in range(16)] for c in range(2)],
    )
    (parts,) = small_call(owned_sum_kernel, "owned_sum", (parts,), [((8, PADDED, 128), bf16)])
    parts = lax.all_to_all(parts, "space", split_axis=0, concat_axis=0, tiled=True)
    (total,) = small_call(last_sum_kernel, "last_sum", (parts,), [((SLOTS, 1, EMB), jnp.float32)])
    return total.reshape(1, SLOTS, EMB)


def on_device(clip_qkv, temporal_qk, proj_weight, caption_tokens, caption_lens, positive):
    lens_row = jnp.broadcast_to(
        caption_lens.astype(jnp.bfloat16)[:, None, None], (1, PADDED - SLOTS, EMB)
    )
    caps = jnp.concatenate([caption_tokens, lens_row], axis=1)
    caps = doubled(caps, flip_y(caps))
    far = flip(caps, 8)
    pieces, started = bring_frames(clip_qkv[0], far)
    time, done = time_weights(temporal_qk[0], started)
    caps = doubled(caps, far)
    attended = spatial_attention(pieces, done)
    caps = doubled(caps, flip(caps, 4), attended)
    caps = doubled(caps, flip(caps, 2))
    other = flip(caps, 1)
    spatial = lax.all_to_all(attended, "space", split_axis=0, concat_axis=0, tiled=True)
    video, stats, grad, lens = token_part(spatial, time, proj_weight, caps, other)
    stats = lax.all_to_all(stats, "space", split_axis=0, concat_axis=0, tiled=True)
    send, keep, loss = coef_part(positive, stats, lens, grad)
    caption_grad = reduce_gradient(send, keep)
    return video[None], caption_grad, loss.reshape(1)


def solution(mesh):
    return jax.shard_map(
        on_device,
        mesh=mesh,
        in_specs=(
            P("dp", None, "space", None),
            P("dp", None, "space", None),
            P(),
            P("dp", None, None),
            P("dp"),
            P("dp"),
        ),
        out_specs=(P("dp", None, "space", None), P("dp", None, None), P("dp")),
        check_vma=False,
    )
```

```python
import functools
import math

import jax
import jax.numpy as jnp
from jax import lax
from jax.experimental import pallas as pl
from jax.experimental.pallas import tpu as pltpu
from jax.sharding import PartitionSpec as P

HEADS = 13
HD = 128
FEATURES = HEADS * HD
EMB = 512
FRAMES = 16
PATCHES = 256
LOCAL = 32
SLOTS = 77
PADDED = 80
CAPTIONS = 32
SHARPNESS = 4.0
LOGIT_SCALE = 10.0
LOG2E = math.log2(math.e)
SCORE_LOG2 = HD ** (-0.5) * LOG2E
SHARP_LOG2 = SHARPNESS * LOG2E
MIB = 1 << 20
GRANT = pltpu.CompilerParams(vmem_limit_bytes=24 * MIB)
VMEM = pl.BlockSpec(memory_space=pltpu.VMEM)
SMEM = pl.BlockSpec(memory_space=pltpu.SMEM)

FAR_OFF = pl.BlockSpec(memory_space=pltpu.HBM)
ANY = pl.BlockSpec(memory_space=pl.ANY)


def owner(g1, a):
    return (g1 * 2 + ((a >> 1) ^ g1)) * 2 + (a & 1)


def place():
    dp, space = lax.axis_index("dp"), lax.axis_index("space")
    return dp >> 4, dp & 1, space >> 1, space & 1, (dp >> 1) & 7


def quad_place():
    _, _, x, y, _ = place()
    return x >> 1, ((x >> 1) ^ (x & 1)) * 2 + y


def held(value):
    return pltpu.with_memory_space_constraint(value, pltpu.HBM)


def nt(a, b):
    return lax.dot_general(a, b, (((1,), (1,)), ((), ())), preferred_element_type=jnp.float32)


SPLIT = 7


ROW = (LOCAL, 3 * FEATURES)
FULL = pltpu.CompilerParams(vmem_limit_bytes=60 * MIB)


def copied(pairs, buf, sems):
    loads = [
        pltpu.make_async_copy(src, buf.at[i], sems.at[0, i]) for i, (src, _) in enumerate(pairs)
    ]
    stores = [
        pltpu.make_async_copy(buf.at[i], dst, sems.at[1, i]) for i, (_, dst) in enumerate(pairs)
    ]
    for load in loads:
        load.start()
    for load, store in zip(loads, stores):
        load.wait()
        store.start()
    for store in stores:
        store.wait()


def copying(kernel, name, operands, shapes, count, params=FULL):
    return pl.pallas_call(
        kernel,
        in_specs=[ANY] * len(operands),
        out_specs=[ANY] * len(shapes),
        out_shape=[jax.ShapeDtypeStruct((n,) + ROW, jnp.bfloat16) for n in shapes],
        scratch_shapes=[
            pltpu.VMEM((count,) + ROW, jnp.bfloat16),
            pltpu.SemaphoreType.DMA((2, count)),
        ],
        compiler_params=params,
        cost_estimate=pl.CostEstimate(flops=0, bytes_accessed=6_000_000, transcendentals=0),
        name=name,
    )(*operands)


def depart_kernel(clip_ref, one, two, three, across_ref, buf, sems):
    g1, a = quad_place()
    pairs = [
        (clip_ref.at[2 * owner(g, a ^ k)], ref.at[g])
        for k, ref in ((1, one), (2, two), (3, three))
        for g in range(2)
    ]
    pairs += [(clip_ref.at[2 * owner(1 - g1, b) + 1], across_ref.at[b]) for b in range(4)]
    copied(pairs, buf, sems)


def own_kernel(clip_ref, first, seconds, kept, buf, sems):
    g1, a = quad_place()
    pairs = [(clip_ref.at[2 * owner(1 - g1, a)], first.at[0])]
    pairs += [(clip_ref.at[2 * owner(g1, a ^ k) + 1], seconds.at[k - 1]) for k in (1, 2, 3)]
    pairs += [(clip_ref.at[2 * owner(g1, a) + f], kept.at[f]) for f in range(2)]
    copied(pairs, buf, sems)


def turn_kernel(first_ref, one, two, three, behind_ref, started_ref, out_ref, buf, sems):
    g1, _ = quad_place()
    pairs = [(first_ref.at[0], out_ref.at[0])]
    pairs += [(ref.at[1 - g1], out_ref.at[k]) for k, ref in ((1, one), (2, two), (3, three))]
    copied(pairs, buf, sems)


def spread_kernel(seconds_ref, across_ref, one, two, three, buf, sems):
    _, a = quad_place()
    pairs = []
    for k, ref in ((1, one), (2, two), (3, three)):
        pairs += [(seconds_ref.at[k - 1], ref.at[0]), (across_ref.at[a ^ k], ref.at[1])]
    copied(pairs, buf, sems)


def swap(value, bits):
    return lax.ppermute(value, "space", [(s, s ^ bits) for s in range(8)])


def bring_frames(clip, behind):
    *quads, across = copying(depart_kernel, "depart", (clip,), (2, 2, 2, 4), 10)
    across = swap(across, 6)
    quads = [swap(quad, k) for k, quad in zip((1, 2, 3), quads)]
    first, seconds, kept = copying(own_kernel, "own", (clip,), (1, 3, 2), 6)
    few = pltpu.CompilerParams(vmem_limit_bytes=8 * MIB)
    pairs = copying(spread_kernel, "spread", (seconds, across), (2, 2, 2), 6, few)
    started = pairs[0]
    pairs = [swap(pair, k) for k, pair in zip((1, 2, 3), pairs)]
    (turned,) = copying(turn_kernel, "turn", (first, *quads, behind, started), (4,), 4, few)
    turned = swap(turned, 6)
    return (kept, across, turned, *quads, *pairs), started


def spatial_kernel(kept_ref, across_ref, turned_ref, *refs):
    quads, pairs, (_, out_ref, buf, res, sems, store_sems) = refs[:3], refs[3:6], refs[6:]
    g1, a = quad_place()
    first = [kept_ref.at[0]] + [ref.at[g1] for ref in quads] + [turned_ref.at[k] for k in range(4)]
    second = [kept_ref.at[1]] + [ref.at[0] for ref in pairs]
    second += [across_ref.at[a]] + [ref.at[1] for ref in pairs]
    loads = [
        [pltpu.make_async_copy(src, buf.at[f, i], sems.at[f, i]) for i, src in enumerate(sources)]
        for f, sources in enumerate((first, second))
    ]
    for f in range(2):
        for load in loads[f]:
            load.start()
    stores = [
        pltpu.make_async_copy(res.at[f], out_ref.at[:, f], store_sems.at[f]) for f in range(2)
    ]
    for f in range(2):
        for load in loads[f]:
            load.wait()
        for h in range(HEADS):
            q = buf[f, :, :, pl.ds(h * HD, HD)].reshape(PATCHES, HD)
            k = buf[f, :, :, pl.ds(FEATURES + h * HD, HD)].reshape(PATCHES, HD)
            v = buf[f, :, :, pl.ds(2 * FEATURES + h * HD, HD)].reshape(PATCHES, HD)
            s = nt(q, k)
            m = jnp.max(s, axis=-1, keepdims=True)
            e = jnp.exp2((s - m) * SCORE_LOG2)
            total = jnp.sum(e, axis=-1, keepdims=True)
            o = jnp.dot(e.astype(jnp.bfloat16), v, preferred_element_type=jnp.float32)
            o = (o * (1.0 / total)).astype(jnp.bfloat16)
            for i in range(8):
                at = owner(g1 if i < 4 else 1 - g1, a ^ (i & 3))
                res[f, at, :, pl.ds(h * HD, HD)] = o[i * LOCAL : (i + 1) * LOCAL]
        stores[f].start()
    for store in stores:
        store.wait()


def spatial_attention(pieces, behind):
    return pl.pallas_call(
        spatial_kernel,
        in_specs=[ANY] * (len(pieces) + 1),
        out_specs=ANY,
        out_shape=jax.ShapeDtypeStruct((8, 2, LOCAL, FEATURES), jnp.bfloat16),
        scratch_shapes=[
            pltpu.VMEM((2, 8) + ROW, jnp.bfloat16),
            pltpu.VMEM((2, 8, LOCAL, FEATURES), jnp.bfloat16),
            pltpu.SemaphoreType.DMA((2, 8)),
            pltpu.SemaphoreType.DMA((2,)),
        ],
        compiler_params=GRANT,
        cost_estimate=pl.CostEstimate(
            flops=8 * HEADS * PATCHES * PATCHES * HD,
            bytes_accessed=2 * PATCHES * 4 * FEATURES * 2,
            transcendentals=2 * HEADS * PATCHES * PATCHES,
        ),
        name="spatial_attention",
    )(*pieces, behind)


ROWS = FRAMES * 16


def time_kernel(tqk_ref, behind_ref, out_ref, mark_ref, tqk, weights, load_sem, sems):
    load = pltpu.make_async_copy(tqk_ref, tqk, load_sem)
    load.start()
    load.wait()
    mark_ref[...] = jnp.zeros_like(mark_ref)
    r = lax.broadcasted_iota(jnp.int32, (ROWS, ROWS), 0)
    c = lax.broadcasted_iota(jnp.int32, (ROWS, ROWS), 1)
    bias = jnp.where((r & 15) == (c & 15), 0.0, -1e30).astype(jnp.float32)
    stores = []
    for h in range(HEADS):
        for g in range(LOCAL // 16):
            part = pl.ds(g * 16, 16)
            q = tqk[:, part, pl.ds(h * HD, HD)].reshape(ROWS, HD)
            k = tqk[:, part, pl.ds(FEATURES + h * HD, HD)].reshape(ROWS, HD)
            s = nt(q, k) + bias
            m = jnp.max(s, axis=-1, keepdims=True)
            e = jnp.exp2((s - m) * SCORE_LOG2)
            total = jnp.sum(e, axis=-1, keepdims=True)
            weights[h, g] = (e * (1.0 / total)).astype(jnp.bfloat16)
        stores.append(pltpu.make_async_copy(weights.at[h], out_ref.at[h], sems.at[h]))
        stores[-1].start()
    for store in stores:
        store.wait()


def time_weights(temporal_qk, behind):
    return pl.pallas_call(
        time_kernel,
        in_specs=[ANY] * 2,
        out_specs=[ANY, VMEM],
        out_shape=[
            jax.ShapeDtypeStruct((HEADS, 2, ROWS, ROWS), jnp.bfloat16),
            jax.ShapeDtypeStruct((8, 128), jnp.float32),
        ],
        scratch_shapes=[
            pltpu.VMEM((FRAMES, LOCAL, 2 * FEATURES), jnp.bfloat16),
            pltpu.VMEM((HEADS, 2, ROWS, ROWS), jnp.bfloat16),
            pltpu.SemaphoreType.DMA,
            pltpu.SemaphoreType.DMA((HEADS,)),
        ],
        compiler_params=GRANT,
        cost_estimate=pl.CostEstimate(
            flops=4 * HEADS * ROWS * ROWS * HD,
            bytes_accessed=7_000_000,
            transcendentals=2 * HEADS * ROWS * ROWS,
        ),
        name="time_weights",
    )(temporal_qk, behind)


def flip(value, bit):
    return lax.ppermute(value, "dp", [(i, i ^ bit) for i in range(32)])


def join_kernel(*refs):
    refs[-1][0] = refs[0][...]
    refs[-1][1] = refs[1][...]


def flip_y(value):
    pairs = [(i * 8 + s, (i ^ 16) * 8 + (s ^ 1)) for i in range(32) for s in range(8)]
    return lax.ppermute(value, ("dp", "space"), pairs)


def doubled(value, other, *behind):
    both = pl.pallas_call(
        join_kernel,
        in_specs=[VMEM] * 2 + [ANY] * len(behind),
        out_specs=VMEM,
        out_shape=jax.ShapeDtypeStruct((2,) + value.shape, value.dtype),
        compiler_params=pltpu.CompilerParams(vmem_limit_bytes=8 * MIB),
        cost_estimate=pl.CostEstimate(flops=0, bytes_accessed=1_000_000, transcendentals=0),
        name="join",
    )(value, other, *behind)
    return both.reshape((-1,) + value.shape[1:])


def token_kernel(
    value, time_ref, proj_ref, mine_ref, other_ref,
    emb_ref, all_stats_ref, grad_ref, lens_ref,
    proj, mine, comb, video, grads, stats_ref, sems, grad_sems,
):
    proj_load = pltpu.make_async_copy(proj_ref, proj, sems.at[0])
    mine_load = pltpu.make_async_copy(mine_ref, mine, sems.at[1])
    proj_load.start()
    mine_load.start()
    for h in range(HEADS):
        cols = pl.ds(h * HD, HD)
        for g in range(LOCAL // 16):
            part = pl.ds(g * 16, 16)
            v = value[:, :, part, cols].reshape(ROWS, HD)
            o = jnp.dot(time_ref[h, g], v, preferred_element_type=jnp.float32)
            o = (v.astype(jnp.float32) + o).astype(jnp.bfloat16)
            comb[:, part, cols] = o.reshape(FRAMES, 16, HD)
    tokens = FRAMES * LOCAL
    proj_load.wait()
    projected = jnp.dot(
        comb[...].reshape(tokens, FEATURES), proj[...], preferred_element_type=jnp.float32
    )
    scale = lax.rsqrt(jnp.mean(projected * projected, axis=-1, keepdims=True) + 1e-06)
    emb = (projected * scale).astype(jnp.bfloat16)
    video[...] = emb.reshape(FRAMES, LOCAL, EMB)
    emb_store = pltpu.make_async_copy(video, emb_ref, sems.at[2])
    emb_store.start()
    mine_load.wait()

    eye = lax.broadcasted_iota(jnp.int32, (PADDED, 128), 0) == lax.broadcasted_iota(
        jnp.int32, (PADDED, 128), 1
    )
    y_hi, core, _, _, z = place()
    group = 8
    stores = []
    for i, (ref, c) in enumerate(((mine, core), (other_ref, 1 - core))):
        for m0 in range(0, CAPTIONS // 2, group):
            sim = nt(ref[pl.ds(m0, group)].reshape(group * PADDED, EMB), emb)
            top = jnp.max(sim, axis=-1, keepdims=True)
            w = jnp.exp2((sim - top) * SHARP_LOG2)
            total = jnp.sum(w, axis=-1, keepdims=True)
            product = jnp.dot(w.astype(jnp.bfloat16), emb, preferred_element_type=jnp.float32)
            slot = i * CAPTIONS // 2 + m0
            grads[pl.ds(slot, group)] = product.astype(jnp.bfloat16).reshape(group, PADDED, EMB)
            for j in range(group):
                m = m0 + j
                flips = (m >> 3 & 1) + (m >> 2 & 1) * 2 + (m >> 1 & 1) * 4
                at = (y_hi ^ (m & 1)) * 16 + (z ^ flips) * 2 + c
                stores.append(
                    pltpu.make_async_copy(
                        grads.at[slot + j], grad_ref.at[at], grad_sems.at[slot + j]
                    )
                )
                stores[-1].start()
                rng = slice(j * PADDED, (j + 1) * PADDED)
                top_row = jnp.sum(jnp.where(eye, top[rng], 0.0), axis=0, keepdims=True)
                total_row = jnp.sum(jnp.where(eye, total[rng], 0.0), axis=0, keepdims=True)
                stats_ref[0, pl.ds(at, 1), :] = top_row
                stats_ref[1, pl.ds(at, 1), :] = total_row
                lens_ref[pl.ds(at, 1), :] = ref[m, SLOTS : SLOTS + 1, :128].astype(jnp.float32)
    for k in range(8):
        all_stats_ref[k] = stats_ref[...]
    emb_store.wait()
    for store in stores:
        store.wait()


def token_part(spatial, time, proj_weight, mine, other):
    bf16 = jnp.bfloat16
    return pl.pallas_call(
        token_kernel,
        in_specs=[VMEM, VMEM, FAR_OFF, FAR_OFF, VMEM],
        out_specs=[FAR_OFF, VMEM, FAR_OFF, VMEM],
        out_shape=[
            pltpu.HBM((FRAMES, LOCAL, EMB), bf16),
            jax.ShapeDtypeStruct((8, 2, CAPTIONS, 128), jnp.float32),
            pltpu.HBM((CAPTIONS, PADDED, EMB), bf16),
            jax.ShapeDtypeStruct((CAPTIONS, 128), jnp.float32),
        ],
        scratch_shapes=[
            pltpu.VMEM((FEATURES, EMB), bf16),
            pltpu.VMEM((CAPTIONS // 2, PADDED, EMB), bf16),
            pltpu.VMEM((FRAMES, LOCAL, FEATURES), bf16),
            pltpu.VMEM((FRAMES, LOCAL, EMB), bf16),
            pltpu.VMEM((CAPTIONS, PADDED, EMB), bf16),
            pltpu.VMEM((2, CAPTIONS, 128), jnp.float32),
            pltpu.SemaphoreType.DMA((3,)),
            pltpu.SemaphoreType.DMA((CAPTIONS,)),
        ],
        compiler_params=GRANT,
        cost_estimate=pl.CostEstimate(
            flops=4_500_000_000, bytes_accessed=12_000_000, transcendentals=1_300_000
        ),
        name="token_part",
    )(spatial, time, held(proj_weight), held(mine), other)


def coef_kernel(
    pos_ref, stats_ref, lens_ref, grad_ref, send_ref, keep_ref, loss_ref, hold, grad, sems
):
    group = 8
    loads = [
        pltpu.make_async_copy(
            grad_ref.at[pl.ds(group * i, group)], grad.at[pl.ds(group * i, group)], sems.at[i]
        )
        for i in range(CAPTIONS // group)
    ]
    for load in loads:
        load.start()
    tops = stats_ref[:, 0]
    totals = stats_ref[:, 1]
    top = jnp.max(tops, axis=0)
    total = jnp.sum(totals * jnp.exp2((tops - top[None]) * SHARP_LOG2), axis=0)
    soft = top + jnp.log(total) / SHARPNESS
    slot = lax.broadcasted_iota(jnp.int32, (CAPTIONS, 128), 1).astype(jnp.float32)
    lens = lens_ref[...]
    live = slot < lens
    lens_col = lens[:, :1]
    score = jnp.sum(jnp.where(live, soft, 0.0), axis=-1, keepdims=True) / lens_col
    logits = LOGIT_SCALE * score
    peak = jnp.max(logits, axis=0, keepdims=True)
    log_total = peak + jnp.log(jnp.sum(jnp.exp(logits - peak), axis=0, keepdims=True))
    onehot = lax.broadcasted_iota(jnp.int32, (CAPTIONS, 1), 0) == pos_ref[0]
    loss_ref[...] = log_total - jnp.sum(jnp.where(onehot, logits, 0.0), axis=0, keepdims=True)
    grad_logit = LOGIT_SCALE * (jnp.exp(logits - log_total) - onehot.astype(jnp.float32))
    coef = jnp.where(live, grad_logit / lens_col, 0.0)
    mine = stats_ref[lax.axis_index("space"), 0]
    hold[...] = coef * jnp.exp2((mine - soft) * SHARP_LOG2)

    eye = lax.broadcasted_iota(jnp.int32, (PADDED, 128), 0) == lax.broadcasted_iota(
        jnp.int32, (PADDED, 128), 1
    )
    core = lax.axis_index("dp") & 1
    for m in range(CAPTIONS // 2):
        if 2 * m % group == 0:
            loads[2 * m // group].wait()
        for j, ref in ((2 * m + 1 - core, send_ref), (2 * m + core, keep_ref)):
            col = jnp.sum(jnp.where(eye, hold[pl.ds(j, 1), :], 0.0), axis=-1, keepdims=True)
            ref[m] = (grad[j].astype(jnp.float32) * col).astype(jnp.bfloat16)


def coef_part(pos, stats, lens, grad):
    half = jax.ShapeDtypeStruct((CAPTIONS // 2, PADDED, EMB), jnp.bfloat16)
    return pl.pallas_call(
        coef_kernel,
        in_specs=[SMEM, VMEM, VMEM, FAR_OFF],
        out_specs=[VMEM] * 3,
        out_shape=[half, half, jax.ShapeDtypeStruct((1, 1), jnp.float32)],
        scratch_shapes=[
            pltpu.VMEM((CAPTIONS, 128), jnp.float32),
            pltpu.VMEM((CAPTIONS, PADDED, EMB), jnp.bfloat16),
            pltpu.SemaphoreType.DMA((4,)),
        ],
        compiler_params=pltpu.CompilerParams(vmem_limit_bytes=12 * MIB),
        cost_estimate=pl.CostEstimate(
            flops=4_000_000, bytes_accessed=6_000_000, transcendentals=100_000
        ),
        name="coef_part",
    )(pos, stats, lens, held(grad))


def small_call(kernel, name, operands, out_shapes, specs=None):
    return pl.pallas_call(
        kernel,
        in_specs=specs or [VMEM] * len(operands),
        out_specs=[VMEM] * len(out_shapes),
        out_shape=[jax.ShapeDtypeStruct(s, d) for s, d in out_shapes],
        compiler_params=pltpu.CompilerParams(vmem_limit_bytes=16 * MIB),
        cost_estimate=pl.CostEstimate(flops=0, bytes_accessed=2_000_000, transcendentals=0),
        name=name,
    )(*operands)


def added(a, b):
    return (a.astype(jnp.float32) + b.astype(jnp.float32)).astype(jnp.bfloat16)


def first_sum_kernel(keep_ref, got_ref, a_keep, a_send, b_keep, b_send):
    x = lax.axis_index("space") >> 1
    plan = (
        (0, ((a_keep, 0, 0), (a_send, 0, 1), (a_send, 1, 2), (a_keep, 1, 3))),
        (8, ((b_keep, 0, 0), (b_keep, 1, 1), (b_send, 1, 2), (b_send, 0, 3))),
    )
    for start, parts in plan:
        for ref, at, flip in parts:
            cols = pl.ds(pl.multiple_of((x ^ flip) * 128, 128), 128)
            for m in range(8):
                ref[m, :, pl.ds(at * 128, 128)] = added(
                    keep_ref[start + m, :, cols], got_ref[start + m, :, cols]
                )


def second_sum_kernel(a_keep, a_got, b_keep, b_got, a_mine, a_send, b_mine, b_send):
    for keep, got, mine, send in ((a_keep, a_got, a_mine, a_send), (b_keep, b_got, b_mine, b_send)):
        mine[...] = added(keep[:, :, :128], got[:, :, :128])
        send[...] = added(keep[:, :, 128:], got[:, :, 128:])


def third_sum_kernel(a_mine, a_got, b_mine, b_got, out):
    out[pl.ds(0, 8)] = added(a_mine[...], a_got[...])
    out[pl.ds(8, 8)] = added(b_mine[...], b_got[...])


def owned_sum_kernel(parts, out):
    total = jnp.sum(parts[...].astype(jnp.float32), axis=0).astype(jnp.bfloat16)
    for k in range(8):
        out[k] = total


def last_sum_kernel(parts, out):
    for x in range(4):
        total = parts[2 * x].astype(jnp.float32) + parts[2 * x + 1].astype(jnp.float32)
        out[:, 0, pl.ds(x * 128, 128)] = total[:SLOTS]


def reduce_gradient(send, keep):
    bf16 = jnp.bfloat16
    one = [(s, s ^ 2) for s in range(8)]
    three = [(s, s ^ 6) for s in range(8)]
    got = lax.ppermute(send, "dp", [(i, i ^ 1) for i in range(32)])
    a_keep, a_send, b_keep, b_send = small_call(
        first_sum_kernel, "first_sum", (keep, got), [((8, PADDED, 256), bf16)] * 4
    )
    a_got = lax.ppermute(a_send, "space", one)
    b_got = lax.ppermute(b_send, "space", three)
    a_mine, a_send, b_mine, b_send = small_call(
        second_sum_kernel, "second_sum", (a_keep, a_got, b_keep, b_got),
        [((8, PADDED, 128), bf16)] * 4,
    )
    a_got = lax.ppermute(a_send, "space", three)
    b_got = lax.ppermute(b_send, "space", one)
    (parts,) = small_call(
        third_sum_kernel, "third_sum", (a_mine, a_got, b_mine, b_got), [((16, PADDED, 128), bf16)]
    )
    parts = lax.all_to_all(
        parts, "dp", split_axis=0, concat_axis=0, tiled=True,
        axis_index_groups=[[2 * m + c for m in range(16)] for c in range(2)],
    )
    (parts,) = small_call(owned_sum_kernel, "owned_sum", (parts,), [((8, PADDED, 128), bf16)])
    parts = lax.all_to_all(parts, "space", split_axis=0, concat_axis=0, tiled=True)
    (total,) = small_call(last_sum_kernel, "last_sum", (parts,), [((SLOTS, 1, EMB), jnp.float32)])
    return total.reshape(1, SLOTS, EMB)


def on_device(clip_qkv, temporal_qk, proj_weight, caption_tokens, caption_lens, positive):
    lens_row = jnp.broadcast_to(
        caption_lens.astype(jnp.bfloat16)[:, None, None], (1, PADDED - SLOTS, EMB)
    )
    caps = jnp.concatenate([caption_tokens, lens_row], axis=1)
    caps = doubled(caps, flip_y(caps))
    far = flip(caps, 8)
    pieces, started = bring_frames(clip_qkv[0], far)
    time, done = time_weights(temporal_qk[0], started)
    caps = doubled(caps, far)
    caps = doubled(caps, flip(caps, 4), pieces[2])
    caps = doubled(caps, flip(caps, 2))
    other = flip(caps, 1)
    attended = spatial_attention(pieces, done)
    spatial = lax.all_to_all(attended, "space", split_axis=0, concat_axis=0, tiled=True)
    video, stats, grad, lens = token_part(spatial, time, proj_weight, caps, other)
    stats = lax.all_to_all(stats, "space", split_axis=0, concat_axis=0, tiled=True)
    send, keep, loss = coef_part(positive, stats, lens, grad)
    caption_grad = reduce_gradient(send, keep)
    return video[None], caption_grad, loss.reshape(1)


def solution(mesh):
    return jax.shard_map(
        on_device,
        mesh=mesh,
        in_specs=(
            P("dp", None, "space", None),
            P("dp", None, "space", None),
            P(),
            P("dp", None, None),
            P("dp"),
            P("dp"),
        ),
        out_specs=(P("dp", None, "space", None), P("dp", None, None), P("dp")),
        check_vma=False,
    )
```

```python
import functools
import math

import jax
import jax.numpy as jnp
from jax import lax
from jax.experimental import pallas as pl
from jax.experimental.pallas import tpu as pltpu
from jax.sharding import PartitionSpec as P

HEADS = 13
HD = 128
FEATURES = HEADS * HD
EMB = 512
FRAMES = 16
PATCHES = 256
LOCAL = 32
SLOTS = 77
PADDED = 80
CAPTIONS = 32
SHARPNESS = 4.0
LOGIT_SCALE = 10.0
LOG2E = math.log2(math.e)
SCORE_LOG2 = HD ** (-0.5) * LOG2E
SHARP_LOG2 = SHARPNESS * LOG2E
MIB = 1 << 20
GRANT = pltpu.CompilerParams(vmem_limit_bytes=24 * MIB)
VMEM = pl.BlockSpec(memory_space=pltpu.VMEM)
SMEM = pl.BlockSpec(memory_space=pltpu.SMEM)

FAR_OFF = pl.BlockSpec(memory_space=pltpu.HBM)
ANY = pl.BlockSpec(memory_space=pl.ANY)


def owner(g1, a):
    return (g1 * 2 + ((a >> 1) ^ g1)) * 2 + (a & 1)


def place():
    dp, space = lax.axis_index("dp"), lax.axis_index("space")
    return dp >> 4, dp & 1, space >> 1, space & 1, (dp >> 1) & 7


def quad_place():
    _, _, x, y, _ = place()
    return x >> 1, ((x >> 1) ^ (x & 1)) * 2 + y


def held(value):
    return pltpu.with_memory_space_constraint(value, pltpu.HBM)


def nt(a, b):
    return lax.dot_general(a, b, (((1,), (1,)), ((), ())), preferred_element_type=jnp.float32)


SPLIT = 7


ROW = (LOCAL, 3 * FEATURES)
FULL = pltpu.CompilerParams(vmem_limit_bytes=60 * MIB)


def copied(pairs, buf, sems):
    loads = [
        pltpu.make_async_copy(src, buf.at[i], sems.at[0, i]) for i, (src, _) in enumerate(pairs)
    ]
    stores = [
        pltpu.make_async_copy(buf.at[i], dst, sems.at[1, i]) for i, (_, dst) in enumerate(pairs)
    ]
    for load in loads:
        load.start()
    for load, store in zip(loads, stores):
        load.wait()
        store.start()
    for store in stores:
        store.wait()


def copying(kernel, name, operands, shapes, count, params=FULL):
    return pl.pallas_call(
        kernel,
        in_specs=[ANY] * len(operands),
        out_specs=[ANY] * len(shapes),
        out_shape=[jax.ShapeDtypeStruct((n,) + ROW, jnp.bfloat16) for n in shapes],
        scratch_shapes=[
            pltpu.VMEM((count,) + ROW, jnp.bfloat16),
            pltpu.SemaphoreType.DMA((2, count)),
        ],
        compiler_params=params,
        cost_estimate=pl.CostEstimate(flops=0, bytes_accessed=6_000_000, transcendentals=0),
        name=name,
    )(*operands)


def depart_kernel(clip_ref, one, two, three, across_ref, buf, sems):
    g1, a = quad_place()
    pairs = [
        (clip_ref.at[2 * owner(g, a ^ k)], ref.at[g])
        for k, ref in ((1, one), (2, two), (3, three))
        for g in range(2)
    ]
    pairs += [(clip_ref.at[2 * owner(1 - g1, b) + 1], across_ref.at[b]) for b in range(4)]
    copied(pairs, buf, sems)


def own_kernel(clip_ref, first, seconds, kept, buf, sems):
    g1, a = quad_place()
    pairs = [(clip_ref.at[2 * owner(1 - g1, a)], first.at[0])]
    pairs += [(clip_ref.at[2 * owner(g1, a ^ k) + 1], seconds.at[k - 1]) for k in (1, 2, 3)]
    pairs += [(clip_ref.at[2 * owner(g1, a) + f], kept.at[f]) for f in range(2)]
    copied(pairs, buf, sems)


def turn_kernel(first_ref, one, two, three, behind_ref, started_ref, out_ref, buf, sems):
    g1, _ = quad_place()
    pairs = [(first_ref.at[0], out_ref.at[0])]
    pairs += [(ref.at[1 - g1], out_ref.at[k]) for k, ref in ((1, one), (2, two), (3, three))]
    copied(pairs, buf, sems)


def spread_kernel(seconds_ref, across_ref, one, two, three, buf, sems):
    _, a = quad_place()
    pairs = []
    for k, ref in ((1, one), (2, two), (3, three)):
        pairs += [(seconds_ref.at[k - 1], ref.at[0]), (across_ref.at[a ^ k], ref.at[1])]
    copied(pairs, buf, sems)


def swap(value, bits):
    return lax.ppermute(value, "space", [(s, s ^ bits) for s in range(8)])


def bring_frames(clip, behind):
    *quads, across = copying(depart_kernel, "depart", (clip,), (2, 2, 2, 4), 10)
    across = swap(across, 6)
    quads = [swap(quad, k) for k, quad in zip((1, 2, 3), quads)]
    first, seconds, kept = copying(own_kernel, "own", (clip,), (1, 3, 2), 6)
    few = pltpu.CompilerParams(vmem_limit_bytes=8 * MIB)
    pairs = copying(spread_kernel, "spread", (seconds, across), (2, 2, 2), 6, few)
    started = pairs[0]
    pairs = [swap(pair, k) for k, pair in zip((1, 2, 3), pairs)]
    (turned,) = copying(turn_kernel, "turn", (first, *quads, behind, started), (4,), 4, few)
    turned = swap(turned, 6)
    return (kept, across, turned, *quads, *pairs), started


def spatial_kernel(kept_ref, across_ref, turned_ref, *refs):
    quads, pairs, (_, out_ref, buf, res, sems, store_sems) = refs[:3], refs[3:6], refs[6:]
    g1, a = quad_place()
    first = [kept_ref.at[0]] + [ref.at[g1] for ref in quads] + [turned_ref.at[k] for k in range(4)]
    second = [kept_ref.at[1]] + [ref.at[0] for ref in pairs]
    second += [across_ref.at[a]] + [ref.at[1] for ref in pairs]
    loads = [
        [pltpu.make_async_copy(src, buf.at[f, i], sems.at[f, i]) for i, src in enumerate(sources)]
        for f, sources in enumerate((first, second))
    ]
    for f in range(2):
        for load in loads[f]:
            load.start()
    stores = [
        pltpu.make_async_copy(res.at[f], out_ref.at[:, f], store_sems.at[f]) for f in range(2)
    ]
    for f in range(2):
        for load in loads[f]:
            load.wait()
        for h in range(HEADS):
            q = buf[f, :, :, pl.ds(h * HD, HD)].reshape(PATCHES, HD)
            k = buf[f, :, :, pl.ds(FEATURES + h * HD, HD)].reshape(PATCHES, HD)
            v = buf[f, :, :, pl.ds(2 * FEATURES + h * HD, HD)].reshape(PATCHES, HD)
            s = nt(q, k)
            m = jnp.max(s, axis=-1, keepdims=True)
            e = jnp.exp2((s - m) * SCORE_LOG2)
            total = jnp.sum(e, axis=-1, keepdims=True)
            o = jnp.dot(e.astype(jnp.bfloat16), v, preferred_element_type=jnp.float32)
            o = (o * (1.0 / total)).astype(jnp.bfloat16)
            for i in range(8):
                at = owner(g1 if i < 4 else 1 - g1, a ^ (i & 3))
                res[f, at, :, pl.ds(h * HD, HD)] = o[i * LOCAL : (i + 1) * LOCAL]
        stores[f].start()
    for store in stores:
        store.wait()


def spatial_attention(pieces, behind):
    return pl.pallas_call(
        spatial_kernel,
        in_specs=[ANY] * (len(pieces) + 1),
        out_specs=ANY,
        out_shape=jax.ShapeDtypeStruct((8, 2, LOCAL, FEATURES), jnp.bfloat16),
        scratch_shapes=[
            pltpu.VMEM((2, 8) + ROW, jnp.bfloat16),
            pltpu.VMEM((2, 8, LOCAL, FEATURES), jnp.bfloat16),
            pltpu.SemaphoreType.DMA((2, 8)),
            pltpu.SemaphoreType.DMA((2,)),
        ],
        compiler_params=GRANT,
        cost_estimate=pl.CostEstimate(
            flops=8 * HEADS * PATCHES * PATCHES * HD,
            bytes_accessed=2 * PATCHES * 4 * FEATURES * 2,
            transcendentals=2 * HEADS * PATCHES * PATCHES,
        ),
        name="spatial_attention",
    )(*pieces, behind)


ROWS = FRAMES * 16


def time_kernel(tqk_ref, behind_ref, out_ref, mark_ref, tqk, weights, load_sem, sems):
    load = pltpu.make_async_copy(tqk_ref, tqk, load_sem)
    load.start()
    load.wait()
    mark_ref[...] = jnp.zeros_like(mark_ref)
    r = lax.broadcasted_iota(jnp.int32, (ROWS, ROWS), 0)
    c = lax.broadcasted_iota(jnp.int32, (ROWS, ROWS), 1)
    bias = jnp.where((r & 15) == (c & 15), 0.0, -1e30).astype(jnp.float32)
    stores = []
    for h in range(HEADS):
        for g in range(LOCAL // 16):
            part = pl.ds(g * 16, 16)
            q = tqk[:, part, pl.ds(h * HD, HD)].reshape(ROWS, HD)
            k = tqk[:, part, pl.ds(FEATURES + h * HD, HD)].reshape(ROWS, HD)
            s = nt(q, k) + bias
            m = jnp.max(s, axis=-1, keepdims=True)
            e = jnp.exp2((s - m) * SCORE_LOG2)
            total = jnp.sum(e, axis=-1, keepdims=True)
            weights[h, g] = (e * (1.0 / total)).astype(jnp.bfloat16)
        stores.append(pltpu.make_async_copy(weights.at[h], out_ref.at[h], sems.at[h]))
        stores[-1].start()
    for store in stores:
        store.wait()


def time_weights(temporal_qk, behind):
    return pl.pallas_call(
        time_kernel,
        in_specs=[ANY] * 2,
        out_specs=[ANY, VMEM],
        out_shape=[
            jax.ShapeDtypeStruct((HEADS, 2, ROWS, ROWS), jnp.bfloat16),
            jax.ShapeDtypeStruct((8, 128), jnp.float32),
        ],
        scratch_shapes=[
            pltpu.VMEM((FRAMES, LOCAL, 2 * FEATURES), jnp.bfloat16),
            pltpu.VMEM((HEADS, 2, ROWS, ROWS), jnp.bfloat16),
            pltpu.SemaphoreType.DMA,
            pltpu.SemaphoreType.DMA((HEADS,)),
        ],
        compiler_params=GRANT,
        cost_estimate=pl.CostEstimate(
            flops=4 * HEADS * ROWS * ROWS * HD,
            bytes_accessed=7_000_000,
            transcendentals=2 * HEADS * ROWS * ROWS,
        ),
        name="time_weights",
    )(temporal_qk, behind)


def flip(value, bit):
    return lax.ppermute(value, "dp", [(i, i ^ bit) for i in range(32)])


def join_kernel(*refs):
    refs[-1][0] = refs[0][...]
    refs[-1][1] = refs[1][...]


def flip_y(value):
    pairs = [(i * 8 + s, (i ^ 16) * 8 + (s ^ 1)) for i in range(32) for s in range(8)]
    return lax.ppermute(value, ("dp", "space"), pairs)


def doubled(value, other, *behind):
    both = pl.pallas_call(
        join_kernel,
        in_specs=[VMEM] * 2 + [ANY] * len(behind),
        out_specs=VMEM,
        out_shape=jax.ShapeDtypeStruct((2,) + value.shape, value.dtype),
        compiler_params=pltpu.CompilerParams(vmem_limit_bytes=8 * MIB),
        cost_estimate=pl.CostEstimate(flops=0, bytes_accessed=1_000_000, transcendentals=0),
        name="join",
    )(value, other, *behind)
    return both.reshape((-1,) + value.shape[1:])


def token_kernel(
    value, time_ref, proj_ref, mine_ref, other_ref,
    emb_ref, all_stats_ref, grad_ref, lens_ref,
    proj, mine, comb, video, grads, stats_ref, sems, grad_sems,
):
    proj_load = pltpu.make_async_copy(proj_ref, proj, sems.at[0])
    mine_load = pltpu.make_async_copy(mine_ref, mine, sems.at[1])
    proj_load.start()
    mine_load.start()
    for h in range(HEADS):
        cols = pl.ds(h * HD, HD)
        for g in range(LOCAL // 16):
            part = pl.ds(g * 16, 16)
            v = value[:, :, part, cols].reshape(ROWS, HD)
            o = jnp.dot(time_ref[h, g], v, preferred_element_type=jnp.float32)
            o = (v.astype(jnp.float32) + o).astype(jnp.bfloat16)
            comb[:, part, cols] = o.reshape(FRAMES, 16, HD)
    tokens = FRAMES * LOCAL
    proj_load.wait()
    projected = jnp.dot(
        comb[...].reshape(tokens, FEATURES), proj[...], preferred_element_type=jnp.float32
    )
    scale = lax.rsqrt(jnp.mean(projected * projected, axis=-1, keepdims=True) + 1e-06)
    emb = (projected * scale).astype(jnp.bfloat16)
    video[...] = emb.reshape(FRAMES, LOCAL, EMB)
    emb_store = pltpu.make_async_copy(video, emb_ref, sems.at[2])
    emb_store.start()
    mine_load.wait()

    eye = lax.broadcasted_iota(jnp.int32, (PADDED, 128), 0) == lax.broadcasted_iota(
        jnp.int32, (PADDED, 128), 1
    )
    y_hi, core, _, _, z = place()
    group = 8
    stores = []
    for i, (ref, c) in enumerate(((mine, core), (other_ref, 1 - core))):
        for m0 in range(0, CAPTIONS // 2, group):
            sim = nt(ref[pl.ds(m0, group)].reshape(group * PADDED, EMB), emb)
            top = jnp.max(sim, axis=-1, keepdims=True)
            w = jnp.exp2((sim - top) * SHARP_LOG2)
            total = jnp.sum(w, axis=-1, keepdims=True)
            product = jnp.dot(w.astype(jnp.bfloat16), emb, preferred_element_type=jnp.float32)
            slot = i * CAPTIONS // 2 + m0
            grads[pl.ds(slot, group)] = product.astype(jnp.bfloat16).reshape(group, PADDED, EMB)
            for j in range(group):
                m = m0 + j
                flips = (m >> 3 & 1) + (m >> 2 & 1) * 2 + (m >> 1 & 1) * 4
                at = (y_hi ^ (m & 1)) * 16 + (z ^ flips) * 2 + c
                stores.append(
                    pltpu.make_async_copy(
                        grads.at[slot + j], grad_ref.at[at], grad_sems.at[slot + j]
                    )
                )
                stores[-1].start()
                rng = slice(j * PADDED, (j + 1) * PADDED)
                top_row = jnp.sum(jnp.where(eye, top[rng], 0.0), axis=0, keepdims=True)
                total_row = jnp.sum(jnp.where(eye, total[rng], 0.0), axis=0, keepdims=True)
                stats_ref[0, pl.ds(at, 1), :] = top_row
                stats_ref[1, pl.ds(at, 1), :] = total_row
                lens_ref[pl.ds(at, 1), :] = ref[m, SLOTS : SLOTS + 1, :128].astype(jnp.float32)
    for k in range(8):
        all_stats_ref[k] = stats_ref[...]
    emb_store.wait()
    for store in stores:
        store.wait()


def token_part(spatial, time, proj_weight, mine, other):
    bf16 = jnp.bfloat16
    return pl.pallas_call(
        token_kernel,
        in_specs=[VMEM, VMEM, FAR_OFF, FAR_OFF, VMEM],
        out_specs=[FAR_OFF, VMEM, FAR_OFF, VMEM],
        out_shape=[
            pltpu.HBM((FRAMES, LOCAL, EMB), bf16),
            jax.ShapeDtypeStruct((8, 2, CAPTIONS, 128), jnp.float32),
            pltpu.HBM((CAPTIONS, PADDED, EMB), bf16),
            jax.ShapeDtypeStruct((CAPTIONS, 128), jnp.float32),
        ],
        scratch_shapes=[
            pltpu.VMEM((FEATURES, EMB), bf16),
            pltpu.VMEM((CAPTIONS // 2, PADDED, EMB), bf16),
            pltpu.VMEM((FRAMES, LOCAL, FEATURES), bf16),
            pltpu.VMEM((FRAMES, LOCAL, EMB), bf16),
            pltpu.VMEM((CAPTIONS, PADDED, EMB), bf16),
            pltpu.VMEM((2, CAPTIONS, 128), jnp.float32),
            pltpu.SemaphoreType.DMA((3,)),
            pltpu.SemaphoreType.DMA((CAPTIONS,)),
        ],
        compiler_params=GRANT,
        cost_estimate=pl.CostEstimate(
            flops=4_500_000_000, bytes_accessed=12_000_000, transcendentals=1_300_000
        ),
        name="token_part",
    )(spatial, time, held(proj_weight), held(mine), other)


def coef_kernel(
    pos_ref, stats_ref, lens_ref, grad_ref, send_ref, keep_ref, loss_ref, hold, grad, sems
):
    group = 8
    loads = [
        pltpu.make_async_copy(
            grad_ref.at[pl.ds(group * i, group)], grad.at[pl.ds(group * i, group)], sems.at[i]
        )
        for i in range(CAPTIONS // group)
    ]
    for load in loads:
        load.start()
    tops = stats_ref[:, 0]
    totals = stats_ref[:, 1]
    top = jnp.max(tops, axis=0)
    total = jnp.sum(totals * jnp.exp2((tops - top[None]) * SHARP_LOG2), axis=0)
    soft = top + jnp.log(total) / SHARPNESS
    slot = lax.broadcasted_iota(jnp.int32, (CAPTIONS, 128), 1).astype(jnp.float32)
    lens = lens_ref[...]
    live = slot < lens
    lens_col = lens[:, :1]
    score = jnp.sum(jnp.where(live, soft, 0.0), axis=-1, keepdims=True) / lens_col
    logits = LOGIT_SCALE * score
    peak = jnp.max(logits, axis=0, keepdims=True)
    log_total = peak + jnp.log(jnp.sum(jnp.exp(logits - peak), axis=0, keepdims=True))
    onehot = lax.broadcasted_iota(jnp.int32, (CAPTIONS, 1), 0) == pos_ref[0]
    loss_ref[...] = log_total - jnp.sum(jnp.where(onehot, logits, 0.0), axis=0, keepdims=True)
    grad_logit = LOGIT_SCALE * (jnp.exp(logits - log_total) - onehot.astype(jnp.float32))
    coef = jnp.where(live, grad_logit / lens_col, 0.0)
    mine = stats_ref[lax.axis_index("space"), 0]
    hold[...] = coef * jnp.exp2((mine - soft) * SHARP_LOG2)

    eye = lax.broadcasted_iota(jnp.int32, (PADDED, 128), 0) == lax.broadcasted_iota(
        jnp.int32, (PADDED, 128), 1
    )
    core = lax.axis_index("dp") & 1
    for m in range(CAPTIONS // 2):
        if 2 * m % group == 0:
            loads[2 * m // group].wait()
        for j, ref in ((2 * m + 1 - core, send_ref), (2 * m + core, keep_ref)):
            col = jnp.sum(jnp.where(eye, hold[pl.ds(j, 1), :], 0.0), axis=-1, keepdims=True)
            ref[m] = (grad[j].astype(jnp.float32) * col).astype(jnp.bfloat16)


def coef_part(pos, stats, lens, grad):
    half = jax.ShapeDtypeStruct((CAPTIONS // 2, PADDED, EMB), jnp.bfloat16)
    return pl.pallas_call(
        coef_kernel,
        in_specs=[SMEM, VMEM, VMEM, FAR_OFF],
        out_specs=[VMEM] * 3,
        out_shape=[half, half, jax.ShapeDtypeStruct((1, 1), jnp.float32)],
        scratch_shapes=[
            pltpu.VMEM((CAPTIONS, 128), jnp.float32),
            pltpu.VMEM((CAPTIONS, PADDED, EMB), jnp.bfloat16),
            pltpu.SemaphoreType.DMA((4,)),
        ],
        compiler_params=pltpu.CompilerParams(vmem_limit_bytes=12 * MIB),
        cost_estimate=pl.CostEstimate(
            flops=4_000_000, bytes_accessed=6_000_000, transcendentals=100_000
        ),
        name="coef_part",
    )(pos, stats, lens, held(grad))


def small_call(kernel, name, operands, out_shapes, specs=None):
    return pl.pallas_call(
        kernel,
        in_specs=specs or [VMEM] * len(operands),
        out_specs=[VMEM] * len(out_shapes),
        out_shape=[jax.ShapeDtypeStruct(s, d) for s, d in out_shapes],
        compiler_params=pltpu.CompilerParams(vmem_limit_bytes=16 * MIB),
        cost_estimate=pl.CostEstimate(flops=0, bytes_accessed=2_000_000, transcendentals=0),
        name=name,
    )(*operands)


def added(a, b):
    return (a.astype(jnp.float32) + b.astype(jnp.float32)).astype(jnp.bfloat16)


def first_sum_kernel(keep_ref, got_ref, a_keep, a_send, b_keep, b_send):
    x = lax.axis_index("space") >> 1
    plan = (
        (0, ((a_keep, 0, 0), (a_send, 0, 1), (a_send, 1, 2), (a_keep, 1, 3))),
        (8, ((b_keep, 0, 0), (b_keep, 1, 1), (b_send, 1, 2), (b_send, 0, 3))),
    )
    for start, parts in plan:
        for ref, at, flip in parts:
            cols = pl.ds(pl.multiple_of((x ^ flip) * 128, 128), 128)
            for m in range(8):
                ref[m, :, pl.ds(at * 128, 128)] = added(
                    keep_ref[start + m, :, cols], got_ref[start + m, :, cols]
                )


def second_sum_kernel(a_keep, a_got, b_keep, b_got, a_mine, a_send, b_mine, b_send):
    for keep, got, mine, send in ((a_keep, a_got, a_mine, a_send), (b_keep, b_got, b_mine, b_send)):
        mine[...] = added(keep[:, :, :128], got[:, :, :128])
        send[...] = added(keep[:, :, 128:], got[:, :, 128:])


def third_sum_kernel(a_mine, a_got, b_mine, b_got, out):
    out[pl.ds(0, 8)] = added(a_mine[...], a_got[...])
    out[pl.ds(8, 8)] = added(b_mine[...], b_got[...])


def owned_sum_kernel(parts, out):
    total = jnp.sum(parts[...].astype(jnp.float32), axis=0).astype(jnp.bfloat16)
    for k in range(8):
        out[k] = total


def last_sum_kernel(parts, out):
    for x in range(4):
        total = parts[2 * x].astype(jnp.float32) + parts[2 * x + 1].astype(jnp.float32)
        out[:, 0, pl.ds(x * 128, 128)] = total[:SLOTS]


def reduce_gradient(send, keep):
    bf16 = jnp.bfloat16
    one = [(s, s ^ 2) for s in range(8)]
    three = [(s, s ^ 6) for s in range(8)]
    got = lax.ppermute(send, "dp", [(i, i ^ 1) for i in range(32)])
    a_keep, a_send, b_keep, b_send = small_call(
        first_sum_kernel, "first_sum", (keep, got), [((8, PADDED, 256), bf16)] * 4
    )
    a_got = lax.ppermute(a_send, "space", one)
    b_got = lax.ppermute(b_send, "space", three)
    a_mine, a_send, b_mine, b_send = small_call(
        second_sum_kernel, "second_sum", (a_keep, a_got, b_keep, b_got),
        [((8, PADDED, 128), bf16)] * 4,
    )
    a_got = lax.ppermute(a_send, "space", three)
    b_got = lax.ppermute(b_send, "space", one)
    (parts,) = small_call(
        third_sum_kernel, "third_sum", (a_mine, a_got, b_mine, b_got), [((16, PADDED, 128), bf16)]
    )
    parts = lax.all_to_all(
        parts, "dp", split_axis=0, concat_axis=0, tiled=True,
        axis_index_groups=[[2 * m + c for m in range(16)] for c in range(2)],
    )
    (parts,) = small_call(owned_sum_kernel, "owned_sum", (parts,), [((8, PADDED, 128), bf16)])
    parts = lax.all_to_all(parts, "space", split_axis=0, concat_axis=0, tiled=True)
    (total,) = small_call(last_sum_kernel, "last_sum", (parts,), [((SLOTS, 1, EMB), jnp.float32)])
    return total.reshape(1, SLOTS, EMB)


def on_device(clip_qkv, temporal_qk, proj_weight, caption_tokens, caption_lens, positive):
    lens_row = jnp.broadcast_to(
        caption_lens.astype(jnp.bfloat16)[:, None, None], (1, PADDED - SLOTS, EMB)
    )
    caps = jnp.concatenate([caption_tokens, lens_row], axis=1)
    caps = doubled(caps, flip_y(caps))
    far = flip(caps, 8)
    pieces, started = bring_frames(clip_qkv[0], far)
    time, done = time_weights(temporal_qk[0], started)
    caps = doubled(caps, far)
    caps = doubled(caps, flip(caps, 4), pieces[2], done)
    caps = doubled(caps, flip(caps, 2))
    other = flip(caps, 1)
    attended = spatial_attention(pieces, done)
    spatial = lax.all_to_all(attended, "space", split_axis=0, concat_axis=0, tiled=True)
    video, stats, grad, lens = token_part(spatial, time, proj_weight, caps, other)
    stats = lax.all_to_all(stats, "space", split_axis=0, concat_axis=0, tiled=True)
    send, keep, loss = coef_part(positive, stats, lens, grad)
    caption_grad = reduce_gradient(send, keep)
    return video[None], caption_grad, loss.reshape(1)


def solution(mesh):
    return jax.shard_map(
        on_device,
        mesh=mesh,
        in_specs=(
            P("dp", None, "space", None),
            P("dp", None, "space", None),
            P(),
            P("dp", None, None),
            P("dp"),
            P("dp"),
        ),
        out_specs=(P("dp", None, "space", None), P("dp", None, None), P("dp")),
        check_vma=False,
    )
```
